512 devices in a mesh: gx: 8 (over x, core), gy: 8 (over z_hi, y), gz: 8 (over z_lo).
Axes of the slice: x: 4, y: 4, z: 16 (z_hi: 2, z_lo: 8; z = z_hi * 8 + z_lo), core: 2. Of those that a mesh axis runs over, the one named last changes fastest.
Arguments:
- positions: float32 [3, 524288], P(None, ('gx', 'gy', 'gz')), may hold values from -1 to 6.5
- charges: float32 [524288], P(('gx', 'gy', 'gz')), may hold values from -1.75 to 1.75
- block_anchor: int32 [3, 4096], P(None, ('gx', 'gy', 'gz')), may hold values from 0 to 120, as said below
- block_atoms: int32 [4096], P(('gx', 'gy', 'gz')), may hold values from 32 to 128, as said below
- brick_blocks: int32 [512], P(('gx', 'gy', 'gz')), may hold values from 4 to 8, as said below
- box_scale: float32 [3], replicated, may hold values from 1.25 to 1.5
Outputs:
- potential: float32 [192, 192, 1024], P('gx', 'gy', 'gz')
- forces: float32 [3, 524288], P(None, ('gx', 'gy', 'gz'))
The draws below stay inside these ranges and needn't reach their ends.
Inputs may be any that keep to these rules, and one draw needn't show every extreme that they name: `block_anchor`: along x, y, z a block's anchor lies from 0 to 16, 16 and 120 respectively. `block_atoms`: some block is full. `brick_blocks`: some brick uses all 8 block slots.
All inputs are finite; a program needn't handle non-finite values.
Results may differ from the reference program's by a relative error of at most 0.0003.
Values sent between devices are 32-bit elements; how exact they have to be, the bound alone decides.
A program may use at most 64 MiB of HBM per device.

```python
import math
import jax
import jax.numpy as jnp
from jax import lax

CX = 24
CY = 24
CZ = 128
NB = 8
BLOCK = 128
PATCH = 16
RIM = 4
RADIUS = 4
NX = 192
NY = 192
NZ = 1024
ATOMS = 524288
BLOCKS = 4096
N_GY = 8
N_GZ = 8
DEVICES = 512


def draw_positions(key, part):
    key = jax.random.fold_in(key, 5)
    keys = jax.random.split(key, 4)
    group = jax.random.randint(keys[0], (3, ATOMS), 0, 20)
    lower = jax.random.uniform(keys[1], (3, ATOMS), jnp.float32, -1.0, -0.6)
    upper = jax.random.uniform(keys[2], (3, ATOMS), jnp.float32, 6.1, 6.5)
    spread_out = jax.random.uniform(keys[3], (3, ATOMS), jnp.float32, -1.0, 6.5)
    placed = jnp.where(group < 7, lower, jnp.where(group < 14, upper, spread_out))
    return placed.astype(jnp.float32)


def draw_charges(key, part):
    key = jax.random.fold_in(key, 7)
    keys = jax.random.split(key, 3)
    sign_draw = jax.random.randint(keys[0], (BLOCKS,), 0, 2)
    block_sign = jnp.where(sign_draw == 0, -1.0, 1.0).astype(jnp.float32)
    block_part = (block_sign[:, None] * jnp.ones((BLOCK,), jnp.float32)[None, :]).reshape(ATOMS)
    rough = jnp.clip(0.6 * jax.random.normal(keys[2], (ATOMS,), jnp.float32), -1.4, 1.4)
    values = 0.35 * block_part + rough
    return values.astype(jnp.float32)


def draw_block_anchor(key, part):
    key = jax.random.fold_in(key, 11)
    keys = jax.random.split(key, 4)
    group = jax.random.randint(keys[3], (3, BLOCKS), 0, 10)
    along_x = jax.random.randint(keys[0], (BLOCKS,), 0, CX - 7)
    along_y = jax.random.randint(keys[1], (BLOCKS,), 0, CY - 7)
    along_z = jax.random.randint(keys[2], (BLOCKS,), 0, CZ - 7)
    spread_out = jnp.stack([along_x, along_y, along_z])
    highest = jnp.array([CX - 8, CY - 8, CZ - 8], jnp.int32)[:, None] * jnp.ones((1, BLOCKS), jnp.int32)
    chosen = jnp.where(group < 3, jnp.zeros_like(spread_out), jnp.where(group < 6, highest, spread_out))
    return chosen.astype(jnp.int32)


def draw_block_atoms(key, part):
    key = jax.random.fold_in(key, 17)
    keys = jax.random.split(key, 3)
    filled = jax.random.randint(keys[0], (BLOCKS,), 32, BLOCK + 1)
    fullest = jax.random.randint(keys[1], (), 0, BLOCKS)
    emptiest = (fullest + 1 + jax.random.randint(keys[2], (), 0, BLOCKS - 1)) % BLOCKS
    block_index = jnp.arange(BLOCKS)
    filled = jnp.where(block_index == fullest, BLOCK, filled)
    filled = jnp.where(block_index == emptiest, 32, filled)
    return filled.astype(jnp.int32)


def draw_brick_blocks(key, part):
    key = jax.random.fold_in(key, 23)
    keys = jax.random.split(key, 3)
    counts = jax.random.randint(keys[0], (DEVICES,), NB // 2, NB + 1)
    fullest = jax.random.randint(keys[1], (), 0, DEVICES)
    emptiest = (fullest + 1 + jax.random.randint(keys[2], (), 0, DEVICES - 1)) % DEVICES
    device_index = jnp.arange(DEVICES)
    counts = jnp.where(device_index == fullest, NB, counts)
    counts = jnp.where(device_index == emptiest, NB // 2, counts)
    return counts.astype(jnp.int32)


def setup_inputs(seed: int = 0) -> dict:
    seeds = jax.random.split(jax.random.key(seed), 7)
    positions = draw_positions(jax.random.fold_in(seeds[6], 71), 0)
    charges = draw_charges(jax.random.fold_in(seeds[6], 71), 0)
    block_anchor = draw_block_anchor(jax.random.fold_in(seeds[6], 71), 0)
    block_atoms = draw_block_atoms(jax.random.fold_in(seeds[6], 71), 0)
    brick_blocks = draw_brick_blocks(jax.random.fold_in(seeds[6], 71), 0)
    box_scale = jnp.clip(jax.random.uniform(seeds[5], (3,), jnp.float32, 1.25, 1.5), 1.25, 1.5)
    return dict(positions=positions, charges=charges, block_anchor=block_anchor, block_atoms=block_atoms, brick_blocks=brick_blocks, box_scale=box_scale)


SPREAD = 1.0
SMOOTH = 1.5
COUPLING = 200.0

def gaussian(offset, spread_width):
    return jnp.exp(-offset * offset / (2.0 * spread_width * spread_width)) / (math.sqrt(2.0 * math.pi) * spread_width)

def block_weights(coords, charge_rows, anchors, filled, block_index, active_blocks, scale):
    spread_width = SPREAD * scale
    shifted = coords * scale[:, None, None]
    slot_index = jnp.arange(charge_rows.shape[1], dtype=jnp.int32)
    active = (block_index[:, None] < active_blocks) & (slot_index[None, :] < filled[:, None])
    weighted = jnp.where(active, charge_rows, jnp.zeros_like(charge_rows))
    cell_index = jnp.arange(PATCH, dtype=jnp.float32)
    offset_x = shifted[0][:, :, None] + RIM - cell_index
    weight_x = gaussian(offset_x, spread_width[0])
    slope_x = -offset_x / (spread_width[0] * spread_width[0]) * weight_x
    offset_y = shifted[1][:, :, None] + RIM - cell_index
    weight_y = gaussian(offset_y, spread_width[1])
    slope_y = -offset_y / (spread_width[1] * spread_width[1]) * weight_y
    offset_z = shifted[2][:, :, None] + RIM - cell_index
    weight_z = gaussian(offset_z, spread_width[2])
    slope_z = -offset_z / (spread_width[2] * spread_width[2]) * weight_z
    patch_index = jnp.arange(PATCH, dtype=jnp.int32)
    row_place = (anchors[0][:, None, None] + patch_index[None, :, None]) * (CY + 2 * RIM) + anchors[1][:, None, None] + patch_index[None, None, :]
    row_place = row_place.reshape(anchors.shape[1], PATCH * PATCH).astype(jnp.int32)
    col_place = (anchors[2][:, None] + patch_index[None, :]).astype(jnp.int32)
    return (weighted, weight_x, slope_x, weight_y, slope_y, weight_z, slope_z, row_place, col_place)

def spread_patches(weights):
    weighted, weight_x, slope_x, weight_y, slope_y, weight_z, slope_z, row_place, col_place = weights
    block_count = weighted.shape[0]
    atom_count = weighted.shape[1]
    terms = (weighted[:, :, None, None] * weight_x[:, :, :, None] * weight_y[:, :, None, :]).reshape(block_count, atom_count, PATCH * PATCH)
    return jnp.einsum('bsm,bsz->bmz', terms, weight_z, precision=lax.Precision.HIGHEST)

def add_patches(density_rows, weights):
    row_place = weights[7]
    col_place = weights[8]
    values = spread_patches(weights)
    return density_rows.at[row_place[:, :, None], col_place[:, None, :]].add(values)

def block_forces(flat_field, weights, scale):
    weighted, weight_x, slope_x, weight_y, slope_y, weight_z, slope_z, row_place, col_place = weights
    block_count = weighted.shape[0]
    atom_count = weighted.shape[1]
    gathered = flat_field[row_place[:, :, None], col_place[:, None, :]]
    values_z = jnp.einsum('bmz,bsz->bsm', gathered, weight_z, precision=lax.Precision.HIGHEST).reshape(block_count, atom_count, PATCH, PATCH)
    slopes_z = jnp.einsum('bmz,bsz->bsm', gathered, slope_z, precision=lax.Precision.HIGHEST).reshape(block_count, atom_count, PATCH, PATCH)
    force_x = -weighted * scale[0] * jnp.einsum('bskl,bsk,bsl->bs', values_z, slope_x, weight_y, precision=lax.Precision.HIGHEST)
    force_y = -weighted * scale[1] * jnp.einsum('bskl,bsk,bsl->bs', values_z, weight_x, slope_y, precision=lax.Precision.HIGHEST)
    force_z = -weighted * scale[2] * jnp.einsum('bskl,bsk,bsl->bs', slopes_z, weight_x, weight_y, precision=lax.Precision.HIGHEST)
    return jnp.stack([force_x, force_y, force_z])

def smooth_axis(field, axis_dim, scale_axis):
    total = jnp.zeros_like(field)
    for shift_by in range(-RADIUS, RADIUS + 1):
        kernel = gaussian(jnp.float32(shift_by), SMOOTH * scale_axis)
        total = total + kernel * jnp.roll(field, shift_by, axis=axis_dim)
    return total

def reference(positions, charges, block_anchor, block_atoms, brick_blocks, box_scale):
    coords_all = positions.reshape(3, DEVICES, NB, BLOCK)
    charge_all = charges.reshape(DEVICES, NB, BLOCK)
    anchor_all = block_anchor.reshape(3, DEVICES, NB)
    filled_all = block_atoms.reshape(DEVICES, NB)
    block_index = jnp.arange(NB, dtype=jnp.int32)

    def brick_cells(device):
        first = device // (N_GY * N_GZ)
        second = device // N_GZ % N_GY
        third = device % N_GZ
        index_x = (first * CX - RIM + jnp.arange(CX + 2 * RIM, dtype=jnp.int32)) % NX
        index_y = (second * CY - RIM + jnp.arange(CY + 2 * RIM, dtype=jnp.int32)) % NY
        index_z = (third * CZ - RIM + jnp.arange(CZ + 2 * RIM, dtype=jnp.int32)) % NZ
        return (index_x, index_y, index_z)

    def brick_weights(device):
        return block_weights(coords_all[:, device], charge_all[device], anchor_all[:, device], filled_all[device], block_index, brick_blocks[device], box_scale)

    def add_brick(device, density):
        local = add_patches(jnp.zeros(((CX + 2 * RIM) * (CY + 2 * RIM), CZ + 2 * RIM), jnp.float32), brick_weights(device))
        local = local.reshape(CX + 2 * RIM, CY + 2 * RIM, CZ + 2 * RIM)
        index_x, index_y, index_z = brick_cells(device)
        return density.at[index_x[:, None, None], index_y[None, :, None], index_z[None, None, :]].add(local)
    density = lax.fori_loop(0, DEVICES, add_brick, jnp.zeros((NX, NY, NZ), jnp.float32))
    field = smooth_axis(density, 0, box_scale[0])
    field = smooth_axis(field, 1, box_scale[1])
    field = smooth_axis(field, 2, box_scale[2])
    potential = COUPLING * field

    def brick_force(device):
        index_x, index_y, index_z = brick_cells(device)
        cube = jnp.take(jnp.take(jnp.take(potential, index_x, axis=0), index_y, axis=1), index_z, axis=2)
        flat_field = cube.reshape(-1, CZ + 2 * RIM)
        return block_forces(flat_field, brick_weights(device), box_scale)
    forces_all = lax.map(brick_force, jnp.arange(DEVICES, dtype=jnp.int32))
    forces = forces_all.transpose(1, 0, 2, 3).reshape(3, ATOMS)
    return (potential, forces)
```

```python
import math
import jax, jax.numpy as jnp
from jax import lax
from jax.experimental import pallas as pl
from jax.experimental.pallas import tpu as pltpu

from jax.sharding import PartitionSpec as P

MESH = pl.DeviceIdType.MESH
CX = 24
CY = 24
CZ = 128
PATCH = 16
RIM = 4
RADIUS = 4
SPREAD = 1.0
SMOOTH = 1.5
COUPLING = 200.0
ROWS = 40
BLOCKS = 8
LANES = 128
SOURCES = 27
SLOTS = SOURCES * BLOCKS
SPAN = 32
Z_ROWS = 176
WAYS = 4
PAD = 40


def norm(width):
    return 1.0 / (math.sqrt(2.0 * math.pi) * width)


def window(coord, place, width):
    offset = coord + RIM - place.astype(jnp.float32)
    inside = (place >= 0) & (place < PATCH)
    weight = jnp.exp(-offset * offset / (2.0 * width * width)) * norm(width)
    weight = jnp.where(inside, weight, 0.0)
    return weight, -offset / (width * width) * weight


def split(value):
    high = value.astype(jnp.bfloat16)
    return high, (value - high.astype(jnp.float32)).astype(jnp.bfloat16)


def field_kernel(meta, scale_ref, atoms, potential, forces, order, tasks, starts, pad_x, pad_y, pad_z, wx_all, wy_all, wz_all, density, field):
    f32 = jnp.float32
    scales = [jnp.full((1, LANES), scale_ref[a], f32) for a in range(3)]
    widths = [SPREAD * s for s in scales]
    taps = []
    for a in range(3):
        tau = SMOOTH * scales[a]
        taps.append([jnp.exp(-float(e * e) / (2.0 * tau * tau)) * norm(tau) for e in range(RADIUS + 1)])
    density[...] = jnp.zeros_like(density)
    for ref in (pad_x, pad_y, pad_z):
        ref[...] = jnp.zeros_like(ref)
    wx_all[pl.ds(SLOTS * SPAN, SPAN), :] = jnp.zeros((SPAN, LANES), f32)
    wy_all[pl.ds(SLOTS * SPAN, SPAN), :] = jnp.zeros((SPAN, LANES), f32)
    wz_all[pl.ds(SLOTS * 24, 24), :] = jnp.zeros((24, LANES), f32)
    starts[SLOTS] = 0

    def choose(n, count):
        cx = n // 9
        cz = n // 3 % 3
        cy = n % 3
        low_x = jnp.where(cx == 1, 5, 0)
        high_x = jnp.where(cx == 2, 11, 999)
        low_y = jnp.where(cy == 1, 5, 0)
        high_y = jnp.where(cy == 2, 11, 999)
        low_z = jnp.where(cz == 1, CZ - 19, 0)
        high_z = jnp.where(cz == 2, 11, 999)
        for b in range(BLOCKS):
            x = meta[n, b]
            y = meta[n, BLOCKS + b]
            z = meta[n, 2 * BLOCKS + b]
            live = meta[n, 3 * BLOCKS + b]
            near = (x >= low_x) & (x <= high_x) & (y >= low_y) & (y <= high_y) & (z >= low_z) & (z <= high_z) & (live > 0)
            order[count] = n * BLOCKS + b
            count = count + near.astype(jnp.int32)
        return count

    blocks = lax.fori_loop(0, SOURCES, choose, jnp.int32(0))
    for extra in range(WAYS - 1):
        order[blocks + extra] = 0

    iota16 = lax.broadcasted_iota(jnp.int32, (PATCH, LANES), 0)

    def weigh(group, count):
        for way in range(WAYS):
            k = group * WAYS + way
            code = order[k]
            n = code // BLOCKS
            b = code % BLOCKS
            cx = n // 9
            cz = n // 3 % 3
            cy = n % 3
            off_x = meta[n, b] + jnp.where(cx == 0, 0, jnp.where(cx == 1, -CX, CX))
            off_y = meta[n, BLOCKS + b] + jnp.where(cy == 0, 0, jnp.where(cy == 1, -CY, CY))
            off_z = meta[n, 2 * BLOCKS + b] + jnp.where(cz == 0, 0, jnp.where(cz == 1, -CZ, CZ))
            row = n * ROWS + b
            x = atoms[pl.ds(row, 1), :] * scales[0]
            y = atoms[pl.ds(row + BLOCKS, 1), :] * scales[1]
            z = atoms[pl.ds(row + 2 * BLOCKS, 1), :] * scales[2]
            q = atoms[pl.ds(row + 3 * BLOCKS, 1), :]
            pad_x[way, pl.ds(PAD, PATCH), :] = q * window(x, iota16, widths[0])[0]
            pad_y[way, pl.ds(PAD, PATCH), :] = window(y, iota16, widths[1])[0]
            pad_z[way, pl.ds(8, PATCH), :] = window(z, iota16, widths[2])[0]
            for a, off, pad, out in ((0, off_x, pad_x, wx_all), (1, off_y, pad_y, wy_all)):
                start = PAD - off
                total = taps[a][0] * pad[way, pl.ds(start, SPAN), :]
                for e in range(1, RADIUS + 1):
                    total = total + taps[a][e] * (pad[way, pl.ds(start - e, SPAN), :] + pad[way, pl.ds(start + e, SPAN), :])
                out[pl.ds(pl.multiple_of(k * SPAN, SPAN), SPAN), :] = total
            first = off_z + 20
            shift = first % 8
            wz_all[pl.ds(pl.multiple_of(k * 24, 8), 24), :] = pad_z[way, pl.ds(8 - shift, 24), :]
            starts[k] = first - shift
            used = k < blocks
            for half in range(2):
                for side in range(2):
                    touches = used & ((cx == 0) | (cx == half + 1)) & ((cy == 0) | (cy == side + 1))
                    tasks[count] = k * 4 + half * 2 + side
                    count = count + touches.astype(jnp.int32)
        return count

    jobs = lax.fori_loop(0, (blocks + WAYS - 1) // WAYS, weigh, jnp.int32(0))
    for extra in range(WAYS - 1):
        tasks[jobs + extra] = SLOTS * 4

    def spread(group, carry):
        for way in range(WAYS):
            code = tasks[group * WAYS + way]
            k = code // 4
            half = code // 2 % 2
            side = code % 2
            wx = wx_all[pl.ds(pl.multiple_of(k * SPAN + half * 16, 16), 16), :]
            wy = wy_all[pl.ds(pl.multiple_of(k * SPAN + side * 16, 16), 16), :]
            product = (wx[:, None, :] * wy[None, :, :]).reshape(256, LANES)
            high, low = split(product)
            wz = wz_all[pl.ds(pl.multiple_of(k * 24, 8), 24), :]
            z_high = wz.astype(jnp.bfloat16).astype(f32)
            left = jnp.concatenate([z_high, wz - z_high], axis=0).astype(jnp.bfloat16)
            patch = lax.dot_general(
                jnp.concatenate([left, left], axis=1), jnp.concatenate([high, low], axis=1),
                (((1,), (1,)), ((), ())), preferred_element_type=f32)
            rows = pl.ds(pl.multiple_of((code % 4) * Z_ROWS + starts[k], 8), 24)
            density[rows, :] = density[rows, :] + patch[:24] + patch[24:]
        return carry

    lax.fori_loop(0, (jobs + WAYS - 1) // WAYS, spread, jnp.int32(0))

    length = CZ + 2 * (RIM + RADIUS)
    gap = lax.broadcasted_iota(jnp.int32, (length, length), 0) - lax.broadcasted_iota(jnp.int32, (length, length), 1)
    tau = SMOOTH * scale_ref[2]
    gap_f = gap.astype(f32)
    tau_v = jnp.full((length, length), tau, f32)
    band = jnp.exp(-gap_f * gap_f / (2.0 * tau_v * tau_v)) * (COUPLING / (math.sqrt(2.0 * math.pi) * tau_v))
    band_high, band_low = split(jnp.where(jnp.abs(gap) <= RADIUS, band, 0.0))
    for half in range(2):
        for side in range(2):
            part = density[pl.ds((half * 2 + side) * Z_ROWS + 16, length), :]
            high, low = split(part)
            smooth = (jnp.dot(band_high, high, preferred_element_type=f32)
                      + jnp.dot(band_high, low, preferred_element_type=f32)
                      + jnp.dot(band_low, high, preferred_element_type=f32))
            turned = smooth[8:8 + CZ].T
            edge = jnp.concatenate([smooth[4:8], smooth[8 + CZ:12 + CZ]], axis=0)
            edge_high = edge.astype(jnp.bfloat16).astype(f32)
            edges = jnp.concatenate([edge_high, edge - edge_high, edge_high, jnp.zeros((LANES - 24, 256), f32)], axis=0).T
            turned_high, turned_low = split(turned)
            cube = turned.reshape(16, 16, CZ)
            low_x, low_y = (1 - half) * RIM, (1 - side) * RIM
            potential[pl.ds(half * 12, 12), pl.ds(side * 12, 12), :] = cube[low_x:low_x + 12, low_y:low_y + 12, :]
            place = (pl.ds(half * 16, 16), pl.ds(side * 16, 16))
            for i, block in enumerate((turned_high, turned_low, turned_high, edges.astype(jnp.bfloat16))):
                field[place[0], place[1], pl.ds(i * LANES, LANES)] = block.reshape(16, 16, LANES)

    iota32 = lax.broadcasted_iota(jnp.int32, (SPAN, LANES), 0)
    iota_z = lax.broadcasted_iota(jnp.int32, (CZ, LANES), 0)
    iota8 = lax.broadcasted_iota(jnp.int32, (8, LANES), 0)
    edge_z = jnp.where(iota8 < 4, iota8 - 4, iota8 + (CZ - 4))

    def force(b):
        x = atoms[pl.ds(b, 1), :] * scales[0]
        y = atoms[pl.ds(b + BLOCKS, 1), :] * scales[1]
        z = atoms[pl.ds(b + 2 * BLOCKS, 1), :] * scales[2]
        q = atoms[pl.ds(b + 3 * BLOCKS, 1), :]
        at_x = meta[0, b]
        at_y = meta[0, BLOCKS + b]
        at_z = meta[0, 2 * BLOCKS + b]
        wx, sx = window(x, iota16, widths[0])
        wy, sy = window(y, iota32 - at_y, widths[1])
        wz, sz = window(z, iota_z - at_z + RIM, widths[2])
        we, se = window(z, edge_z - at_z + RIM, widths[2])
        main_high, main_low = split(jnp.concatenate([wz, sz], axis=1))
        rim = jnp.concatenate([we, se], axis=1)
        rim_high = rim.astype(jnp.bfloat16).astype(f32)
        rim = jnp.concatenate([rim_high, rim_high, rim - rim_high, jnp.zeros((LANES - 24, 256), f32)], axis=0).astype(jnp.bfloat16)
        right = jnp.concatenate([main_high, main_high, main_low, rim], axis=0)
        left = field[pl.ds(at_x, PATCH)].reshape(PATCH * SPAN, 4 * LANES)
        values = jnp.dot(left, right, preferred_element_type=f32).reshape(PATCH, SPAN, 256)
        by_sx = jnp.zeros((SPAN, LANES), f32)
        by_wx = jnp.zeros((SPAN, LANES), f32)
        by_wz = jnp.zeros((SPAN, LANES), f32)
        for i in range(PATCH):
            level = values[i, :, :LANES]
            by_sx = by_sx + level * sx[i:i + 1]
            by_wx = by_wx + level * wx[i:i + 1]
            by_wz = by_wz + values[i, :, LANES:] * wx[i:i + 1]
        for a, total in enumerate((by_sx * wy, by_wx * sy, by_wz * wy)):
            forces[a:a + 1, b * LANES:(b + 1) * LANES] = -q * scales[a] * jnp.sum(total, axis=0, keepdims=True)

    for b in range(BLOCKS):
        force(b)


def make_field(atoms, meta, box_scale):
    smem = pl.BlockSpec(memory_space=pltpu.SMEM)
    vmem = pl.BlockSpec(memory_space=pltpu.VMEM)
    f32 = jnp.float32
    return pl.pallas_call(
        field_kernel,
        out_shape=(jax.ShapeDtypeStruct((CX, CY, CZ), f32), jax.ShapeDtypeStruct((3, BLOCKS * LANES), f32)),
        in_specs=[smem, smem, vmem],
        out_specs=(vmem, vmem),
        scratch_shapes=[
            pltpu.SMEM((SLOTS + 8,), jnp.int32),
            pltpu.SMEM((SLOTS * 4 + 8,), jnp.int32),
            pltpu.SMEM((SLOTS + 8,), jnp.int32),
            pltpu.VMEM((WAYS, 96, LANES), f32),
            pltpu.VMEM((WAYS, 96, LANES), f32),
            pltpu.VMEM((WAYS, 32, LANES), f32),
            pltpu.VMEM(((SLOTS + 4) * SPAN, LANES), f32),
            pltpu.VMEM(((SLOTS + 4) * SPAN, LANES), f32),
            pltpu.VMEM(((SLOTS + 4) * 24, LANES), f32),
            pltpu.VMEM((4 * Z_ROWS, 256), f32),
            pltpu.VMEM((SPAN, SPAN, 4 * LANES), jnp.bfloat16),
        ],
        compiler_params=pltpu.CompilerParams(vmem_limit_bytes=40 * 1024 * 1024),
        name="field_and_forces",
    )(meta, box_scale, atoms.reshape(SOURCES * ROWS, LANES))


def exchange_kernel(pos_ref, q_ref, anchor_ref, atoms_ref, blocks_ref, atoms_out, meta_out, send_sems, recv_sems):
    me = {a: lax.axis_index(a) for a in ("gx", "gy", "gz")}
    def near(axis, step):
        n = lax.axis_size(axis)
        return {axis: lax.rem(me[axis] + step + n, n)}
    barrier = pltpu.get_barrier_semaphore()
    for axis in ("gy", "gz", "gx"):
        for step in (1, -1):
            pl.semaphore_signal(barrier, inc=1, device_id=near(axis, step), device_id_type=MESH)
    far = {1: lax.rem(me["gy"], 4) == 3, -1: lax.rem(me["gy"], 4) == 0}
    wrap = {1: me["gz"] == lax.axis_size("gz") - 1, -1: me["gz"] == 0}
    corners = [(sy, sz) for sy in (1, -1) for sz in (1, -1)]
    def corner_id(sy, sz):
        return {**near("gy", sy), **near("gz", sz)}
    for sy, sz in corners:
        @pl.when(far[sy] & wrap[sz])
        def _():
            pl.semaphore_signal(barrier, inc=1, device_id=corner_id(sy, sz), device_id_type=MESH)
    for a in range(3):
        for b in range(8):
            atoms_out[0, pl.ds(a * 8 + b, 1), :] = pos_ref[pl.ds(a, 1), pl.ds(b * 128, 128)]
    row = lax.broadcasted_iota(jnp.int32, (8, 128), 0)
    lane = lax.broadcasted_iota(jnp.int32, (8, 128), 1)
    filled = jnp.zeros((8, 128), jnp.int32)
    for b in range(8):
        filled = jnp.where(row == b, jnp.where(b < blocks_ref[0], atoms_ref[b], 0), filled)
    atoms_out[0, pl.ds(24, 8), :] = jnp.where(lane < filled, q_ref[...], 0.0)
    meta = jnp.zeros((8, 128), jnp.int32)
    for a in range(3):
        for b in range(8):
            meta = jnp.where(lane == a * 8 + b, anchor_ref[a, b], meta)
    for b in range(8):
        meta = jnp.where(lane == 24 + b, jnp.where(b < blocks_ref[0], 1, 0), meta)
    atoms_out[0, pl.ds(32, 8), :] = meta.astype(jnp.float32)
    at_corner = (far[1] | far[-1]) & (wrap[1] | wrap[-1])
    pl.semaphore_wait(barrier, 6 + at_corner.astype(jnp.int32))

    def slot(cx, cz, cy):
        return (cx * 3 + cz) * 3 + cy
    code = {1: 1, -1: 2}
    def piece(src, dst, target, send_index=None):
        return pltpu.make_async_remote_copy(
            src_ref=atoms_out.at[src], dst_ref=atoms_out.at[dst],
            send_sem=send_sems.at[dst if send_index is None else send_index], recv_sem=recv_sems.at[dst],
            device_id=target, device_id_type=MESH)
    def y_piece(step):
        return piece(0, slot(0, 0, code[step]), near("gy", step))
    def z_piece(cy, step):
        return piece(slot(0, 0, cy), slot(0, code[step], cy), near("gz", step))
    def x_piece(cz, cy, step):
        return piece(slot(0, cz, cy), slot(code[step], cz, cy), near("gx", step))
    def corner_piece(k, sy, sz):
        return piece(0, slot(0, code[sz], code[sy]), corner_id(sy, sz), 27 + k)
    def relays(cy, step):
        return jnp.logical_not((far[-1] if cy == 1 else far[1]) & wrap[step])
    for step in (1, -1):
        y_piece(step).start()
    for k, (sy, sz) in enumerate(corners):
        @pl.when(far[sy] & wrap[sz])
        def _():
            corner_piece(k, sy, sz).start()
    for step in (1, -1):
        z_piece(0, step).start()
    for step in (1, -1):
        x_piece(0, 0, step).start()
    def send_y_on(cy):
        y_piece(1 if cy == 1 else -1).wait_recv()
        for step in (1, -1):
            @pl.when(relays(cy, step))
            def _():
                z_piece(cy, step).start()
        for step in (1, -1):
            x_piece(0, cy, step).start()
    def send_z_on(cz, cy):
        z_piece(cy, 1 if cz == 1 else -1).wait_recv()
        for step in (1, -1):
            x_piece(cz, cy, step).start()
    low = lax.rem(me["gy"], 4) == 0
    @pl.when(low)
    def _():
        send_y_on(2)
        send_z_on(1, 0)
        send_z_on(2, 0)
        send_z_on(1, 2)
        send_z_on(2, 2)
        send_y_on(1)
        send_z_on(1, 1)
        send_z_on(2, 1)
    @pl.when(jnp.logical_not(low))
    def _():
        send_y_on(1)
        send_z_on(1, 0)
        send_z_on(2, 0)
        send_z_on(1, 1)
        send_z_on(2, 1)
        send_y_on(2)
        send_z_on(1, 2)
        send_z_on(2, 2)
    for step in (1, -1):
        for cz in range(3):
            for cy in range(3):
                x_piece(cz, cy, step).wait_recv()
    for step in (1, -1):
        y_piece(step).wait_send()
        for cz in range(3):
            for cy in range(3):
                x_piece(cz, cy, step).wait_send()
        z_piece(0, step).wait_send()
        for cy in (1, 2):
            @pl.when(relays(cy, step))
            def _():
                z_piece(cy, step).wait_send()
    for k, (sy, sz) in enumerate(corners):
        @pl.when(far[sy] & wrap[sz])
        def _():
            corner_piece(k, sy, sz).wait_send()
    for n in range(27):
        meta_out[pl.ds(n, 1), :] = atoms_out[n, pl.ds(32, 1), :].astype(jnp.int32)

def exchange(positions, charges, block_anchor, block_atoms, brick_blocks):
    smem = pl.BlockSpec(memory_space=pltpu.SMEM)
    vmem = pl.BlockSpec(memory_space=pltpu.VMEM)
    return pl.pallas_call(
        exchange_kernel,
        out_shape=(jax.ShapeDtypeStruct((27, ROWS, 128), jnp.float32), jax.ShapeDtypeStruct((32, 128), jnp.int32)),
        in_specs=[vmem, vmem, smem, smem, smem],
        out_specs=(vmem, vmem),
        scratch_shapes=[pltpu.SemaphoreType.DMA((32,)), pltpu.SemaphoreType.DMA((27,))],
        compiler_params=pltpu.CompilerParams(collective_id=0, has_side_effects=True),
        name="exchange_atoms",
    )(positions, charges.reshape(8, 128), block_anchor, block_atoms, brick_blocks)


def per_device(positions, charges, block_anchor, block_atoms, brick_blocks, box_scale):
    atoms, meta = exchange(positions, charges, block_anchor, block_atoms, brick_blocks)
    potential, forces = make_field(atoms, meta, box_scale)
    return (potential, forces)


def solution(mesh):
    split_all = ("gx", "gy", "gz")
    return jax.shard_map(
        per_device,
        mesh=mesh,
        in_specs=(P(None, split_all), P(split_all), P(None, split_all), P(split_all), P(split_all), P()),
        out_specs=(P("gx", "gy", "gz"), P(None, split_all)),
        check_vma=False,
    )
```

```python
import math
import jax, jax.numpy as jnp
from jax import lax
from jax.experimental import pallas as pl
from jax.experimental.pallas import tpu as pltpu

from jax.sharding import PartitionSpec as P

MESH = pl.DeviceIdType.MESH
CX = 24
CY = 24
CZ = 128
PATCH = 16
RIM = 4
RADIUS = 4
SPREAD = 1.0
SMOOTH = 1.5
COUPLING = 200.0
ROWS = 40
BLOCKS = 8
LANES = 128
SOURCES = 27
SLOTS = SOURCES * BLOCKS
SPAN = 32
Z_ROWS = 176
WAYS = 4
PAD = 40


def norm(width):
    return 1.0 / (math.sqrt(2.0 * math.pi) * width)


def window(coord, place, width):
    offset = coord + RIM - place.astype(jnp.float32)
    inside = (place >= 0) & (place < PATCH)
    weight = jnp.exp(-offset * offset / (2.0 * width * width)) * norm(width)
    weight = jnp.where(inside, weight, 0.0)
    return weight, -offset / (width * width) * weight


def split(value):
    high = value.astype(jnp.bfloat16)
    return high, (value - high.astype(jnp.float32)).astype(jnp.bfloat16)


def field_kernel(meta, scale_ref, atoms, potential, forces, order, tasks, starts, pad_x, pad_y, pad_z, wx_all, wy_all, wz_all, density, field):
    f32 = jnp.float32
    scales = [jnp.full((1, LANES), scale_ref[a], f32) for a in range(3)]
    widths = [SPREAD * s for s in scales]
    taps = []
    for a in range(3):
        tau = SMOOTH * scales[a]
        taps.append([jnp.exp(-float(e * e) / (2.0 * tau * tau)) * norm(tau) for e in range(RADIUS + 1)])
    density[...] = jnp.zeros_like(density)
    for ref in (pad_x, pad_y, pad_z):
        ref[...] = jnp.zeros_like(ref)
    wx_all[pl.ds(SLOTS * SPAN, SPAN), :] = jnp.zeros((SPAN, LANES), f32)
    wy_all[pl.ds(SLOTS * SPAN, SPAN), :] = jnp.zeros((SPAN, LANES), f32)
    wz_all[pl.ds(SLOTS * 24, 24), :] = jnp.zeros((24, LANES), f32)
    starts[SLOTS] = 0

    def choose(n, count):
        cx = n // 9
        cz = n // 3 % 3
        cy = n % 3
        low_x = jnp.where(cx == 1, 5, 0)
        high_x = jnp.where(cx == 2, 11, 999)
        low_y = jnp.where(cy == 1, 5, 0)
        high_y = jnp.where(cy == 2, 11, 999)
        low_z = jnp.where(cz == 1, CZ - 19, 0)
        high_z = jnp.where(cz == 2, 11, 999)
        for b in range(BLOCKS):
            x = meta[n, b]
            y = meta[n, BLOCKS + b]
            z = meta[n, 2 * BLOCKS + b]
            live = meta[n, 3 * BLOCKS + b]
            near = (x >= low_x) & (x <= high_x) & (y >= low_y) & (y <= high_y) & (z >= low_z) & (z <= high_z) & (live > 0)
            order[count] = n * BLOCKS + b
            count = count + near.astype(jnp.int32)
        return count

    blocks = lax.fori_loop(0, SOURCES, choose, jnp.int32(0))
    for extra in range(WAYS - 1):
        order[blocks + extra] = 0

    iota16 = lax.broadcasted_iota(jnp.int32, (PATCH, LANES), 0)

    def weigh(group, count):
        for way in range(WAYS):
            k = group * WAYS + way
            code = order[k]
            n = code // BLOCKS
            b = code % BLOCKS
            cx = n // 9
            cz = n // 3 % 3
            cy = n % 3
            off_x = meta[n, b] + jnp.where(cx == 0, 0, jnp.where(cx == 1, -CX, CX))
            off_y = meta[n, BLOCKS + b] + jnp.where(cy == 0, 0, jnp.where(cy == 1, -CY, CY))
            off_z = meta[n, 2 * BLOCKS + b] + jnp.where(cz == 0, 0, jnp.where(cz == 1, -CZ, CZ))
            row = n * ROWS + b
            x = atoms[pl.ds(row, 1), :] * scales[0]
            y = atoms[pl.ds(row + BLOCKS, 1), :] * scales[1]
            z = atoms[pl.ds(row + 2 * BLOCKS, 1), :] * scales[2]
            q = atoms[pl.ds(row + 3 * BLOCKS, 1), :]
            pad_x[way, pl.ds(PAD, PATCH), :] = q * window(x, iota16, widths[0])[0]
            pad_y[way, pl.ds(PAD, PATCH), :] = window(y, iota16, widths[1])[0]
            pad_z[way, pl.ds(8, PATCH), :] = window(z, iota16, widths[2])[0]
            for a, off, pad, out in ((0, off_x, pad_x, wx_all), (1, off_y, pad_y, wy_all)):
                start = PAD - off
                total = taps[a][0] * pad[way, pl.ds(start, SPAN), :]
                for e in range(1, RADIUS + 1):
                    total = total + taps[a][e] * (pad[way, pl.ds(start - e, SPAN), :] + pad[way, pl.ds(start + e, SPAN), :])
                out[pl.ds(pl.multiple_of(k * SPAN, SPAN), SPAN), :] = total
            first = off_z + 20
            shift = first % 8
            wz_all[pl.ds(pl.multiple_of(k * 24, 8), 24), :] = pad_z[way, pl.ds(8 - shift, 24), :]
            starts[k] = first - shift
            used = k < blocks
            for half in range(2):
                for side in range(2):
                    touches = used & ((cx == 0) | (cx == half + 1)) & ((cy == 0) | (cy == side + 1))
                    tasks[count] = k * 4 + half * 2 + side
                    count = count + touches.astype(jnp.int32)
        return count

    jobs = lax.fori_loop(0, (blocks + WAYS - 1) // WAYS, weigh, jnp.int32(0))
    for extra in range(WAYS - 1):
        tasks[jobs + extra] = SLOTS * 4

    def spread(group, carry):
        for way in range(WAYS):
            code = tasks[group * WAYS + way]
            k = code // 4
            half = code // 2 % 2
            side = code % 2
            wx = wx_all[pl.ds(pl.multiple_of(k * SPAN + half * 16, 16), 16), :]
            wy = wy_all[pl.ds(pl.multiple_of(k * SPAN + side * 16, 16), 16), :]
            product = (wx[:, None, :] * wy[None, :, :]).reshape(256, LANES)
            high, low = split(product)
            wz = wz_all[pl.ds(pl.multiple_of(k * 24, 8), 24), :]
            z_high = wz.astype(jnp.bfloat16).astype(f32)
            left = jnp.concatenate([z_high, wz - z_high], axis=0).astype(jnp.bfloat16)
            patch = lax.dot_general(
                jnp.concatenate([left, left], axis=1), jnp.concatenate([high, low], axis=1),
                (((1,), (1,)), ((), ())), preferred_element_type=f32)
            rows = pl.ds(pl.multiple_of((code % 4) * Z_ROWS + starts[k], 8), 24)
            density[rows, :] = density[rows, :] + patch[:24] + patch[24:]
        return carry

    lax.fori_loop(0, (jobs + WAYS - 1) // WAYS, spread, jnp.int32(0))

    length = CZ + 2 * (RIM + RADIUS)
    gap = lax.broadcasted_iota(jnp.int32, (length, length), 0) - lax.broadcasted_iota(jnp.int32, (length, length), 1)
    tau = SMOOTH * scale_ref[2]
    gap_f = gap.astype(f32)
    tau_v = jnp.full((length, length), tau, f32)
    band = jnp.exp(-gap_f * gap_f / (2.0 * tau_v * tau_v)) * (COUPLING / (math.sqrt(2.0 * math.pi) * tau_v))
    band_high, band_low = split(jnp.where(jnp.abs(gap) <= RADIUS, band, 0.0))
    for half in range(2):
        for side in range(2):
            part = density[pl.ds((half * 2 + side) * Z_ROWS + 16, length), :]
            high, low = split(part)
            smooth = (jnp.dot(band_high, high, preferred_element_type=f32)
                      + jnp.dot(band_high, low, preferred_element_type=f32)
                      + jnp.dot(band_low, high, preferred_element_type=f32))
            turned = smooth[8:8 + CZ].T
            edge = jnp.concatenate([smooth[4:8], smooth[8 + CZ:12 + CZ]], axis=0)
            edge_high = edge.astype(jnp.bfloat16).astype(f32)
            edges = jnp.concatenate([edge_high, edge - edge_high, edge_high, jnp.zeros((LANES - 24, 256), f32)], axis=0).T
            turned_high, turned_low = split(turned)
            cube = turned.reshape(16, 16, CZ)
            low_x, low_y = (1 - half) * RIM, (1 - side) * RIM
            potential[pl.ds(half * 12, 12), pl.ds(side * 12, 12), :] = cube[low_x:low_x + 12, low_y:low_y + 12, :]
            place = (pl.ds(half * 16, 16), pl.ds(side * 16, 16))
            for i, block in enumerate((turned_high, turned_low, turned_high, edges.astype(jnp.bfloat16))):
                field[place[0], place[1], pl.ds(i * LANES, LANES)] = block.reshape(16, 16, LANES)

    iota32 = lax.broadcasted_iota(jnp.int32, (SPAN, LANES), 0)
    iota_z = lax.broadcasted_iota(jnp.int32, (CZ, LANES), 0)
    iota8 = lax.broadcasted_iota(jnp.int32, (8, LANES), 0)
    edge_z = jnp.where(iota8 < 4, iota8 - 4, iota8 + (CZ - 4))

    def force(b):
        x = atoms[pl.ds(b, 1), :] * scales[0]
        y = atoms[pl.ds(b + BLOCKS, 1), :] * scales[1]
        z = atoms[pl.ds(b + 2 * BLOCKS, 1), :] * scales[2]
        q = atoms[pl.ds(b + 3 * BLOCKS, 1), :]
        at_x = meta[0, b]
        at_y = meta[0, BLOCKS + b]
        at_z = meta[0, 2 * BLOCKS + b]
        wx, sx = window(x, iota16, widths[0])
        wy, sy = window(y, iota32 - at_y, widths[1])
        wz, sz = window(z, iota_z - at_z + RIM, widths[2])
        we, se = window(z, edge_z - at_z + RIM, widths[2])
        main_high, main_low = split(jnp.concatenate([wz, sz], axis=1))
        rim = jnp.concatenate([we, se], axis=1)
        rim_high = rim.astype(jnp.bfloat16).astype(f32)
        rim = jnp.concatenate([rim_high, rim_high, rim - rim_high, jnp.zeros((LANES - 24, 256), f32)], axis=0).astype(jnp.bfloat16)
        right = jnp.concatenate([main_high, main_high, main_low, rim], axis=0)
        left = field[pl.ds(at_x, PATCH)].reshape(PATCH * SPAN, 4 * LANES)
        values = jnp.dot(left, right, preferred_element_type=f32).reshape(PATCH, SPAN, 256)
        by_sx = jnp.zeros((SPAN, LANES), f32)
        by_wx = jnp.zeros((SPAN, LANES), f32)
        by_wz = jnp.zeros((SPAN, LANES), f32)
        for i in range(PATCH):
            level = values[i, :, :LANES]
            by_sx = by_sx + level * sx[i:i + 1]
            by_wx = by_wx + level * wx[i:i + 1]
            by_wz = by_wz + values[i, :, LANES:] * wx[i:i + 1]
        for a, total in enumerate((by_sx * wy, by_wx * sy, by_wz * wy)):
            forces[a:a + 1, b * LANES:(b + 1) * LANES] = -q * scales[a] * jnp.sum(total, axis=0, keepdims=True)

    for b in range(BLOCKS):
        force(b)


def make_field(atoms, meta, box_scale):
    smem = pl.BlockSpec(memory_space=pltpu.SMEM)
    vmem = pl.BlockSpec(memory_space=pltpu.VMEM)
    f32 = jnp.float32
    return pl.pallas_call(
        field_kernel,
        out_shape=(jax.ShapeDtypeStruct((CX, CY, CZ), f32), jax.ShapeDtypeStruct((3, BLOCKS * LANES), f32)),
        in_specs=[smem, smem, vmem],
        out_specs=(vmem, vmem),
        scratch_shapes=[
            pltpu.SMEM((SLOTS + 8,), jnp.int32),
            pltpu.SMEM((SLOTS * 4 + 8,), jnp.int32),
            pltpu.SMEM((SLOTS + 8,), jnp.int32),
            pltpu.VMEM((WAYS, 96, LANES), f32),
            pltpu.VMEM((WAYS, 96, LANES), f32),
            pltpu.VMEM((WAYS, 32, LANES), f32),
            pltpu.VMEM(((SLOTS + 4) * SPAN, LANES), f32),
            pltpu.VMEM(((SLOTS + 4) * SPAN, LANES), f32),
            pltpu.VMEM(((SLOTS + 4) * 24, LANES), f32),
            pltpu.VMEM((4 * Z_ROWS, 256), f32),
            pltpu.VMEM((SPAN, SPAN, 4 * LANES), jnp.bfloat16),
        ],
        compiler_params=pltpu.CompilerParams(vmem_limit_bytes=40 * 1024 * 1024),
        name="field_and_forces",
    )(meta, box_scale, atoms.reshape(SOURCES * ROWS, LANES))


def exchange_kernel(pos_ref, q_ref, anchor_ref, atoms_ref, blocks_ref, atoms_out, meta_out, send_sems, recv_sems, ready_sems):
    gx, gy, gz = (lax.axis_index(a) for a in ("gx", "gy", "gz"))
    nx, ny, nz = (lax.axis_size(a) for a in ("gx", "gy", "gz"))
    half = ny // 2

    def device(dx, dy, dz):
        return (lax.rem(gx + dx + nx, nx), lax.rem(gy + dy + ny, ny), lax.rem(gz + dz + nz, nz))

    late = gy >= half
    far = {1: lax.rem(gy, half) == half - 1, -1: lax.rem(gy, half) == 0}
    wrap = {1: gz == nz - 1, -1: gz == 0}
    far_any = far[1] | far[-1]
    corner = far_any & (wrap[1] | wrap[-1])
    far_step = jnp.where(far[1], 1, -1)
    wrap_step = jnp.where(wrap[1], 1, -1)
    steps = (1, -1)
    code = {1: 1, -1: 2}
    across = (0, 1, -1)
    ready_z, ready_y, ready_c = (ready_sems.at[i] for i in range(3))

    def when(condition, action):
        pl.when(condition)(action)

    def both(condition, other):
        return condition & jnp.logical_not(other)

    def signal(semaphore, *offsets):
        pl.semaphore_signal(semaphore, inc=1, device_id=device(*offsets), device_id_type=MESH)

    barrier = pltpu.get_barrier_semaphore()

    def greet_far():
        signal(barrier, 0, far_step, 0)

    def greet_corner():
        for dx in across:
            signal(barrier, dx, far_step, wrap_step)

    def greet_wrap(step):
        for dx in across:
            signal(barrier, dx, 0, step)

    when(both(far_any, late), greet_far)
    when(both(corner, late), greet_corner)
    for step in steps:
        signal(barrier, step, 0, 0)
        when(jnp.logical_not(far[step]), lambda: signal(barrier, 0, step, 0))
    greet_wrap(-1)
    when(jnp.logical_not(wrap[1]), lambda: greet_wrap(1))
    for a in range(3):
        for b in range(8):
            atoms_out[0, pl.ds(a * 8 + b, 1), :] = pos_ref[pl.ds(a, 1), pl.ds(b * 128, 128)]
    row = lax.broadcasted_iota(jnp.int32, (8, 128), 0)
    lane = lax.broadcasted_iota(jnp.int32, (8, 128), 1)
    filled = jnp.zeros((8, 128), jnp.int32)
    for b in range(8):
        filled = jnp.where(row == b, jnp.where(b < blocks_ref[0], atoms_ref[b], 0), filled)
    atoms_out[0, pl.ds(24, 8), :] = jnp.where(lane < filled, q_ref[...], 0.0)
    meta = jnp.zeros((8, 128), jnp.int32)
    for a in range(3):
        for b in range(8):
            meta = jnp.where(lane == a * 8 + b, anchor_ref[a, b], meta)
    for b in range(8):
        meta = jnp.where(lane == 24 + b, jnp.where(b < blocks_ref[0], 1, 0), meta)
    atoms_out[0, pl.ds(32, 8), :] = meta.astype(jnp.float32)
    peers = 7 + jnp.where(wrap[-1], 0, 3) - jnp.where(both(far_any, late), 1, 0) + jnp.where(corner & late, 3, 0)
    pl.semaphore_wait(barrier, peers)

    def answer_wrap():
        for dx in across:
            signal(ready_z, dx, 0, 1)

    def answer_corner():
        for dx in across:
            signal(ready_c, dx, far_step, wrap_step)

    when(far_any & late, lambda: signal(ready_y, 0, far_step, 0))
    when(wrap[1], answer_wrap)
    when(corner & late, answer_corner)

    def slot(cx, cz, cy):
        return (cx * 3 + cz) * 3 + cy

    def piece(src, dst, target, index):
        return pltpu.make_async_remote_copy(
            src_ref=atoms_out.at[src], dst_ref=atoms_out.at[dst],
            send_sem=send_sems.at[index], recv_sem=recv_sems.at[dst],
            device_id=target, device_id_type=MESH)

    def along_y(step):
        dst = slot(0, 0, code[step])
        return [piece(0, dst, device(0, step, 0), dst)]

    def along_x(cy):
        return [piece(cy, slot(code[dx], 0, cy), device(dx, 0, 0), slot(code[dx], 0, cy)) for dx in steps]

    def fan(cy, step):
        places = [(dx, slot(code[dx] if dx else 0, code[step], cy)) for dx in across]
        return [piece(cy, dst, device(dx, 0, step), dst) for dx, dst in places]

    def corners():
        out = []
        for i, dx in enumerate(across):
            dst = slot(code[dx] if dx else 0, jnp.where(wrap[1], 1, 2), jnp.where(far[1], 1, 2))
            out.append(piece(0, dst, device(dx, far_step, wrap_step), 27 + i))
        return out

    def start(copies):
        for copy in copies:
            copy.start()

    def finish(copies):
        for copy in copies:
            copy.wait_send()

    from_far = {1: far[-1], 2: far[1]}

    def send_early(cy):
        start(along_x(cy))
        start(fan(cy, 1))
        when(jnp.logical_not(wrap[-1]), lambda: start(fan(cy, -1)))

    def pass_near(cy):
        along_y(1 if cy == 1 else -1)[0].wait_recv()
        send_early(cy)

    def pass_far(cy):
        along_y(1 if cy == 1 else -1)[0].wait_recv()
        start(along_x(cy))
        for step in steps:
            when(jnp.logical_not(wrap[step]), lambda: start(fan(cy, step)))

    def open_wrap():
        pl.semaphore_wait(ready_z, 3)
        start(fan(0, -1))
        for cy in (1, 2):
            when(jnp.logical_not(from_far[cy]), lambda: start(fan(cy, -1)))

    def open_corner():
        pl.semaphore_wait(ready_c, 3)
        start(corners())

    def open_far():
        pl.semaphore_wait(ready_y, 1)
        for step in steps:
            when(far[step], lambda: start(along_y(step)))

    for step in steps:
        when(jnp.logical_not(both(far[step], late)), lambda: start(along_y(step)))
    when(corner & late, lambda: start(corners()))
    send_early(0)
    for cy in (1, 2):
        when(jnp.logical_not(from_far[cy]), lambda: pass_near(cy))
    when(wrap[-1], open_wrap)
    when(both(corner, late), open_corner)
    when(both(far_any, late), open_far)
    for cy in (1, 2):
        when(from_far[cy], lambda: pass_far(cy))
    for cy in range(3):
        for copy in along_x(cy) + fan(cy, 1) + fan(cy, -1):
            copy.wait_recv()
    for step in steps:
        finish(along_y(step))
    for cy in range(3):
        finish(along_x(cy))
        for step in steps:
            if cy == 0:
                finish(fan(cy, step))
            else:
                when(jnp.logical_not(from_far[cy] & wrap[step]), lambda: finish(fan(cy, step)))
    when(corner, lambda: finish(corners()))
    for n in range(27):
        meta_out[pl.ds(n, 1), :] = atoms_out[n, pl.ds(32, 1), :].astype(jnp.int32)

def exchange(positions, charges, block_anchor, block_atoms, brick_blocks):
    smem = pl.BlockSpec(memory_space=pltpu.SMEM)
    vmem = pl.BlockSpec(memory_space=pltpu.VMEM)
    return pl.pallas_call(
        exchange_kernel,
        out_shape=(jax.ShapeDtypeStruct((27, ROWS, 128), jnp.float32), jax.ShapeDtypeStruct((32, 128), jnp.int32)),
        in_specs=[vmem, vmem, smem, smem, smem],
        out_specs=(vmem, vmem),
        scratch_shapes=[pltpu.SemaphoreType.DMA((32,)), pltpu.SemaphoreType.DMA((27,)),
                        pltpu.SemaphoreType.REGULAR((3,))],
        compiler_params=pltpu.CompilerParams(collective_id=0, has_side_effects=True),
        name="exchange_atoms",
    )(positions, charges.reshape(8, 128), block_anchor, block_atoms, brick_blocks)


def per_device(positions, charges, block_anchor, block_atoms, brick_blocks, box_scale):
    atoms, meta = exchange(positions, charges, block_anchor, block_atoms, brick_blocks)
    potential, forces = make_field(atoms, meta, box_scale)
    return (potential, forces)


def solution(mesh):
    split_all = ("gx", "gy", "gz")
    return jax.shard_map(
        per_device,
        mesh=mesh,
        in_specs=(P(None, split_all), P(split_all), P(None, split_all), P(split_all), P(split_all), P()),
        out_specs=(P("gx", "gy", "gz"), P(None, split_all)),
        check_vma=False,
    )
```

```python
import math
import jax, jax.numpy as jnp
from jax import lax
from jax.experimental import pallas as pl
from jax.experimental.pallas import tpu as pltpu

from jax.sharding import PartitionSpec as P

MESH = pl.DeviceIdType.MESH
CX = 24
CY = 24
CZ = 128
PATCH = 16
RIM = 4
RADIUS = 4
SPREAD = 1.0
SMOOTH = 1.5
COUPLING = 200.0
ROWS = 33
ONE_SIDED = 3
BLOCKS = 8
LANES = 128
SOURCES = 27
SLOTS = SOURCES * BLOCKS
SPAN = 32
Z_ROWS = 176
WAYS = 16
EMPTY = SLOTS + WAYS
PAD = 40


def norm(width):
    return 1.0 / (math.sqrt(2.0 * math.pi) * width)


def window(coord, place, width):
    offset = coord + RIM - place.astype(jnp.float32)
    inside = (place >= 0) & (place < PATCH)
    weight = jnp.exp(-offset * offset / (2.0 * width * width)) * norm(width)
    weight = jnp.where(inside, weight, 0.0)
    return weight, -offset / (width * width) * weight


def split(value):
    high = value.astype(jnp.bfloat16)
    return high, (value - high.astype(jnp.float32)).astype(jnp.bfloat16)


def field_kernel(meta_in, atoms_in, potential, forces, meta, atoms, load_sems, order, tasks, starts, pad_x, pad_y, pad_z, wx_all, wy_all, wz_all, density, field):
    f32 = jnp.float32
    load_meta = pltpu.make_async_copy(meta_in, meta, load_sems.at[0])
    load_meta.start()
    load_atoms = pltpu.make_async_copy(atoms_in, atoms, load_sems.at[1])
    load_atoms.start()
    density[...] = jnp.zeros_like(density)
    for ref in (pad_x, pad_y, pad_z):
        ref[...] = jnp.zeros_like(ref)
    wx_all[pl.ds(EMPTY * SPAN, SPAN), :] = jnp.zeros((SPAN, LANES), f32)
    wy_all[pl.ds(EMPTY * SPAN, SPAN), :] = jnp.zeros((SPAN, LANES), f32)
    wz_all[pl.ds(EMPTY * 24, 24), :] = jnp.zeros((24, LANES), f32)
    starts[EMPTY] = 0
    load_meta.wait()

    def choose(n, count):
        for b in range(BLOCKS):
            order[count] = n * BLOCKS + b
            count = count + meta[n, 4 * BLOCKS + b]
        return count

    blocks = lax.fori_loop(0, SOURCES, choose, jnp.int32(0))
    for extra in range(WAYS - 1):
        order[blocks + extra] = 0
    load_atoms.wait()
    scales = [atoms[SOURCES, pl.ds(a, 1), :] for a in range(3)]
    widths = [SPREAD * s for s in scales]
    taps = []
    for a in range(3):
        tau = SMOOTH * scales[a]
        taps.append([jnp.exp(-float(e * e) / (2.0 * tau * tau)) * norm(tau) for e in range(RADIUS + 1)])

    iota16 = lax.broadcasted_iota(jnp.int32, (PATCH, LANES), 0)

    def weigh(group, count):
        for way in range(WAYS):
            k = group * WAYS + way
            code = order[k]
            n = code // BLOCKS
            b = code % BLOCKS
            cx = n // 9
            cy = n % 3
            off_x = meta[n, b]
            off_y = meta[n, BLOCKS + b]
            off_z = meta[n, 2 * BLOCKS + b]
            x = atoms[n, pl.ds(b, 1), :] * scales[0]
            y = atoms[n, pl.ds(b + BLOCKS, 1), :] * scales[1]
            z = atoms[n, pl.ds(b + 2 * BLOCKS, 1), :] * scales[2]
            q = atoms[n, pl.ds(b + 3 * BLOCKS, 1), :]
            pad_x[way, pl.ds(PAD, PATCH), :] = q * window(x, iota16, widths[0])[0]
            pad_y[way, pl.ds(PAD, PATCH), :] = window(y, iota16, widths[1])[0]
            pad_z[way, pl.ds(8, PATCH), :] = window(z, iota16, widths[2])[0]
            for a, off, pad, out in ((0, off_x, pad_x, wx_all), (1, off_y, pad_y, wy_all)):
                start = PAD - off
                total = taps[a][0] * pad[way, pl.ds(start, SPAN), :]
                for e in range(1, RADIUS + 1):
                    total = total + taps[a][e] * (pad[way, pl.ds(start - e, SPAN), :] + pad[way, pl.ds(start + e, SPAN), :])
                out[pl.ds(pl.multiple_of(k * SPAN, SPAN), SPAN), :] = total
            first = off_z + 20
            shift = first & 7
            wz_all[pl.ds(pl.multiple_of(k * 24, 8), 24), :] = pad_z[way, pl.ds(8 - shift, 24), :]
            starts[k] = first - shift
            used = k < blocks
            for half in range(2):
                for side in range(2):
                    touches = used & ((cx == 0) | (cx == half + 1)) & ((cy == 0) | (cy == side + 1))
                    tasks[count] = k * 4 + half * 2 + side
                    count = count + touches.astype(jnp.int32)
        return count

    jobs = lax.fori_loop(0, (blocks + WAYS - 1) // WAYS, weigh, jnp.int32(0))
    for extra in range(WAYS - 1):
        tasks[jobs + extra] = EMPTY * 4

    def spread(group, carry):
        for way in range(WAYS):
            code = tasks[group * WAYS + way]
            k = code // 4
            half = code // 2 % 2
            side = code % 2
            wx = wx_all[pl.ds(pl.multiple_of(k * SPAN + half * 16, 16), 16), :]
            wy = wy_all[pl.ds(pl.multiple_of(k * SPAN + side * 16, 16), 16), :]
            product = (wx[:, None, :] * wy[None, :, :]).reshape(256, LANES)
            high, low = split(product)
            wz = wz_all[pl.ds(pl.multiple_of(k * 24, 8), 24), :]
            z_high = wz.astype(jnp.bfloat16).astype(f32)
            left = jnp.concatenate([z_high, wz - z_high], axis=0).astype(jnp.bfloat16)
            patch = lax.dot_general(
                jnp.concatenate([left, left], axis=1), jnp.concatenate([high, low], axis=1),
                (((1,), (1,)), ((), ())), preferred_element_type=f32)
            rows = pl.ds(pl.multiple_of((code % 4) * Z_ROWS + starts[k], 8), 24)
            density[rows, :] = density[rows, :] + patch[:24] + patch[24:]
        return carry

    lax.fori_loop(0, (jobs + WAYS - 1) // WAYS, spread, jnp.int32(0))

    length = CZ + 2 * (RIM + RADIUS)
    gap = lax.broadcasted_iota(jnp.int32, (length, length), 0) - lax.broadcasted_iota(jnp.int32, (length, length), 1)
    gap_f = gap.astype(f32)
    tau_v = jnp.broadcast_to(SMOOTH * scales[2][:, :1], (length, length))
    band = jnp.exp(-gap_f * gap_f / (2.0 * tau_v * tau_v)) * (COUPLING / (math.sqrt(2.0 * math.pi) * tau_v))
    band_high, band_low = split(jnp.where(jnp.abs(gap) <= RADIUS, band, 0.0))
    for half in range(2):
        for side in range(2):
            part = density[pl.ds((half * 2 + side) * Z_ROWS + 16, length), :]
            high, low = split(part)
            smooth = (jnp.dot(band_high, high, preferred_element_type=f32)
                      + jnp.dot(band_high, low, preferred_element_type=f32)
                      + jnp.dot(band_low, high, preferred_element_type=f32))
            turned = smooth[8:8 + CZ].T
            edge = jnp.concatenate([smooth[4:8], smooth[8 + CZ:12 + CZ]], axis=0)
            edge_high = edge.astype(jnp.bfloat16).astype(f32)
            edges = jnp.concatenate([edge_high, edge - edge_high, edge_high, jnp.zeros((LANES - 24, 256), f32)], axis=0).T
            turned_high, turned_low = split(turned)
            cube = turned.reshape(16, 16, CZ)
            low_x, low_y = (1 - half) * RIM, (1 - side) * RIM
            potential[pl.ds(half * 12, 12), pl.ds(side * 12, 12), :] = cube[low_x:low_x + 12, low_y:low_y + 12, :]
            place = (pl.ds(half * 16, 16), pl.ds(side * 16, 16))
            for i, block in enumerate((turned_high, turned_low, turned_high, edges.astype(jnp.bfloat16))):
                field[place[0], place[1], pl.ds(i * LANES, LANES)] = block.reshape(16, 16, LANES)

    iota32 = lax.broadcasted_iota(jnp.int32, (SPAN, LANES), 0)
    iota_z = lax.broadcasted_iota(jnp.int32, (CZ, LANES), 0)
    iota8 = lax.broadcasted_iota(jnp.int32, (8, LANES), 0)
    edge_z = jnp.where(iota8 < 4, iota8 - 4, iota8 + (CZ - 4))

    def force(b):
        x = atoms[0, pl.ds(b, 1), :] * scales[0]
        y = atoms[0, pl.ds(b + BLOCKS, 1), :] * scales[1]
        z = atoms[0, pl.ds(b + 2 * BLOCKS, 1), :] * scales[2]
        q = atoms[0, pl.ds(b + 3 * BLOCKS, 1), :]
        at_x = meta[0, b]
        at_y = meta[0, BLOCKS + b]
        at_z = meta[0, 2 * BLOCKS + b]
        wx, sx = window(x, iota16, widths[0])
        wy, sy = window(y, iota32 - at_y, widths[1])
        wz, sz = window(z, iota_z - at_z + RIM, widths[2])
        we, se = window(z, edge_z - at_z + RIM, widths[2])
        main_high, main_low = split(jnp.concatenate([wz, sz], axis=1))
        rim = jnp.concatenate([we, se], axis=1)
        rim_high = rim.astype(jnp.bfloat16).astype(f32)
        rim = jnp.concatenate([rim_high, rim_high, rim - rim_high, jnp.zeros((LANES - 24, 256), f32)], axis=0).astype(jnp.bfloat16)
        right = jnp.concatenate([main_high, main_high, main_low, rim], axis=0)
        left = field[pl.ds(at_x, PATCH)].reshape(PATCH * SPAN, 4 * LANES)
        values = jnp.dot(left, right, preferred_element_type=f32).reshape(PATCH, SPAN, 256)
        by_sx = jnp.zeros((SPAN, LANES), f32)
        by_wx = jnp.zeros((SPAN, LANES), f32)
        by_wz = jnp.zeros((SPAN, LANES), f32)
        for i in range(PATCH):
            level = values[i, :, :LANES]
            by_sx = by_sx + level * sx[i:i + 1]
            by_wx = by_wx + level * wx[i:i + 1]
            by_wz = by_wz + values[i, :, LANES:] * wx[i:i + 1]
        for a, total in enumerate((by_sx * wy, by_wx * sy, by_wz * wy)):
            forces[a:a + 1, b * LANES:(b + 1) * LANES] = -q * scales[a] * jnp.sum(total, axis=0, keepdims=True)

    for b in range(BLOCKS):
        force(b)


def make_field(atoms, meta):
    anywhere = pl.BlockSpec(memory_space=pl.ANY)
    vmem = pl.BlockSpec(memory_space=pltpu.VMEM)
    f32, i32 = jnp.float32, jnp.int32
    return pl.pallas_call(
        field_kernel,
        out_shape=(jax.ShapeDtypeStruct((CX, CY, CZ), f32), jax.ShapeDtypeStruct((3, BLOCKS * LANES), f32)),
        in_specs=[anywhere, anywhere],
        out_specs=(vmem, vmem),
        scratch_shapes=[
            pltpu.SMEM((32, LANES), i32),
            pltpu.VMEM((SOURCES + 1, ROWS, LANES), f32),
            pltpu.SemaphoreType.DMA((2,)),
            pltpu.SMEM((EMPTY + 1,), i32),
            pltpu.SMEM((SLOTS * 4 + WAYS,), i32),
            pltpu.SMEM((EMPTY + 1,), i32),
            pltpu.VMEM((WAYS, 96, LANES), f32),
            pltpu.VMEM((WAYS, 96, LANES), f32),
            pltpu.VMEM((WAYS, 32, LANES), f32),
            pltpu.VMEM(((EMPTY + 1) * SPAN, LANES), f32),
            pltpu.VMEM(((EMPTY + 1) * SPAN, LANES), f32),
            pltpu.VMEM(((EMPTY + 1) * 24, LANES), f32),
            pltpu.VMEM((4 * Z_ROWS, 256), f32),
            pltpu.VMEM((SPAN, SPAN, 4 * LANES), jnp.bfloat16),
        ],
        compiler_params=pltpu.CompilerParams(vmem_limit_bytes=40 * 1024 * 1024),
        name="field_and_forces",
    )(meta, atoms)


def exchange_kernel(pos_in, q_in, anchor_in, atoms_in, blocks_in, scale_in, atoms_out, meta_out, pos_ref, q_ref, anchor_ref, atoms_ref, blocks_ref, scale_ref, rows_ref, load_sems, send_sems, recv_sems, ready_sems):
    gx, gy, gz = (lax.axis_index(a) for a in ("gx", "gy", "gz"))
    nx, ny, nz = (lax.axis_size(a) for a in ("gx", "gy", "gz"))
    half = ny // 2

    def device(dx, dy, dz):
        return (lax.rem(gx + dx + nx, nx), lax.rem(gy + dy + ny, ny), lax.rem(gz + dz + nz, nz))

    def both(condition, other):
        return condition & jnp.logical_not(other)

    late = gy >= half
    far = {1: lax.rem(gy, half) == half - 1, -1: lax.rem(gy, half) == 0}
    wrap = {1: gz == nz - 1, -1: gz == 0}
    far_any = far[1] | far[-1]
    sided_y = gz < ONE_SIDED
    sided_z = jnp.logical_not(late & jnp.logical_not(far_any))
    hold = wrap[-1] & sided_z
    ends = wrap[1] | wrap[-1]
    direct = both(far_any, ends)
    corner = far_any & (wrap[1] | wrap[-1])
    pushes = corner & late & wrap[-1]
    pushed = both(corner & wrap[-1], late)
    hands = both(corner, wrap[1] & jnp.logical_not(late))
    far_step = jnp.where(far[1], 1, -1)
    wrap_step = jnp.where(wrap[1], 1, -1)
    steps = (1, -1)
    code = {1: 1, -1: 2}
    across = (0, 1, -1)
    ready_z, ready_y, ready_c = (ready_sems.at[i] for i in range(3))

    def when(condition, action):
        pl.when(condition)(action)

    def signal(semaphore, *offsets):
        pl.semaphore_signal(semaphore, inc=1, device_id=device(*offsets), device_id_type=MESH)

    barrier = pltpu.get_barrier_semaphore()

    def greet_far():
        signal(barrier, 0, far_step, 0)

    def greet_corner():
        for dx in across:
            signal(barrier, dx, far_step, wrap_step)

    def greet_z(step):
        signal(barrier, 0, 0, step)
        for dx in steps:
            when(jnp.logical_not(wrap[step]), lambda: signal(barrier, dx, 0, step))

    when(both(direct, late & sided_y) | pushed, greet_far)
    when(both(corner, late), greet_corner)
    for step in steps:
        signal(barrier, step, 0, 0)
        when(jnp.logical_not(far[step]), lambda: signal(barrier, 0, step, 0))
    greet_z(-1)
    when(jnp.logical_not(wrap[1] & sided_z), lambda: greet_z(1))
    loads = []
    for i, (src, dst) in enumerate(((pos_in, pos_ref), (q_in, q_ref), (anchor_in, anchor_ref), (atoms_in, atoms_ref), (blocks_in, blocks_ref), (scale_in, scale_ref))):
        loads.append(pltpu.make_async_copy(src, dst, load_sems.at[i]))
        loads[-1].start()
    for load in loads:
        load.wait()
    for a in range(3):
        for b in range(BLOCKS):
            atoms_out[0, pl.ds(a * BLOCKS + b, 1), :] = pos_ref[pl.ds(a, 1), pl.ds(b * LANES, LANES)]
    row = lax.broadcasted_iota(jnp.int32, (BLOCKS, LANES), 0)
    lane = lax.broadcasted_iota(jnp.int32, (BLOCKS, LANES), 1)
    filled = jnp.zeros((BLOCKS, LANES), jnp.int32)
    for b in range(BLOCKS):
        filled = jnp.where(row == b, jnp.where(b < blocks_ref[0], atoms_ref[b], 0), filled)
    atoms_out[0, pl.ds(3 * BLOCKS, BLOCKS), :] = jnp.where(lane < filled, q_ref[...], 0.0)
    meta = jnp.zeros((BLOCKS, LANES), jnp.int32)
    for a in range(3):
        for b in range(BLOCKS):
            meta = jnp.where(lane == a * BLOCKS + b, anchor_ref[a, b], meta)
    for b in range(BLOCKS):
        meta = jnp.where(lane == 3 * BLOCKS + b, jnp.where(b < blocks_ref[0], 1, 0), meta)
    atoms_out[0, pl.ds(32, 1), :] = meta[:1].astype(jnp.float32)
    peers = 10 - jnp.where(hold, 3, jnp.where(ends, 2, 0)) - jnp.where(both(corner, pushes) | both(direct & sided_y, late), 1, 0) + jnp.where(corner & late, 3, 0)
    pl.semaphore_wait(barrier, peers)

    def answer_corner():
        for dx in across:
            signal(ready_c, dx, far_step, wrap_step)

    when(direct & late & sided_y, lambda: signal(ready_y, 0, far_step, 0))
    when(wrap[1] & sided_z, lambda: signal(ready_z, 0, 0, 1))
    when(corner & late, answer_corner)

    def slot(cx, cz, cy):
        return (cx * 3 + cz) * 3 + cy

    def piece(src, dst, target, index):
        return pltpu.make_async_remote_copy(
            src_ref=atoms_out.at[src], dst_ref=atoms_out.at[dst],
            send_sem=send_sems.at[index], recv_sem=recv_sems.at[dst],
            device_id=target, device_id_type=MESH)

    def along_y(step):
        dst = slot(0, 0, code[step])
        return [piece(0, dst, device(0, step, 0), dst)]

    def along_x(cy):
        return [piece(cy, slot(code[dx], 0, cy), device(dx, 0, 0), slot(code[dx], 0, cy)) for dx in steps]

    def fan(cy, step):
        places = [(dx, slot(code[dx] if dx else 0, code[step], cy)) for dx in across]
        return [piece(cy, dst, device(dx, 0, step), dst) for dx, dst in places]

    def corners():
        out = []
        for i, dx in enumerate(across):
            dst = slot(code[dx] if dx else 0, jnp.where(wrap[1], 1, 2), jnp.where(far[1], 1, 2))
            out.append(piece(0, dst, device(dx, far_step, wrap_step), 27 + i))
        return out

    def start(copies):
        for copy in copies:
            copy.start()

    def finish(copies):
        for copy in copies:
            copy.wait_send()

    from_far = {1: far[-1], 2: far[1]}

    def send_early(cy):
        start(along_x(cy))
        start(fan(cy, 1)[:1])
        when(jnp.logical_not(hold), lambda: start(fan(cy, -1)[:1]))
        for step in steps:
            when(jnp.logical_not(wrap[step]), lambda: start(fan(cy, step)[1:]))

    def pass_near(cy):
        along_y(1 if cy == 1 else -1)[0].wait_recv()
        send_early(cy)

    def pass_far(cy):
        along_y(1 if cy == 1 else -1)[0].wait_recv()
        start(along_x(cy))
        for step in steps:
            when(jnp.logical_not(wrap[step]), lambda: start(fan(cy, step)))

    def open_wrap():
        pl.semaphore_wait(ready_z, 1)
        start(fan(0, -1)[:1])
        for cy in (1, 2):
            when(jnp.logical_not(from_far[cy]), lambda: start(fan(cy, -1)[:1]))

    def onward(cy, step):
        src = slot(0, code[step], cy)
        return [piece(src, slot(code[dx], code[step], cy), device(dx, 0, 0), 31 + cy * 2 + i) for i, dx in enumerate(steps)]

    def pass_wrap(cy, step):
        fan(cy, step)[0].wait_recv()
        start(onward(cy, step))

    def open_corner():
        pl.semaphore_wait(ready_c, 3)
        start(corners())

    def handed():
        corner_slot = slot(0, jnp.where(wrap[1], 2, 1), jnp.where(far[1], 2, 1))
        own_slot = slot(0, 0, jnp.where(far[1], 2, 1))
        return piece(corner_slot, own_slot, device(0, 0, wrap_step), 30)

    def forward_corner():
        corner_slot = slot(0, jnp.where(wrap[1], 2, 1), jnp.where(far[1], 2, 1))
        piece(corner_slot, corner_slot, device(0, 0, wrap_step), 30).wait_recv()
        when(hands, handed().start)

    def open_far():
        pl.semaphore_wait(ready_y, 1)
        for step in steps:
            when(far[step], lambda: start(along_y(step)))

    for step in steps:
        when(jnp.logical_not(far[step] & (ends | both(sided_y, late))) | (far[step] & pushes), lambda: start(along_y(step)))
    when(corner & late, lambda: start(corners()))
    send_early(0)
    for cy in (1, 2):
        when(jnp.logical_not(from_far[cy]), lambda: pass_near(cy))
    when(hold, open_wrap)
    when(both(corner, late), open_corner)
    when(corner, forward_corner)
    for step in steps:
        when(wrap[-step], lambda: pass_wrap(0, step))
        for cy in (1, 2):
            when(both(wrap[-step], from_far[cy]), lambda: pass_wrap(cy, step))
    when(both(direct & sided_y, late), open_far)
    for cy in (1, 2):
        when(from_far[cy], lambda: pass_far(cy))
    for cy in range(3):
        for copy in along_x(cy):
            copy.wait_recv()
        for step in steps:
            copies = fan(cy, step)
            when(jnp.logical_not(wrap[-step]), copies[0].wait_recv)
            for copy in copies[1:]:
                copy.wait_recv()
    for step in steps:
        when(jnp.logical_not(far[step] & ends) | (far[step] & pushes), lambda: finish(along_y(step)))
    for cy in range(3):
        finish(along_x(cy))
        for step in steps:
            when(jnp.logical_not(wrap[step]), lambda: finish(fan(cy, step)[1:]))
            if cy == 0:
                finish(fan(cy, step)[:1])
                when(wrap[-step], lambda: finish(onward(cy, step)))
            else:
                when(jnp.logical_not(from_far[cy] & wrap[step]), lambda: finish(fan(cy, step)[:1]))
                when(both(wrap[-step], from_far[cy]), lambda: finish(onward(cy, step)))
    when(corner, lambda: finish(corners()))
    when(hands, lambda: finish([handed()]))
    for a in range(3):
        atoms_out[SOURCES, pl.ds(a, 1), :] = jnp.full((1, LANES), scale_ref[a], jnp.float32)
    rows_ref[...] = jnp.zeros_like(rows_ref)
    for n in range(SOURCES):
        rows_ref[pl.ds(n, 1), :] = atoms_out[n, pl.ds(32, 1), :]
    value = rows_ref[...].astype(jnp.int32)
    source = lax.broadcasted_iota(jnp.int32, value.shape, 0)
    place = lax.broadcasted_iota(jnp.int32, value.shape, 1)
    one = jnp.ones_like(value)
    zero = jnp.zeros_like(value)
    cx = jnp.where(source >= 9, one, zero) + jnp.where(source >= 18, one, zero)
    rest = source - 9 * cx
    cz = jnp.where(rest >= 3, one, zero) + jnp.where(rest >= 6, one, zero)
    cy = rest - 3 * cz
    is_z = (place >= 2 * BLOCKS) & (place < 3 * BLOCKS)
    is_live = place >= 3 * BLOCKS
    kind = jnp.where(place < BLOCKS, cx, jnp.where(place < 2 * BLOCKS, cy, cz))
    period = jnp.where(is_z, CZ, CX)
    low = jnp.where(is_live, 1, jnp.where(kind == 1, jnp.where(is_z, CZ - 19, 5), 0))
    high = jnp.where(jnp.logical_not(is_live) & (kind == 2), 11, 999)
    fits = jnp.where((value >= low) & (value <= high), one, zero)
    used = fits
    for group in (1, 2, 3):
        used = used * pltpu.roll(fits, LANES - group * BLOCKS, 1)
    used = pltpu.roll(used, 4 * BLOCKS, 1)
    shifted = value + jnp.where(is_live | (kind == 0), 0, jnp.where(kind == 1, -period, period))
    meta_out[...] = jnp.where(place >= 4 * BLOCKS, used, shifted)


def exchange(positions, charges, block_anchor, block_atoms, brick_blocks, box_scale):
    anywhere = pl.BlockSpec(memory_space=pl.ANY)
    vmem = pl.BlockSpec(memory_space=pltpu.VMEM)
    f32, i32 = jnp.float32, jnp.int32
    return pl.pallas_call(
        exchange_kernel,
        out_shape=(jax.ShapeDtypeStruct((SOURCES + 1, ROWS, LANES), f32), jax.ShapeDtypeStruct((32, LANES), i32)),
        in_specs=[anywhere] * 6,
        out_specs=(vmem, vmem),
        scratch_shapes=[
            pltpu.VMEM((3, BLOCKS * LANES), f32),
            pltpu.VMEM((BLOCKS, LANES), f32),
            pltpu.SMEM((3, BLOCKS), i32),
            pltpu.SMEM((BLOCKS,), i32),
            pltpu.SMEM((1,), i32),
            pltpu.SMEM((3,), f32),
            pltpu.VMEM((32, LANES), f32),
            pltpu.SemaphoreType.DMA((6,)),
            pltpu.SemaphoreType.DMA((40,)),
            pltpu.SemaphoreType.DMA((SOURCES,)),
            pltpu.SemaphoreType.REGULAR((3,)),
        ],
        compiler_params=pltpu.CompilerParams(collective_id=0, has_side_effects=True),
        name="exchange_atoms",
    )(positions, charges.reshape(BLOCKS, LANES), block_anchor, block_atoms, brick_blocks, box_scale)


def per_device(positions, charges, block_anchor, block_atoms, brick_blocks, box_scale):
    atoms, meta = exchange(positions, charges, block_anchor, block_atoms, brick_blocks, box_scale)
    potential, forces = make_field(atoms, meta)
    return (potential, forces)


def solution(mesh):
    split_all = ("gx", "gy", "gz")
    return jax.shard_map(
        per_device,
        mesh=mesh,
        in_specs=(P(None, split_all), P(split_all), P(None, split_all), P(split_all), P(split_all), P()),
        out_specs=(P("gx", "gy", "gz"), P(None, split_all)),
        check_vma=False,
    )
```

```python
import math
import jax, jax.numpy as jnp
from jax import lax
from jax.experimental import pallas as pl
from jax.experimental.pallas import tpu as pltpu

from jax.sharding import PartitionSpec as P

MESH = pl.DeviceIdType.MESH
CX = 24
CY = 24
CZ = 128
PATCH = 16
RIM = 4
RADIUS = 4
SPREAD = 1.0
SMOOTH = 1.5
COUPLING = 200.0
ROWS = 33
ONE_SIDED = 3
BLOCKS = 8
LANES = 128
SOURCES = 27
SLOTS = SOURCES * BLOCKS
SPAN = 32
Z_ROWS = 176
WAYS = 16
EMPTY = SLOTS + WAYS
PAD = 40


def norm(width):
    return 1.0 / (math.sqrt(2.0 * math.pi) * width)


def window(coord, place, width):
    offset = coord + RIM - place.astype(jnp.float32)
    inside = (place >= 0) & (place < PATCH)
    weight = jnp.exp(-offset * offset / (2.0 * width * width)) * norm(width)
    weight = jnp.where(inside, weight, 0.0)
    return weight, -offset / (width * width) * weight


def split(value):
    high = value.astype(jnp.bfloat16)
    return high, (value - high.astype(jnp.float32)).astype(jnp.bfloat16)


def field_kernel(meta_in, atoms_in, potential, forces, meta, atoms, load_sems, order, tasks, starts, pad_x, pad_y, pad_z, wx_all, wy_all, wz_all, density, field):
    f32 = jnp.float32
    load_meta = pltpu.make_async_copy(meta_in, meta, load_sems.at[0])
    load_meta.start()
    load_atoms = pltpu.make_async_copy(atoms_in, atoms, load_sems.at[1])
    load_atoms.start()
    density[...] = jnp.zeros_like(density)
    for ref in (pad_x, pad_y, pad_z):
        ref[...] = jnp.zeros_like(ref)
    wx_all[pl.ds(EMPTY * SPAN, SPAN), :] = jnp.zeros((SPAN, LANES), f32)
    wy_all[pl.ds(EMPTY * SPAN, SPAN), :] = jnp.zeros((SPAN, LANES), f32)
    wz_all[pl.ds(EMPTY * 24, 24), :] = jnp.zeros((24, LANES), f32)
    starts[EMPTY] = 0
    load_meta.wait()

    def choose(n, count):
        for b in range(BLOCKS):
            order[count] = n * BLOCKS + b
            count = count + meta[n, 4 * BLOCKS + b]
        return count

    blocks = lax.fori_loop(0, SOURCES, choose, jnp.int32(0))
    for extra in range(WAYS - 1):
        order[blocks + extra] = 0
    load_atoms.wait()
    scales = [atoms[SOURCES, pl.ds(a, 1), :] for a in range(3)]
    widths = [SPREAD * s for s in scales]
    taps = []
    for a in range(3):
        tau = SMOOTH * scales[a]
        taps.append([jnp.exp(-float(e * e) / (2.0 * tau * tau)) * norm(tau) for e in range(RADIUS + 1)])

    iota16 = lax.broadcasted_iota(jnp.int32, (PATCH, LANES), 0)

    def weigh(group, count):
        for way in range(WAYS):
            k = group * WAYS + way
            code = order[k]
            n = code // BLOCKS
            b = code % BLOCKS
            cx = n // 9
            cy = n % 3
            off_x = meta[n, b]
            off_y = meta[n, BLOCKS + b]
            off_z = meta[n, 2 * BLOCKS + b]
            x = atoms[n, pl.ds(b, 1), :] * scales[0]
            y = atoms[n, pl.ds(b + BLOCKS, 1), :] * scales[1]
            z = atoms[n, pl.ds(b + 2 * BLOCKS, 1), :] * scales[2]
            q = atoms[n, pl.ds(b + 3 * BLOCKS, 1), :]
            pad_x[way, pl.ds(PAD, PATCH), :] = q * window(x, iota16, widths[0])[0]
            pad_y[way, pl.ds(PAD, PATCH), :] = window(y, iota16, widths[1])[0]
            pad_z[way, pl.ds(8, PATCH), :] = window(z, iota16, widths[2])[0]
            for a, off, pad, out in ((0, off_x, pad_x, wx_all), (1, off_y, pad_y, wy_all)):
                start = PAD - off
                total = taps[a][0] * pad[way, pl.ds(start, SPAN), :]
                for e in range(1, RADIUS + 1):
                    total = total + taps[a][e] * (pad[way, pl.ds(start - e, SPAN), :] + pad[way, pl.ds(start + e, SPAN), :])
                out[pl.ds(pl.multiple_of(k * SPAN, SPAN), SPAN), :] = total
            first = off_z + 20
            shift = first & 7
            wz_all[pl.ds(pl.multiple_of(k * 24, 8), 24), :] = pad_z[way, pl.ds(8 - shift, 24), :]
            starts[k] = first - shift
            used = k < blocks
            for half in range(2):
                for side in range(2):
                    touches = used & ((cx == 0) | (cx == half + 1)) & ((cy == 0) | (cy == side + 1))
                    tasks[count] = k * 4 + half * 2 + side
                    count = count + touches.astype(jnp.int32)
        return count

    jobs = lax.fori_loop(0, (blocks + WAYS - 1) // WAYS, weigh, jnp.int32(0))
    for extra in range(WAYS - 1):
        tasks[jobs + extra] = EMPTY * 4

    def spread(group, carry):
        for way in range(WAYS):
            code = tasks[group * WAYS + way]
            k = code // 4
            half = code // 2 % 2
            side = code % 2
            wx = wx_all[pl.ds(pl.multiple_of(k * SPAN + half * 16, 16), 16), :]
            wy = wy_all[pl.ds(pl.multiple_of(k * SPAN + side * 16, 16), 16), :]
            product = (wx[:, None, :] * wy[None, :, :]).reshape(256, LANES)
            high, low = split(product)
            wz = wz_all[pl.ds(pl.multiple_of(k * 24, 8), 24), :]
            z_high = wz.astype(jnp.bfloat16).astype(f32)
            left = jnp.concatenate([z_high, wz - z_high], axis=0).astype(jnp.bfloat16)
            patch = lax.dot_general(
                jnp.concatenate([left, left], axis=1), jnp.concatenate([high, low], axis=1),
                (((1,), (1,)), ((), ())), preferred_element_type=f32)
            rows = pl.ds(pl.multiple_of((code % 4) * Z_ROWS + starts[k], 8), 24)
            density[rows, :] = density[rows, :] + patch[:24] + patch[24:]
        return carry

    lax.fori_loop(0, (jobs + WAYS - 1) // WAYS, spread, jnp.int32(0))

    length = CZ + 2 * (RIM + RADIUS)
    gap = lax.broadcasted_iota(jnp.int32, (length, length), 0) - lax.broadcasted_iota(jnp.int32, (length, length), 1)
    gap_f = gap.astype(f32)
    tau_v = jnp.broadcast_to(SMOOTH * scales[2][:, :1], (length, length))
    band = jnp.exp(-gap_f * gap_f / (2.0 * tau_v * tau_v)) * (COUPLING / (math.sqrt(2.0 * math.pi) * tau_v))
    band_high, band_low = split(jnp.where(jnp.abs(gap) <= RADIUS, band, 0.0))
    for half in range(2):
        for side in range(2):
            part = density[pl.ds((half * 2 + side) * Z_ROWS + 16, length), :]
            high, low = split(part)
            smooth = (jnp.dot(band_high, high, preferred_element_type=f32)
                      + jnp.dot(band_high, low, preferred_element_type=f32)
                      + jnp.dot(band_low, high, preferred_element_type=f32))
            turned = smooth[8:8 + CZ].T
            edge = jnp.concatenate([smooth[4:8], smooth[8 + CZ:12 + CZ]], axis=0)
            edge_high = edge.astype(jnp.bfloat16).astype(f32)
            edges = jnp.concatenate([edge_high, edge - edge_high, edge_high, jnp.zeros((LANES - 24, 256), f32)], axis=0).T
            turned_high, turned_low = split(turned)
            cube = turned.reshape(16, 16, CZ)
            low_x, low_y = (1 - half) * RIM, (1 - side) * RIM
            potential[pl.ds(half * 12, 12), pl.ds(side * 12, 12), :] = cube[low_x:low_x + 12, low_y:low_y + 12, :]
            place = (pl.ds(half * 16, 16), pl.ds(side * 16, 16))
            for i, block in enumerate((turned_high, turned_low, turned_high, edges.astype(jnp.bfloat16))):
                field[place[0], place[1], pl.ds(i * LANES, LANES)] = block.reshape(16, 16, LANES)

    iota32 = lax.broadcasted_iota(jnp.int32, (SPAN, LANES), 0)
    iota_z = lax.broadcasted_iota(jnp.int32, (CZ, LANES), 0)
    iota8 = lax.broadcasted_iota(jnp.int32, (8, LANES), 0)
    edge_z = jnp.where(iota8 < 4, iota8 - 4, iota8 + (CZ - 4))

    def force(b):
        x = atoms[0, pl.ds(b, 1), :] * scales[0]
        y = atoms[0, pl.ds(b + BLOCKS, 1), :] * scales[1]
        z = atoms[0, pl.ds(b + 2 * BLOCKS, 1), :] * scales[2]
        q = atoms[0, pl.ds(b + 3 * BLOCKS, 1), :]
        at_x = meta[0, b]
        at_y = meta[0, BLOCKS + b]
        at_z = meta[0, 2 * BLOCKS + b]
        wx, sx = window(x, iota16, widths[0])
        wy, sy = window(y, iota32 - at_y, widths[1])
        wz, sz = window(z, iota_z - at_z + RIM, widths[2])
        we, se = window(z, edge_z - at_z + RIM, widths[2])
        main_high, main_low = split(jnp.concatenate([wz, sz], axis=1))
        rim = jnp.concatenate([we, se], axis=1)
        rim_high = rim.astype(jnp.bfloat16).astype(f32)
        rim = jnp.concatenate([rim_high, rim_high, rim - rim_high, jnp.zeros((LANES - 24, 256), f32)], axis=0).astype(jnp.bfloat16)
        right = jnp.concatenate([main_high, main_high, main_low, rim], axis=0)
        left = field[pl.ds(at_x, PATCH)].reshape(PATCH * SPAN, 4 * LANES)
        values = jnp.dot(left, right, preferred_element_type=f32).reshape(PATCH, SPAN, 256)
        by_sx = jnp.zeros((SPAN, LANES), f32)
        by_wx = jnp.zeros((SPAN, LANES), f32)
        by_wz = jnp.zeros((SPAN, LANES), f32)
        for i in range(PATCH):
            level = values[i, :, :LANES]
            by_sx = by_sx + level * sx[i:i + 1]
            by_wx = by_wx + level * wx[i:i + 1]
            by_wz = by_wz + values[i, :, LANES:] * wx[i:i + 1]
        for a, total in enumerate((by_sx * wy, by_wx * sy, by_wz * wy)):
            forces[a:a + 1, b * LANES:(b + 1) * LANES] = -q * scales[a] * jnp.sum(total, axis=0, keepdims=True)

    for b in range(BLOCKS):
        force(b)


def make_field(atoms, meta):
    anywhere = pl.BlockSpec(memory_space=pl.ANY)
    vmem = pl.BlockSpec(memory_space=pltpu.VMEM)
    f32, i32 = jnp.float32, jnp.int32
    return pl.pallas_call(
        field_kernel,
        out_shape=(jax.ShapeDtypeStruct((CX, CY, CZ), f32), jax.ShapeDtypeStruct((3, BLOCKS * LANES), f32)),
        in_specs=[anywhere, anywhere],
        out_specs=(vmem, vmem),
        scratch_shapes=[
            pltpu.SMEM((32, LANES), i32),
            pltpu.VMEM((SOURCES + 1, ROWS, LANES), f32),
            pltpu.SemaphoreType.DMA((2,)),
            pltpu.SMEM((EMPTY + 1,), i32),
            pltpu.SMEM((SLOTS * 4 + WAYS,), i32),
            pltpu.SMEM((EMPTY + 1,), i32),
            pltpu.VMEM((WAYS, 96, LANES), f32),
            pltpu.VMEM((WAYS, 96, LANES), f32),
            pltpu.VMEM((WAYS, 32, LANES), f32),
            pltpu.VMEM(((EMPTY + 1) * SPAN, LANES), f32),
            pltpu.VMEM(((EMPTY + 1) * SPAN, LANES), f32),
            pltpu.VMEM(((EMPTY + 1) * 24, LANES), f32),
            pltpu.VMEM((4 * Z_ROWS, 256), f32),
            pltpu.VMEM((SPAN, SPAN, 4 * LANES), jnp.bfloat16),
        ],
        compiler_params=pltpu.CompilerParams(vmem_limit_bytes=60 * 1024 * 1024),
        name="field_and_forces",
    )(meta, atoms)


def exchange_kernel(pos_in, q_in, anchor_in, atoms_in, blocks_in, scale_in, atoms_out, meta_out, pos_ref, q_ref, anchor_ref, atoms_ref, blocks_ref, scale_ref, rows_ref, load_sems, send_sems, recv_sems, ready_sems):
    gx, gy, gz = (lax.axis_index(a) for a in ("gx", "gy", "gz"))
    nx, ny, nz = (lax.axis_size(a) for a in ("gx", "gy", "gz"))
    half = ny // 2

    def device(dx, dy, dz):
        return (lax.rem(gx + dx + nx, nx), lax.rem(gy + dy + ny, ny), lax.rem(gz + dz + nz, nz))

    def both(condition, other):
        return condition & jnp.logical_not(other)

    late = gy >= half
    far = {1: lax.rem(gy, half) == half - 1, -1: lax.rem(gy, half) == 0}
    wrap = {1: gz == nz - 1, -1: gz == 0}
    far_any = far[1] | far[-1]
    sided_y = gz < ONE_SIDED
    sided_z = jnp.logical_not(late & jnp.logical_not(far_any))
    hold = wrap[-1] & sided_z
    ends = wrap[1] | wrap[-1]
    direct = both(far_any, ends)
    corner = far_any & (wrap[1] | wrap[-1])
    pushes = corner & late & wrap[-1]
    pushed = both(corner & wrap[-1], late)
    hands = both(corner, wrap[1] & jnp.logical_not(late))
    far_step = jnp.where(far[1], 1, -1)
    wrap_step = jnp.where(wrap[1], 1, -1)
    steps = (1, -1)
    code = {1: 1, -1: 2}
    across = (0, 1, -1)
    ready_z, ready_y, ready_c = (ready_sems.at[i] for i in range(3))

    def when(condition, action):
        pl.when(condition)(action)

    def signal(semaphore, *offsets):
        pl.semaphore_signal(semaphore, inc=1, device_id=device(*offsets), device_id_type=MESH)

    barrier = pltpu.get_barrier_semaphore()

    def greet_far():
        signal(barrier, 0, far_step, 0)

    def greet_corner():
        for dx in across:
            signal(barrier, dx, far_step, wrap_step)

    def greet_z(step):
        signal(barrier, 0, 0, step)
        for dx in steps:
            when(jnp.logical_not(wrap[step]), lambda: signal(barrier, dx, 0, step))

    when(both(direct, late & sided_y) | pushed, greet_far)
    when(both(corner, late), greet_corner)
    for step in steps:
        signal(barrier, step, 0, 0)
        when(jnp.logical_not(far[step]), lambda: signal(barrier, 0, step, 0))
    greet_z(-1)
    when(jnp.logical_not(wrap[1] & sided_z), lambda: greet_z(1))
    loads = []
    for i, (src, dst) in enumerate(((pos_in, pos_ref), (q_in, q_ref), (anchor_in, anchor_ref), (atoms_in, atoms_ref), (blocks_in, blocks_ref), (scale_in, scale_ref))):
        loads.append(pltpu.make_async_copy(src, dst, load_sems.at[i]))
        loads[-1].start()
    for load in loads:
        load.wait()
    for a in range(3):
        for b in range(BLOCKS):
            atoms_out[0, pl.ds(a * BLOCKS + b, 1), :] = pos_ref[pl.ds(a, 1), pl.ds(b * LANES, LANES)]
    row = lax.broadcasted_iota(jnp.int32, (BLOCKS, LANES), 0)
    lane = lax.broadcasted_iota(jnp.int32, (BLOCKS, LANES), 1)
    filled = jnp.zeros((BLOCKS, LANES), jnp.int32)
    for b in range(BLOCKS):
        filled = jnp.where(row == b, jnp.where(b < blocks_ref[0], atoms_ref[b], 0), filled)
    atoms_out[0, pl.ds(3 * BLOCKS, BLOCKS), :] = jnp.where(lane < filled, q_ref[...], 0.0)
    meta = jnp.zeros((BLOCKS, LANES), jnp.int32)
    for a in range(3):
        for b in range(BLOCKS):
            meta = jnp.where(lane == a * BLOCKS + b, anchor_ref[a, b], meta)
    for b in range(BLOCKS):
        meta = jnp.where(lane == 3 * BLOCKS + b, jnp.where(b < blocks_ref[0], 1, 0), meta)
    atoms_out[0, pl.ds(32, 1), :] = meta[:1].astype(jnp.float32)
    peers = 10 - jnp.where(hold, 3, jnp.where(ends, 2, 0)) - jnp.where(both(corner, pushes) | both(direct & sided_y, late), 1, 0) + jnp.where(corner & late, 3, 0)
    pl.semaphore_wait(barrier, peers)

    def answer_corner():
        for dx in across:
            signal(ready_c, dx, far_step, wrap_step)

    when(direct & late & sided_y, lambda: signal(ready_y, 0, far_step, 0))
    when(wrap[1] & sided_z, lambda: signal(ready_z, 0, 0, 1))
    when(corner & late, answer_corner)

    def slot(cx, cz, cy):
        return (cx * 3 + cz) * 3 + cy

    def piece(src, dst, target, index):
        return pltpu.make_async_remote_copy(
            src_ref=atoms_out.at[src], dst_ref=atoms_out.at[dst],
            send_sem=send_sems.at[index], recv_sem=recv_sems.at[dst],
            device_id=target, device_id_type=MESH)

    def along_y(step):
        dst = slot(0, 0, code[step])
        return [piece(0, dst, device(0, step, 0), dst)]

    def along_x(cy):
        return [piece(cy, slot(code[dx], 0, cy), device(dx, 0, 0), slot(code[dx], 0, cy)) for dx in steps]

    def fan(cy, step):
        places = [(dx, slot(code[dx] if dx else 0, code[step], cy)) for dx in across]
        return [piece(cy, dst, device(dx, 0, step), dst) for dx, dst in places]

    def corners():
        out = []
        for i, dx in enumerate(across):
            dst = slot(code[dx] if dx else 0, jnp.where(wrap[1], 1, 2), jnp.where(far[1], 1, 2))
            out.append(piece(0, dst, device(dx, far_step, wrap_step), 27 + i))
        return out

    def start(copies):
        for copy in copies:
            copy.start()

    def finish(copies):
        for copy in copies:
            copy.wait_send()

    from_far = {1: far[-1], 2: far[1]}

    def send_early(cy):
        start(along_x(cy))
        start(fan(cy, 1)[:1])
        when(jnp.logical_not(hold), lambda: start(fan(cy, -1)[:1]))
        for step in steps:
            when(jnp.logical_not(wrap[step]), lambda: start(fan(cy, step)[1:]))

    def pass_near(cy):
        along_y(1 if cy == 1 else -1)[0].wait_recv()
        send_early(cy)

    def pass_far(cy):
        along_y(1 if cy == 1 else -1)[0].wait_recv()
        start(along_x(cy))
        for step in steps:
            when(jnp.logical_not(wrap[step]), lambda: start(fan(cy, step)))

    def open_wrap():
        pl.semaphore_wait(ready_z, 1)
        start(fan(0, -1)[:1])
        for cy in (1, 2):
            when(jnp.logical_not(from_far[cy]), lambda: start(fan(cy, -1)[:1]))

    def onward(cy, step):
        src = slot(0, code[step], cy)
        return [piece(src, slot(code[dx], code[step], cy), device(dx, 0, 0), 31 + cy * 2 + i) for i, dx in enumerate(steps)]

    def pass_wrap(cy, step):
        fan(cy, step)[0].wait_recv()
        start(onward(cy, step))

    def open_corner():
        pl.semaphore_wait(ready_c, 3)
        start(corners())

    def handed():
        corner_slot = slot(0, jnp.where(wrap[1], 2, 1), jnp.where(far[1], 2, 1))
        own_slot = slot(0, 0, jnp.where(far[1], 2, 1))
        return piece(corner_slot, own_slot, device(0, 0, wrap_step), 30)

    def forward_corner():
        corner_slot = slot(0, jnp.where(wrap[1], 2, 1), jnp.where(far[1], 2, 1))
        piece(corner_slot, corner_slot, device(0, 0, wrap_step), 30).wait_recv()
        when(hands, handed().start)

    def open_far():
        pl.semaphore_wait(ready_y, 1)
        for step in steps:
            when(far[step], lambda: start(along_y(step)))

    for step in steps:
        when(jnp.logical_not(far[step] & (ends | both(sided_y, late))) | (far[step] & pushes), lambda: start(along_y(step)))
    when(corner & late, lambda: start(corners()))
    send_early(0)
    for cy in (1, 2):
        when(jnp.logical_not(from_far[cy]), lambda: pass_near(cy))
    when(hold, open_wrap)
    when(both(corner, late), open_corner)
    when(corner, forward_corner)
    for step in steps:
        when(wrap[-step], lambda: pass_wrap(0, step))
        for cy in (1, 2):
            when(both(wrap[-step], from_far[cy]), lambda: pass_wrap(cy, step))
    when(both(direct & sided_y, late), open_far)
    for cy in (1, 2):
        when(from_far[cy], lambda: pass_far(cy))
    for cy in range(3):
        for copy in along_x(cy):
            copy.wait_recv()
        for step in steps:
            copies = fan(cy, step)
            when(jnp.logical_not(wrap[-step]), copies[0].wait_recv)
            for copy in copies[1:]:
                copy.wait_recv()
    for step in steps:
        when(jnp.logical_not(far[step] & ends) | (far[step] & pushes), lambda: finish(along_y(step)))
    for cy in range(3):
        finish(along_x(cy))
        for step in steps:
            when(jnp.logical_not(wrap[step]), lambda: finish(fan(cy, step)[1:]))
            if cy == 0:
                finish(fan(cy, step)[:1])
                when(wrap[-step], lambda: finish(onward(cy, step)))
            else:
                when(jnp.logical_not(from_far[cy] & wrap[step]), lambda: finish(fan(cy, step)[:1]))
                when(both(wrap[-step], from_far[cy]), lambda: finish(onward(cy, step)))
    when(corner, lambda: finish(corners()))
    when(hands, lambda: finish([handed()]))
    for a in range(3):
        atoms_out[SOURCES, pl.ds(a, 1), :] = jnp.full((1, LANES), scale_ref[a], jnp.float32)
    rows_ref[...] = jnp.zeros_like(rows_ref)
    for n in range(SOURCES):
        rows_ref[pl.ds(n, 1), :] = atoms_out[n, pl.ds(32, 1), :]
    value = rows_ref[...].astype(jnp.int32)
    source = lax.broadcasted_iota(jnp.int32, value.shape, 0)
    place = lax.broadcasted_iota(jnp.int32, value.shape, 1)
    one = jnp.ones_like(value)
    zero = jnp.zeros_like(value)
    cx = jnp.where(source >= 9, one, zero) + jnp.where(source >= 18, one, zero)
    rest = source - 9 * cx
    cz = jnp.where(rest >= 3, one, zero) + jnp.where(rest >= 6, one, zero)
    cy = rest - 3 * cz
    is_z = (place >= 2 * BLOCKS) & (place < 3 * BLOCKS)
    is_live = place >= 3 * BLOCKS
    kind = jnp.where(place < BLOCKS, cx, jnp.where(place < 2 * BLOCKS, cy, cz))
    period = jnp.where(is_z, CZ, CX)
    low = jnp.where(is_live, 1, jnp.where(kind == 1, jnp.where(is_z, CZ - 19, 5), 0))
    high = jnp.where(jnp.logical_not(is_live) & (kind == 2), 11, 999)
    fits = jnp.where((value >= low) & (value <= high), one, zero)
    used = fits
    for group in (1, 2, 3):
        used = used * pltpu.roll(fits, LANES - group * BLOCKS, 1)
    used = pltpu.roll(used, 4 * BLOCKS, 1)
    shifted = value + jnp.where(is_live | (kind == 0), 0, jnp.where(kind == 1, -period, period))
    meta_out[...] = jnp.where(place >= 4 * BLOCKS, used, shifted)


def exchange(positions, charges, block_anchor, block_atoms, brick_blocks, box_scale):
    anywhere = pl.BlockSpec(memory_space=pl.ANY)
    vmem = pl.BlockSpec(memory_space=pltpu.VMEM)
    f32, i32 = jnp.float32, jnp.int32
    return pl.pallas_call(
        exchange_kernel,
        out_shape=(jax.ShapeDtypeStruct((SOURCES + 1, ROWS, LANES), f32), jax.ShapeDtypeStruct((32, LANES), i32)),
        in_specs=[anywhere] * 6,
        out_specs=(vmem, vmem),
        scratch_shapes=[
            pltpu.VMEM((3, BLOCKS * LANES), f32),
            pltpu.VMEM((BLOCKS, LANES), f32),
            pltpu.SMEM((3, BLOCKS), i32),
            pltpu.SMEM((BLOCKS,), i32),
            pltpu.SMEM((1,), i32),
            pltpu.SMEM((3,), f32),
            pltpu.VMEM((32, LANES), f32),
            pltpu.SemaphoreType.DMA((6,)),
            pltpu.SemaphoreType.DMA((40,)),
            pltpu.SemaphoreType.DMA((SOURCES,)),
            pltpu.SemaphoreType.REGULAR((3,)),
        ],
        compiler_params=pltpu.CompilerParams(collective_id=0, has_side_effects=True),
        name="exchange_atoms",
    )(positions, charges.reshape(BLOCKS, LANES), block_anchor, block_atoms, brick_blocks, box_scale)


def per_device(positions, charges, block_anchor, block_atoms, brick_blocks, box_scale):
    atoms, meta = exchange(positions, charges, block_anchor, block_atoms, brick_blocks, box_scale)
    potential, forces = make_field(atoms, meta)
    return (potential, forces)


def solution(mesh):
    split_all = ("gx", "gy", "gz")
    return jax.shard_map(
        per_device,
        mesh=mesh,
        in_specs=(P(None, split_all), P(split_all), P(None, split_all), P(split_all), P(split_all), P()),
        out_specs=(P("gx", "gy", "gz"), P(None, split_all)),
        check_vma=False,
    )
```

```python
import math
import jax, jax.numpy as jnp
from jax import lax
from jax.experimental import pallas as pl
from jax.experimental.pallas import tpu as pltpu

from jax.sharding import PartitionSpec as P

MESH = pl.DeviceIdType.MESH
CX = 24
CY = 24
CZ = 128
PATCH = 16
RIM = 4
RADIUS = 4
SPREAD = 1.0
SMOOTH = 1.5
COUPLING = 200.0
ROWS = 33
ONE_SIDED = 3
BLOCKS = 8
LANES = 128
SOURCES = 27
SLOTS = SOURCES * BLOCKS
SPAN = 32
Z_ROWS = 176
WAYS = 16
EMPTY = SLOTS + WAYS
PAD = 40
LENGTH = CZ + 2 * (RIM + RADIUS)


def norm(width):
    return 1.0 / (math.sqrt(2.0 * math.pi) * width)


def window(coord, place, width):
    offset = coord + RIM - place.astype(jnp.float32)
    inside = (place >= 0) & (place < PATCH)
    weight = jnp.exp(-offset * offset / (2.0 * width * width)) * norm(width)
    weight = jnp.where(inside, weight, 0.0)
    return weight, -offset / (width * width) * weight


def split(value):
    high = value.astype(jnp.bfloat16)
    return high, (value - high.astype(jnp.float32)).astype(jnp.bfloat16)


def kernel_taps(scales):
    taps = []
    for scale in scales:
        tau = SMOOTH * scale
        taps.append([jnp.exp(-float(e * e) / (2.0 * tau * tau)) * norm(tau) for e in range(RADIUS + 1)])
    return taps


def field_kernel(meta_in, atoms_in, own_in, potential, forces, meta, atoms, load_sems, order, tasks, starts, pad_x, pad_y, pad_z, wx_all, wy_all, wz_all, density, field):
    f32 = jnp.float32
    load_meta = pltpu.make_async_copy(meta_in, meta, load_sems.at[0])
    load_meta.start()
    load_atoms = pltpu.make_async_copy(atoms_in, atoms, load_sems.at[1])
    load_atoms.start()
    load_own = []
    for quarter in range(4):
        load_own.append(pltpu.make_async_copy(own_in.at[quarter], density.at[pl.ds(quarter * Z_ROWS + 16, LENGTH)], load_sems.at[2 + quarter]))
        load_own[-1].start()
    for quarter in range(4):
        for first in (0, 16 + LENGTH):
            density[pl.ds(quarter * Z_ROWS + first, 16), :] = jnp.zeros((16, 256), f32)
    for ref in (pad_x, pad_y, pad_z):
        ref[...] = jnp.zeros_like(ref)
    wx_all[pl.ds(EMPTY * SPAN, SPAN), :] = jnp.zeros((SPAN, LANES), f32)
    wy_all[pl.ds(EMPTY * SPAN, SPAN), :] = jnp.zeros((SPAN, LANES), f32)
    wz_all[pl.ds(EMPTY * 24, 24), :] = jnp.zeros((24, LANES), f32)
    starts[EMPTY] = 0
    load_meta.wait()

    def choose(n, count):
        for b in range(BLOCKS):
            order[count] = n * BLOCKS + b
            count = count + meta[n, 4 * BLOCKS + b]
        return count

    blocks = lax.fori_loop(1, SOURCES, choose, jnp.int32(0))
    for extra in range(WAYS - 1):
        order[blocks + extra] = 0
    load_atoms.wait()
    scales = [atoms[SOURCES, pl.ds(a, 1), :] for a in range(3)]
    widths = [SPREAD * s for s in scales]
    taps = kernel_taps(scales)

    iota16 = lax.broadcasted_iota(jnp.int32, (PATCH, LANES), 0)

    def weigh(group, count):
        for way in range(WAYS):
            k = group * WAYS + way
            code = order[k]
            n = code // BLOCKS
            b = code % BLOCKS
            cx = n // 9
            cy = n % 3
            off_x = meta[n, b]
            off_y = meta[n, BLOCKS + b]
            off_z = meta[n, 2 * BLOCKS + b]
            x = atoms[n, pl.ds(b, 1), :] * scales[0]
            y = atoms[n, pl.ds(b + BLOCKS, 1), :] * scales[1]
            z = atoms[n, pl.ds(b + 2 * BLOCKS, 1), :] * scales[2]
            q = atoms[n, pl.ds(b + 3 * BLOCKS, 1), :]
            pad_x[way, pl.ds(PAD, PATCH), :] = q * window(x, iota16, widths[0])[0]
            pad_y[way, pl.ds(PAD, PATCH), :] = window(y, iota16, widths[1])[0]
            pad_z[way, pl.ds(8, PATCH), :] = window(z, iota16, widths[2])[0]
            for a, off, pad, out in ((0, off_x, pad_x, wx_all), (1, off_y, pad_y, wy_all)):
                start = PAD - off
                total = taps[a][0] * pad[way, pl.ds(start, SPAN), :]
                for e in range(1, RADIUS + 1):
                    total = total + taps[a][e] * (pad[way, pl.ds(start - e, SPAN), :] + pad[way, pl.ds(start + e, SPAN), :])
                out[pl.ds(pl.multiple_of(k * SPAN, SPAN), SPAN), :] = total
            first = off_z + 20
            shift = first & 7
            wz_all[pl.ds(pl.multiple_of(k * 24, 8), 24), :] = pad_z[way, pl.ds(8 - shift, 24), :]
            starts[k] = first - shift
            used = k < blocks
            for half in range(2):
                for side in range(2):
                    touches = used & ((cx == 0) | (cx == half + 1)) & ((cy == 0) | (cy == side + 1))
                    tasks[count] = k * 4 + half * 2 + side
                    count = count + touches.astype(jnp.int32)
        return count

    jobs = lax.fori_loop(0, (blocks + WAYS - 1) // WAYS, weigh, jnp.int32(0))
    for extra in range(WAYS - 1):
        tasks[jobs + extra] = EMPTY * 4

    for load in load_own:
        load.wait()

    def spread(group, carry):
        for way in range(WAYS):
            code = tasks[group * WAYS + way]
            k = code // 4
            half = code // 2 % 2
            side = code % 2
            wx = wx_all[pl.ds(pl.multiple_of(k * SPAN + half * 16, 16), 16), :]
            wy = wy_all[pl.ds(pl.multiple_of(k * SPAN + side * 16, 16), 16), :]
            product = (wx[:, None, :] * wy[None, :, :]).reshape(256, LANES)
            high, low = split(product)
            wz = wz_all[pl.ds(pl.multiple_of(k * 24, 8), 24), :]
            z_high = wz.astype(jnp.bfloat16).astype(f32)
            left = jnp.concatenate([z_high, wz - z_high], axis=0).astype(jnp.bfloat16)
            patch = lax.dot_general(
                jnp.concatenate([left, left], axis=1), jnp.concatenate([high, low], axis=1),
                (((1,), (1,)), ((), ())), preferred_element_type=f32)
            rows = pl.ds(pl.multiple_of((code % 4) * Z_ROWS + starts[k], 8), 24)
            density[rows, :] = density[rows, :] + patch[:24] + patch[24:]
        return carry

    lax.fori_loop(0, (jobs + WAYS - 1) // WAYS, spread, jnp.int32(0))

    length = LENGTH
    gap = lax.broadcasted_iota(jnp.int32, (length, length), 0) - lax.broadcasted_iota(jnp.int32, (length, length), 1)
    gap_f = gap.astype(f32)
    tau_v = jnp.broadcast_to(SMOOTH * scales[2][:, :1], (length, length))
    band = jnp.exp(-gap_f * gap_f / (2.0 * tau_v * tau_v)) * (COUPLING / (math.sqrt(2.0 * math.pi) * tau_v))
    band_high, band_low = split(jnp.where(jnp.abs(gap) <= RADIUS, band, 0.0))
    for half in range(2):
        for side in range(2):
            part = density[pl.ds((half * 2 + side) * Z_ROWS + 16, length), :]
            high, low = split(part)
            smooth = (jnp.dot(band_high, high, preferred_element_type=f32)
                      + jnp.dot(band_high, low, preferred_element_type=f32)
                      + jnp.dot(band_low, high, preferred_element_type=f32))
            turned = smooth[8:8 + CZ].T
            edge = jnp.concatenate([smooth[4:8], smooth[8 + CZ:12 + CZ]], axis=0)
            edge_high = edge.astype(jnp.bfloat16).astype(f32)
            edges = jnp.concatenate([edge_high, edge - edge_high, edge_high, jnp.zeros((LANES - 24, 256), f32)], axis=0).T
            turned_high, turned_low = split(turned)
            cube = turned.reshape(16, 16, CZ)
            low_x, low_y = (1 - half) * RIM, (1 - side) * RIM
            potential[pl.ds(half * 12, 12), pl.ds(side * 12, 12), :] = cube[low_x:low_x + 12, low_y:low_y + 12, :]
            place = (pl.ds(half * 16, 16), pl.ds(side * 16, 16))
            for i, block in enumerate((turned_high, turned_low, turned_high, edges.astype(jnp.bfloat16))):
                field[place[0], place[1], pl.ds(i * LANES, LANES)] = block.reshape(16, 16, LANES)

    iota32 = lax.broadcasted_iota(jnp.int32, (SPAN, LANES), 0)
    iota_z = lax.broadcasted_iota(jnp.int32, (CZ, LANES), 0)
    iota8 = lax.broadcasted_iota(jnp.int32, (8, LANES), 0)
    edge_z = jnp.where(iota8 < 4, iota8 - 4, iota8 + (CZ - 4))

    def force(b):
        x = atoms[0, pl.ds(b, 1), :] * scales[0]
        y = atoms[0, pl.ds(b + BLOCKS, 1), :] * scales[1]
        z = atoms[0, pl.ds(b + 2 * BLOCKS, 1), :] * scales[2]
        q = atoms[0, pl.ds(b + 3 * BLOCKS, 1), :]
        at_x = meta[0, b]
        at_y = meta[0, BLOCKS + b]
        at_z = meta[0, 2 * BLOCKS + b]
        wx, sx = window(x, iota16, widths[0])
        wy, sy = window(y, iota32 - at_y, widths[1])
        wz, sz = window(z, iota_z - at_z + RIM, widths[2])
        we, se = window(z, edge_z - at_z + RIM, widths[2])
        main_high, main_low = split(jnp.concatenate([wz, sz], axis=1))
        rim = jnp.concatenate([we, se], axis=1)
        rim_high = rim.astype(jnp.bfloat16).astype(f32)
        rim = jnp.concatenate([rim_high, rim_high, rim - rim_high, jnp.zeros((LANES - 24, 256), f32)], axis=0).astype(jnp.bfloat16)
        right = jnp.concatenate([main_high, main_high, main_low, rim], axis=0)
        left = field[pl.ds(at_x, PATCH)].reshape(PATCH * SPAN, 4 * LANES)
        values = jnp.dot(left, right, preferred_element_type=f32).reshape(PATCH, SPAN, 256)
        by_sx = jnp.zeros((SPAN, LANES), f32)
        by_wx = jnp.zeros((SPAN, LANES), f32)
        by_wz = jnp.zeros((SPAN, LANES), f32)
        for i in range(PATCH):
            level = values[i, :, :LANES]
            by_sx = by_sx + level * sx[i:i + 1]
            by_wx = by_wx + level * wx[i:i + 1]
            by_wz = by_wz + values[i, :, LANES:] * wx[i:i + 1]
        for a, total in enumerate((by_sx * wy, by_wx * sy, by_wz * wy)):
            forces[a:a + 1, b * LANES:(b + 1) * LANES] = -q * scales[a] * jnp.sum(total, axis=0, keepdims=True)

    for b in range(BLOCKS):
        force(b)


def make_field(atoms, meta, own):
    anywhere = pl.BlockSpec(memory_space=pl.ANY)
    vmem = pl.BlockSpec(memory_space=pltpu.VMEM)
    f32, i32 = jnp.float32, jnp.int32
    return pl.pallas_call(
        field_kernel,
        out_shape=(jax.ShapeDtypeStruct((CX, CY, CZ), f32), jax.ShapeDtypeStruct((3, BLOCKS * LANES), f32)),
        in_specs=[anywhere, anywhere, anywhere],
        out_specs=(vmem, vmem),
        scratch_shapes=[
            pltpu.SMEM((32, LANES), i32),
            pltpu.VMEM((SOURCES + 1, ROWS, LANES), f32),
            pltpu.SemaphoreType.DMA((6,)),
            pltpu.SMEM((EMPTY + 1,), i32),
            pltpu.SMEM((SLOTS * 4 + WAYS,), i32),
            pltpu.SMEM((EMPTY + 1,), i32),
            pltpu.VMEM((WAYS, 96, LANES), f32),
            pltpu.VMEM((WAYS, 96, LANES), f32),
            pltpu.VMEM((WAYS, 32, LANES), f32),
            pltpu.VMEM(((EMPTY + 1) * SPAN, LANES), f32),
            pltpu.VMEM(((EMPTY + 1) * SPAN, LANES), f32),
            pltpu.VMEM(((EMPTY + 1) * 24, LANES), f32),
            pltpu.VMEM((4 * Z_ROWS, 256), f32),
            pltpu.VMEM((SPAN, SPAN, 4 * LANES), jnp.bfloat16),
        ],
        compiler_params=pltpu.CompilerParams(vmem_limit_bytes=60 * 1024 * 1024),
        name="field_and_forces",
    )(meta, atoms, own)


def exchange_kernel(pos_in, q_in, anchor_in, atoms_in, blocks_in, scale_in, atoms_out, meta_out, own_out, pos_ref, q_ref, anchor_ref, atoms_ref, blocks_ref, scale_ref, rows_ref, pad_x, pad_y, pad_z, wx_own, wy_own, wz_own, load_sems, send_sems, recv_sems, ready_sems):
    gx, gy, gz = (lax.axis_index(a) for a in ("gx", "gy", "gz"))
    nx, ny, nz = (lax.axis_size(a) for a in ("gx", "gy", "gz"))
    half = ny // 2

    def device(dx, dy, dz):
        return (lax.rem(gx + dx + nx, nx), lax.rem(gy + dy + ny, ny), lax.rem(gz + dz + nz, nz))

    def both(condition, other):
        return condition & jnp.logical_not(other)

    late = gy >= half
    far = {1: lax.rem(gy, half) == half - 1, -1: lax.rem(gy, half) == 0}
    wrap = {1: gz == nz - 1, -1: gz == 0}
    far_any = far[1] | far[-1]
    sided_y = gz < ONE_SIDED
    sided_z = jnp.logical_not(late & jnp.logical_not(far_any))
    hold = wrap[-1] & sided_z
    ends = wrap[1] | wrap[-1]
    direct = both(far_any, ends)
    corner = far_any & (wrap[1] | wrap[-1])
    pushes = corner & late & wrap[-1]
    pushed = both(corner & wrap[-1], late)
    hands = both(corner, wrap[1] & jnp.logical_not(late))
    far_step = jnp.where(far[1], 1, -1)
    wrap_step = jnp.where(wrap[1], 1, -1)
    steps = (1, -1)
    code = {1: 1, -1: 2}
    across = (0, 1, -1)
    ready_z, ready_y, ready_c = (ready_sems.at[i] for i in range(3))

    def when(condition, action):
        pl.when(condition)(action)

    def signal(semaphore, *offsets):
        pl.semaphore_signal(semaphore, inc=1, device_id=device(*offsets), device_id_type=MESH)

    barrier = pltpu.get_barrier_semaphore()

    def greet_far():
        signal(barrier, 0, far_step, 0)

    def greet_corner():
        for dx in across:
            signal(barrier, dx, far_step, wrap_step)

    def greet_z(step):
        signal(barrier, 0, 0, step)
        for dx in steps:
            when(jnp.logical_not(wrap[step]), lambda: signal(barrier, dx, 0, step))

    when(both(direct, late & sided_y) | pushed, greet_far)
    when(both(corner, late), greet_corner)
    for step in steps:
        signal(barrier, step, 0, 0)
        when(jnp.logical_not(far[step]), lambda: signal(barrier, 0, step, 0))
    greet_z(-1)
    when(jnp.logical_not(wrap[1] & sided_z), lambda: greet_z(1))
    loads = []
    for i, (src, dst) in enumerate(((pos_in, pos_ref), (q_in, q_ref), (anchor_in, anchor_ref), (atoms_in, atoms_ref), (blocks_in, blocks_ref), (scale_in, scale_ref))):
        loads.append(pltpu.make_async_copy(src, dst, load_sems.at[i]))
        loads[-1].start()
    for load in loads:
        load.wait()
    for a in range(3):
        for b in range(BLOCKS):
            atoms_out[0, pl.ds(a * BLOCKS + b, 1), :] = pos_ref[pl.ds(a, 1), pl.ds(b * LANES, LANES)]
    row = lax.broadcasted_iota(jnp.int32, (BLOCKS, LANES), 0)
    lane = lax.broadcasted_iota(jnp.int32, (BLOCKS, LANES), 1)
    filled = jnp.zeros((BLOCKS, LANES), jnp.int32)
    for b in range(BLOCKS):
        filled = jnp.where(row == b, jnp.where(b < blocks_ref[0], atoms_ref[b], 0), filled)
    atoms_out[0, pl.ds(3 * BLOCKS, BLOCKS), :] = jnp.where(lane < filled, q_ref[...], 0.0)
    meta = jnp.zeros((BLOCKS, LANES), jnp.int32)
    for a in range(3):
        for b in range(BLOCKS):
            meta = jnp.where(lane == a * BLOCKS + b, anchor_ref[a, b], meta)
    for b in range(BLOCKS):
        meta = jnp.where(lane == 3 * BLOCKS + b, jnp.where(b < blocks_ref[0], 1, 0), meta)
    atoms_out[0, pl.ds(32, 1), :] = meta[:1].astype(jnp.float32)
    peers = 10 - jnp.where(hold, 3, jnp.where(ends, 2, 0)) - jnp.where(both(corner, pushes) | both(direct & sided_y, late), 1, 0) + jnp.where(corner & late, 3, 0)
    pl.semaphore_wait(barrier, peers)

    def answer_corner():
        for dx in across:
            signal(ready_c, dx, far_step, wrap_step)

    when(direct & late & sided_y, lambda: signal(ready_y, 0, far_step, 0))
    when(wrap[1] & sided_z, lambda: signal(ready_z, 0, 0, 1))
    when(corner & late, answer_corner)

    def slot(cx, cz, cy):
        return (cx * 3 + cz) * 3 + cy

    def piece(src, dst, target, index):
        return pltpu.make_async_remote_copy(
            src_ref=atoms_out.at[src], dst_ref=atoms_out.at[dst],
            send_sem=send_sems.at[index], recv_sem=recv_sems.at[dst],
            device_id=target, device_id_type=MESH)

    def along_y(step):
        dst = slot(0, 0, code[step])
        return [piece(0, dst, device(0, step, 0), dst)]

    def along_x(cy):
        return [piece(cy, slot(code[dx], 0, cy), device(dx, 0, 0), slot(code[dx], 0, cy)) for dx in steps]

    def fan(cy, step):
        places = [(dx, slot(code[dx] if dx else 0, code[step], cy)) for dx in across]
        return [piece(cy, dst, device(dx, 0, step), dst) for dx, dst in places]

    def corners():
        out = []
        for i, dx in enumerate(across):
            dst = slot(code[dx] if dx else 0, jnp.where(wrap[1], 1, 2), jnp.where(far[1], 1, 2))
            out.append(piece(0, dst, device(dx, far_step, wrap_step), 27 + i))
        return out

    def start(copies):
        for copy in copies:
            copy.start()

    def finish(copies):
        for copy in copies:
            copy.wait_send()

    from_far = {1: far[-1], 2: far[1]}

    def send_early(cy):
        start(along_x(cy))
        start(fan(cy, 1)[:1])
        when(jnp.logical_not(hold), lambda: start(fan(cy, -1)[:1]))
        for step in steps:
            when(jnp.logical_not(wrap[step]), lambda: start(fan(cy, step)[1:]))

    def pass_near(cy):
        along_y(1 if cy == 1 else -1)[0].wait_recv()
        send_early(cy)

    def pass_far(cy):
        along_y(1 if cy == 1 else -1)[0].wait_recv()
        start(along_x(cy))
        for step in steps:
            when(jnp.logical_not(wrap[step]), lambda: start(fan(cy, step)))

    def open_wrap():
        pl.semaphore_wait(ready_z, 1)
        start(fan(0, -1)[:1])
        for cy in (1, 2):
            when(jnp.logical_not(from_far[cy]), lambda: start(fan(cy, -1)[:1]))

    def onward(cy, step):
        src = slot(0, code[step], cy)
        return [piece(src, slot(code[dx], code[step], cy), device(dx, 0, 0), 31 + cy * 2 + i) for i, dx in enumerate(steps)]

    def pass_wrap(cy, step):
        fan(cy, step)[0].wait_recv()
        start(onward(cy, step))

    def open_corner():
        pl.semaphore_wait(ready_c, 3)
        start(corners())

    def handed():
        corner_slot = slot(0, jnp.where(wrap[1], 2, 1), jnp.where(far[1], 2, 1))
        own_slot = slot(0, 0, jnp.where(far[1], 2, 1))
        return piece(corner_slot, own_slot, device(0, 0, wrap_step), 30)

    def forward_corner():
        corner_slot = slot(0, jnp.where(wrap[1], 2, 1), jnp.where(far[1], 2, 1))
        piece(corner_slot, corner_slot, device(0, 0, wrap_step), 30).wait_recv()
        when(hands, handed().start)

    def open_far():
        pl.semaphore_wait(ready_y, 1)
        for step in steps:
            when(far[step], lambda: start(along_y(step)))

    for step in steps:
        when(jnp.logical_not(far[step] & (ends | both(sided_y, late))) | (far[step] & pushes), lambda: start(along_y(step)))
    when(corner & late, lambda: start(corners()))
    send_early(0)
    for cy in (1, 2):
        when(jnp.logical_not(from_far[cy]), lambda: pass_near(cy))
    spread_own(atoms_out, anchor_ref, scale_ref, pad_x, pad_y, pad_z, wx_own, wy_own, wz_own, own_out)
    when(hold, open_wrap)
    when(both(corner, late), open_corner)
    when(corner, forward_corner)
    for step in steps:
        when(wrap[-step], lambda: pass_wrap(0, step))
        for cy in (1, 2):
            when(both(wrap[-step], from_far[cy]), lambda: pass_wrap(cy, step))
    when(both(direct & sided_y, late), open_far)
    for cy in (1, 2):
        when(from_far[cy], lambda: pass_far(cy))
    for cy in range(3):
        for copy in along_x(cy):
            copy.wait_recv()
        for step in steps:
            copies = fan(cy, step)
            when(jnp.logical_not(wrap[-step]), copies[0].wait_recv)
            for copy in copies[1:]:
                copy.wait_recv()
    for step in steps:
        when(jnp.logical_not(far[step] & ends) | (far[step] & pushes), lambda: finish(along_y(step)))
    for cy in range(3):
        finish(along_x(cy))
        for step in steps:
            when(jnp.logical_not(wrap[step]), lambda: finish(fan(cy, step)[1:]))
            if cy == 0:
                finish(fan(cy, step)[:1])
                when(wrap[-step], lambda: finish(onward(cy, step)))
            else:
                when(jnp.logical_not(from_far[cy] & wrap[step]), lambda: finish(fan(cy, step)[:1]))
                when(both(wrap[-step], from_far[cy]), lambda: finish(onward(cy, step)))
    when(corner, lambda: finish(corners()))
    when(hands, lambda: finish([handed()]))
    for a in range(3):
        atoms_out[SOURCES, pl.ds(a, 1), :] = jnp.full((1, LANES), scale_ref[a], jnp.float32)
    rows_ref[...] = jnp.zeros_like(rows_ref)
    for n in range(SOURCES):
        rows_ref[pl.ds(n, 1), :] = atoms_out[n, pl.ds(32, 1), :]
    value = rows_ref[...].astype(jnp.int32)
    source = lax.broadcasted_iota(jnp.int32, value.shape, 0)
    place = lax.broadcasted_iota(jnp.int32, value.shape, 1)
    one = jnp.ones_like(value)
    zero = jnp.zeros_like(value)
    cx = jnp.where(source >= 9, one, zero) + jnp.where(source >= 18, one, zero)
    rest = source - 9 * cx
    cz = jnp.where(rest >= 3, one, zero) + jnp.where(rest >= 6, one, zero)
    cy = rest - 3 * cz
    is_z = (place >= 2 * BLOCKS) & (place < 3 * BLOCKS)
    is_live = place >= 3 * BLOCKS
    kind = jnp.where(place < BLOCKS, cx, jnp.where(place < 2 * BLOCKS, cy, cz))
    period = jnp.where(is_z, CZ, CX)
    low = jnp.where(is_live, 1, jnp.where(kind == 1, jnp.where(is_z, CZ - 19, 5), 0))
    high = jnp.where(jnp.logical_not(is_live) & (kind == 2), 11, 999)
    fits = jnp.where((value >= low) & (value <= high), one, zero)
    used = fits
    for group in (1, 2, 3):
        used = used * pltpu.roll(fits, LANES - group * BLOCKS, 1)
    used = pltpu.roll(used, 4 * BLOCKS, 1)
    shifted = value + jnp.where(is_live | (kind == 0), 0, jnp.where(kind == 1, -period, period))
    meta_out[...] = jnp.where(place >= 4 * BLOCKS, used, shifted)


def spread_own(atoms, anchor, scale_ref, pad_x, pad_y, pad_z, wx_own, wy_own, wz_own, own_out):
    f32 = jnp.float32
    scales = [jnp.full((1, LANES), scale_ref[a], f32) for a in range(3)]
    widths = [SPREAD * s for s in scales]
    taps = kernel_taps(scales)
    iota16 = lax.broadcasted_iota(jnp.int32, (PATCH, LANES), 0)
    for ref in (pad_x, pad_y, pad_z):
        ref[...] = jnp.zeros_like(ref)

    def weigh(b, carry):
        x = atoms[0, pl.ds(b, 1), :] * scales[0]
        y = atoms[0, pl.ds(b + BLOCKS, 1), :] * scales[1]
        z = atoms[0, pl.ds(b + 2 * BLOCKS, 1), :] * scales[2]
        q = atoms[0, pl.ds(b + 3 * BLOCKS, 1), :]
        pad_x[b, pl.ds(PAD, PATCH), :] = q * window(x, iota16, widths[0])[0]
        pad_y[b, pl.ds(PAD, PATCH), :] = window(y, iota16, widths[1])[0]
        pad_z[b, pl.ds(LENGTH, PATCH), :] = window(z, iota16, widths[2])[0]
        for a, pad, out in ((0, pad_x, wx_own), (1, pad_y, wy_own)):
            start = PAD - anchor[a, b]
            total = taps[a][0] * pad[b, pl.ds(start, SPAN), :]
            for e in range(1, RADIUS + 1):
                total = total + taps[a][e] * (pad[b, pl.ds(start - e, SPAN), :] + pad[b, pl.ds(start + e, SPAN), :])
            out[b] = total
        high, low = split(pad_z[b, pl.ds(LENGTH - 4 - anchor[2, b], LENGTH), :])
        wz_own[b, pl.ds(0, LENGTH), :] = high
        wz_own[b, pl.ds(LENGTH, LENGTH), :] = low
        return carry

    lax.fori_loop(0, BLOCKS, weigh, jnp.int32(0))

    def spread(quarter, carry):
        half = quarter // 2
        side = quarter % 2
        left, right = [], []
        for b in range(BLOCKS):
            wx = wx_own[b, pl.ds(pl.multiple_of(half * 16, 16), 16), :]
            wy = wy_own[b, pl.ds(pl.multiple_of(side * 16, 16), 16), :]
            right += split((wx[:, None, :] * wy[None, :, :]).reshape(256, LANES))
            left += [wz_own[b]] * 2
        patch = lax.dot_general(
            jnp.concatenate(left, axis=1), jnp.concatenate(right, axis=1),
            (((1,), (1,)), ((), ())), preferred_element_type=f32)
        own_out[quarter] = patch[:LENGTH] + patch[LENGTH:]
        return carry

    lax.fori_loop(0, 4, spread, jnp.int32(0))


def exchange(positions, charges, block_anchor, block_atoms, brick_blocks, box_scale):
    anywhere = pl.BlockSpec(memory_space=pl.ANY)
    vmem = pl.BlockSpec(memory_space=pltpu.VMEM)
    f32, i32 = jnp.float32, jnp.int32
    return pl.pallas_call(
        exchange_kernel,
        out_shape=(jax.ShapeDtypeStruct((SOURCES + 1, ROWS, LANES), f32), jax.ShapeDtypeStruct((32, LANES), i32),
                   jax.ShapeDtypeStruct((4, LENGTH, 256), f32)),
        in_specs=[anywhere] * 6,
        out_specs=(vmem, vmem, vmem),
        scratch_shapes=[
            pltpu.VMEM((3, BLOCKS * LANES), f32),
            pltpu.VMEM((BLOCKS, LANES), f32),
            pltpu.SMEM((3, BLOCKS), i32),
            pltpu.SMEM((BLOCKS,), i32),
            pltpu.SMEM((1,), i32),
            pltpu.SMEM((3,), f32),
            pltpu.VMEM((32, LANES), f32),
            pltpu.VMEM((BLOCKS, 96, LANES), f32),
            pltpu.VMEM((BLOCKS, 96, LANES), f32),
            pltpu.VMEM((BLOCKS, 2 * LENGTH + PATCH, LANES), f32),
            pltpu.VMEM((BLOCKS, SPAN, LANES), f32),
            pltpu.VMEM((BLOCKS, SPAN, LANES), f32),
            pltpu.VMEM((BLOCKS, 2 * LENGTH, LANES), jnp.bfloat16),
            pltpu.SemaphoreType.DMA((6,)),
            pltpu.SemaphoreType.DMA((40,)),
            pltpu.SemaphoreType.DMA((SOURCES,)),
            pltpu.SemaphoreType.REGULAR((3,)),
        ],
        compiler_params=pltpu.CompilerParams(collective_id=0, has_side_effects=True, vmem_limit_bytes=60 * 1024 * 1024),
        name="exchange_atoms",
    )(positions, charges.reshape(BLOCKS, LANES), block_anchor, block_atoms, brick_blocks, box_scale)


def per_device(positions, charges, block_anchor, block_atoms, brick_blocks, box_scale):
    atoms, meta, own = exchange(positions, charges, block_anchor, block_atoms, brick_blocks, box_scale)
    potential, forces = make_field(atoms, meta, own)
    return (potential, forces)


def solution(mesh):
    split_all = ("gx", "gy", "gz")
    return jax.shard_map(
        per_device,
        mesh=mesh,
        in_specs=(P(None, split_all), P(split_all), P(None, split_all), P(split_all), P(split_all), P()),
        out_specs=(P("gx", "gy", "gz"), P(None, split_all)),
        check_vma=False,
    )
```

```python
import math
import jax, jax.numpy as jnp
from jax import lax
from jax.experimental import pallas as pl
from jax.experimental.pallas import tpu as pltpu

from jax.sharding import PartitionSpec as P

MESH = pl.DeviceIdType.MESH
CX = 24
CY = 24
CZ = 128
PATCH = 16
RIM = 4
RADIUS = 4
SPREAD = 1.0
SMOOTH = 1.5
COUPLING = 200.0
ROWS = 33
ONE_SIDED = 3
BLOCKS = 8
LANES = 128
SOURCES = 27
SLOTS = SOURCES * BLOCKS
SPAN = 32
Z_ROWS = 176
WAYS = 16
EMPTY = SLOTS + WAYS
PAD = 40
LENGTH = CZ + 2 * (RIM + RADIUS)


def norm(width):
    return 1.0 / (math.sqrt(2.0 * math.pi) * width)


def window(coord, place, width):
    offset = coord + RIM - place.astype(jnp.float32)
    inside = (place >= 0) & (place < PATCH)
    weight = jnp.exp(-offset * offset / (2.0 * width * width)) * norm(width)
    weight = jnp.where(inside, weight, 0.0)
    return weight, -offset / (width * width) * weight


def split(value):
    high = value.astype(jnp.bfloat16)
    return high, (value - high.astype(jnp.float32)).astype(jnp.bfloat16)


def kernel_taps(scales):
    taps = []
    for scale in scales:
        tau = SMOOTH * scale
        taps.append([jnp.exp(-float(e * e) / (2.0 * tau * tau)) * norm(tau) for e in range(RADIUS + 1)])
    return taps


def field_kernel(meta_in, atoms, near_in, rights, potential, forces, meta, load_sems, order, tasks, starts, pad_x, pad_y, pad_z, wx_all, wy_all, wz_all, density, field):
    f32 = jnp.float32
    load_meta = pltpu.make_async_copy(meta_in, meta, load_sems.at[0])
    load_meta.start()
    load_near = []
    for quarter in range(4):
        load_near.append(pltpu.make_async_copy(near_in.at[quarter], density.at[pl.ds(quarter * Z_ROWS + 16, LENGTH)], load_sems.at[1 + quarter]))
        load_near[-1].start()
    for quarter in range(4):
        for first in (0, 16 + LENGTH):
            density[pl.ds(quarter * Z_ROWS + first, 16), :] = jnp.zeros((16, 256), f32)
    for ref in (pad_x, pad_y, pad_z):
        ref[...] = jnp.zeros_like(ref)
    wx_all[pl.ds(EMPTY * SPAN, SPAN), :] = jnp.zeros((SPAN, LANES), f32)
    wy_all[pl.ds(EMPTY * SPAN, SPAN), :] = jnp.zeros((SPAN, LANES), f32)
    wz_all[pl.ds(EMPTY * 24, 24), :] = jnp.zeros((24, LANES), f32)
    starts[EMPTY] = 0
    load_meta.wait()

    def choose(n, count):
        for b in range(BLOCKS):
            order[count] = n * BLOCKS + b
            count = count + meta[n, 4 * BLOCKS + b]
        return count

    blocks = lax.fori_loop(1, SOURCES, choose, jnp.int32(0))
    for extra in range(WAYS - 1):
        order[blocks + extra] = 0
    scales = [atoms[SOURCES, pl.ds(a, 1), :] for a in range(3)]
    widths = [SPREAD * s for s in scales]
    taps = kernel_taps(scales)

    iota16 = lax.broadcasted_iota(jnp.int32, (PATCH, LANES), 0)

    def weigh(group, count):
        for way in range(WAYS):
            k = group * WAYS + way
            code = order[k]
            n = code // BLOCKS
            b = code % BLOCKS
            cx = n // 9
            cy = n % 3
            off_x = meta[n, b]
            off_y = meta[n, BLOCKS + b]
            off_z = meta[n, 2 * BLOCKS + b]
            x = atoms[n, pl.ds(b, 1), :] * scales[0]
            y = atoms[n, pl.ds(b + BLOCKS, 1), :] * scales[1]
            z = atoms[n, pl.ds(b + 2 * BLOCKS, 1), :] * scales[2]
            q = atoms[n, pl.ds(b + 3 * BLOCKS, 1), :]
            pad_x[way, pl.ds(PAD, PATCH), :] = q * window(x, iota16, widths[0])[0]
            pad_y[way, pl.ds(PAD, PATCH), :] = window(y, iota16, widths[1])[0]
            pad_z[way, pl.ds(8, PATCH), :] = window(z, iota16, widths[2])[0]
            for a, off, pad, out in ((0, off_x, pad_x, wx_all), (1, off_y, pad_y, wy_all)):
                start = PAD - off
                total = taps[a][0] * pad[way, pl.ds(start, SPAN), :]
                for e in range(1, RADIUS + 1):
                    total = total + taps[a][e] * (pad[way, pl.ds(start - e, SPAN), :] + pad[way, pl.ds(start + e, SPAN), :])
                out[pl.ds(pl.multiple_of(k * SPAN, SPAN), SPAN), :] = total
            first = off_z + 20
            shift = first & 7
            wz_all[pl.ds(pl.multiple_of(k * 24, 8), 24), :] = pad_z[way, pl.ds(8 - shift, 24), :]
            starts[k] = first - shift
            used = k < blocks
            for half in range(2):
                for side in range(2):
                    touches = used & ((cx == 0) | (cx == half + 1)) & ((cy == 0) | (cy == side + 1))
                    tasks[count] = k * 4 + half * 2 + side
                    count = count + touches.astype(jnp.int32)
        return count

    jobs = lax.fori_loop(0, (blocks + WAYS - 1) // WAYS, weigh, jnp.int32(0))
    for extra in range(WAYS - 1):
        tasks[jobs + extra] = EMPTY * 4

    for load in load_near:
        load.wait()

    def spread(group, carry):
        for way in range(WAYS):
            code = tasks[group * WAYS + way]
            k = code // 4
            half = code // 2 % 2
            side = code % 2
            wx = wx_all[pl.ds(pl.multiple_of(k * SPAN + half * 16, 16), 16), :]
            wy = wy_all[pl.ds(pl.multiple_of(k * SPAN + side * 16, 16), 16), :]
            product = (wx[:, None, :] * wy[None, :, :]).reshape(256, LANES)
            high, low = split(product)
            wz = wz_all[pl.ds(pl.multiple_of(k * 24, 8), 24), :]
            z_high = wz.astype(jnp.bfloat16).astype(f32)
            left = jnp.concatenate([z_high, wz - z_high], axis=0).astype(jnp.bfloat16)
            patch = lax.dot_general(
                jnp.concatenate([left, left], axis=1), jnp.concatenate([high, low], axis=1),
                (((1,), (1,)), ((), ())), preferred_element_type=f32)
            rows = pl.ds(pl.multiple_of((code % 4) * Z_ROWS + starts[k], 8), 24)
            density[rows, :] = density[rows, :] + patch[:24] + patch[24:]
        return carry

    lax.fori_loop(0, (jobs + WAYS - 1) // WAYS, spread, jnp.int32(0))

    length = LENGTH
    gap = lax.broadcasted_iota(jnp.int32, (length, length), 0) - lax.broadcasted_iota(jnp.int32, (length, length), 1)
    gap_f = gap.astype(f32)
    tau_v = jnp.broadcast_to(SMOOTH * scales[2][:, :1], (length, length))
    band = jnp.exp(-gap_f * gap_f / (2.0 * tau_v * tau_v)) * (COUPLING / (math.sqrt(2.0 * math.pi) * tau_v))
    band_high, band_low = split(jnp.where(jnp.abs(gap) <= RADIUS, band, 0.0))
    for half in range(2):
        for side in range(2):
            part = density[pl.ds((half * 2 + side) * Z_ROWS + 16, length), :]
            high, low = split(part)
            smooth = (jnp.dot(band_high, high, preferred_element_type=f32)
                      + jnp.dot(band_high, low, preferred_element_type=f32)
                      + jnp.dot(band_low, high, preferred_element_type=f32))
            turned = smooth[8:8 + CZ].T
            edge = jnp.concatenate([smooth[4:8], smooth[8 + CZ:12 + CZ]], axis=0)
            edge_high = edge.astype(jnp.bfloat16).astype(f32)
            edges = jnp.concatenate([edge_high, edge - edge_high, edge_high, jnp.zeros((LANES - 24, 256), f32)], axis=0).T
            turned_high, turned_low = split(turned)
            cube = turned.reshape(16, 16, CZ)
            low_x, low_y = (1 - half) * RIM, (1 - side) * RIM
            potential[pl.ds(half * 12, 12), pl.ds(side * 12, 12), :] = cube[low_x:low_x + 12, low_y:low_y + 12, :]
            place = (pl.ds(half * 16, 16), pl.ds(side * 16, 16))
            for i, block in enumerate((turned_high, turned_low, turned_high, edges.astype(jnp.bfloat16))):
                field[place[0], place[1], pl.ds(i * LANES, LANES)] = block.reshape(16, 16, LANES)

    iota32 = lax.broadcasted_iota(jnp.int32, (SPAN, LANES), 0)
    def force(b):
        x = atoms[0, pl.ds(b, 1), :] * scales[0]
        y = atoms[0, pl.ds(b + BLOCKS, 1), :] * scales[1]
        q = atoms[0, pl.ds(b + 3 * BLOCKS, 1), :]
        at_x = meta[0, b]
        at_y = meta[0, BLOCKS + b]
        wx, sx = window(x, iota16, widths[0])
        wy, sy = window(y, iota32 - at_y, widths[1])
        left = field[pl.ds(at_x, PATCH)].reshape(PATCH * SPAN, 4 * LANES)
        values = jnp.dot(left, rights[b], preferred_element_type=f32).reshape(PATCH, SPAN, 256)
        by_sx = jnp.zeros((SPAN, LANES), f32)
        by_wx = jnp.zeros((SPAN, LANES), f32)
        by_wz = jnp.zeros((SPAN, LANES), f32)
        for i in range(PATCH):
            level = values[i, :, :LANES]
            by_sx = by_sx + level * sx[i:i + 1]
            by_wx = by_wx + level * wx[i:i + 1]
            by_wz = by_wz + values[i, :, LANES:] * wx[i:i + 1]
        for a, total in enumerate((by_sx * wy, by_wx * sy, by_wz * wy)):
            forces[a:a + 1, b * LANES:(b + 1) * LANES] = -q * scales[a] * jnp.sum(total, axis=0, keepdims=True)

    for b in range(BLOCKS):
        force(b)


def make_field(atoms, meta, near, rights):
    anywhere = pl.BlockSpec(memory_space=pl.ANY)
    vmem = pl.BlockSpec(memory_space=pltpu.VMEM)
    f32, i32 = jnp.float32, jnp.int32
    return pl.pallas_call(
        field_kernel,
        out_shape=(jax.ShapeDtypeStruct((CX, CY, CZ), f32), jax.ShapeDtypeStruct((3, BLOCKS * LANES), f32)),
        in_specs=[anywhere, vmem, anywhere, vmem],
        out_specs=(vmem, vmem),
        scratch_shapes=[
            pltpu.SMEM((32, LANES), i32),
            pltpu.SemaphoreType.DMA((5,)),
            pltpu.SMEM((EMPTY + 1,), i32),
            pltpu.SMEM((SLOTS * 4 + WAYS,), i32),
            pltpu.SMEM((EMPTY + 1,), i32),
            pltpu.VMEM((WAYS, 96, LANES), f32),
            pltpu.VMEM((WAYS, 96, LANES), f32),
            pltpu.VMEM((WAYS, 32, LANES), f32),
            pltpu.VMEM(((EMPTY + 1) * SPAN, LANES), f32),
            pltpu.VMEM(((EMPTY + 1) * SPAN, LANES), f32),
            pltpu.VMEM(((EMPTY + 1) * 24, LANES), f32),
            pltpu.VMEM((4 * Z_ROWS, 256), f32),
            pltpu.VMEM((SPAN, SPAN, 4 * LANES), jnp.bfloat16),
        ],
        compiler_params=pltpu.CompilerParams(vmem_limit_bytes=24 * 1024 * 1024),
        name="field_and_forces",
    )(meta, atoms, near, rights)


def exchange_kernel(pos_in, q_in, anchor_in, atoms_in, blocks_in, scale_in, atoms_out, meta_out, near_out, right_out, pos_ref, q_ref, anchor_ref, atoms_ref, blocks_ref, scale_ref, rows_ref, pad_x, pad_y, pad_z, wx_near, wy_near, wz_near, near_sum, rights, load_sems, send_sems, recv_sems, ready_sems):
    gx, gy, gz = (lax.axis_index(a) for a in ("gx", "gy", "gz"))
    nx, ny, nz = (lax.axis_size(a) for a in ("gx", "gy", "gz"))
    half = ny // 2

    def device(dx, dy, dz):
        return (lax.rem(gx + dx + nx, nx), lax.rem(gy + dy + ny, ny), lax.rem(gz + dz + nz, nz))

    def both(condition, other):
        return condition & jnp.logical_not(other)

    late = gy >= half
    far = {1: lax.rem(gy, half) == half - 1, -1: lax.rem(gy, half) == 0}
    wrap = {1: gz == nz - 1, -1: gz == 0}
    far_any = far[1] | far[-1]
    sided_y = gz < ONE_SIDED
    sided_z = jnp.logical_not(late & jnp.logical_not(far_any))
    hold = wrap[-1] & sided_z
    ends = wrap[1] | wrap[-1]
    direct = both(far_any, ends)
    corner = far_any & (wrap[1] | wrap[-1])
    pushes = corner & late & wrap[-1]
    pushed = both(corner & wrap[-1], late)
    hands = both(corner, wrap[1] & jnp.logical_not(late))
    far_step = jnp.where(far[1], 1, -1)
    wrap_step = jnp.where(wrap[1], 1, -1)
    steps = (1, -1)
    code = {1: 1, -1: 2}
    across = (0, 1, -1)
    ready_z, ready_y, ready_c = (ready_sems.at[i] for i in range(3))

    def when(condition, action):
        pl.when(condition)(action)

    def signal(semaphore, *offsets):
        pl.semaphore_signal(semaphore, inc=1, device_id=device(*offsets), device_id_type=MESH)

    barrier = pltpu.get_barrier_semaphore()

    def greet_far():
        signal(barrier, 0, far_step, 0)

    def greet_corner():
        for dx in across:
            signal(barrier, dx, far_step, wrap_step)

    def greet_z(step):
        signal(barrier, 0, 0, step)
        for dx in steps:
            when(jnp.logical_not(wrap[step]), lambda: signal(barrier, dx, 0, step))

    when(both(direct, late & sided_y) | pushed, greet_far)
    when(both(corner, late), greet_corner)
    for step in steps:
        signal(barrier, step, 0, 0)
        when(jnp.logical_not(far[step]), lambda: signal(barrier, 0, step, 0))
    greet_z(-1)
    when(jnp.logical_not(wrap[1] & sided_z), lambda: greet_z(1))
    loads = []
    for i, (src, dst) in enumerate(((pos_in, pos_ref), (q_in, q_ref), (anchor_in, anchor_ref), (atoms_in, atoms_ref), (blocks_in, blocks_ref), (scale_in, scale_ref))):
        loads.append(pltpu.make_async_copy(src, dst, load_sems.at[i]))
        loads[-1].start()
    for load in loads:
        load.wait()
    for a in range(3):
        for b in range(BLOCKS):
            atoms_out[0, pl.ds(a * BLOCKS + b, 1), :] = pos_ref[pl.ds(a, 1), pl.ds(b * LANES, LANES)]
    row = lax.broadcasted_iota(jnp.int32, (BLOCKS, LANES), 0)
    lane = lax.broadcasted_iota(jnp.int32, (BLOCKS, LANES), 1)
    filled = jnp.zeros((BLOCKS, LANES), jnp.int32)
    for b in range(BLOCKS):
        filled = jnp.where(row == b, jnp.where(b < blocks_ref[0], atoms_ref[b], 0), filled)
    atoms_out[0, pl.ds(3 * BLOCKS, BLOCKS), :] = jnp.where(lane < filled, q_ref[...], 0.0)
    meta = jnp.zeros((BLOCKS, LANES), jnp.int32)
    for a in range(3):
        for b in range(BLOCKS):
            meta = jnp.where(lane == a * BLOCKS + b, anchor_ref[a, b], meta)
    for b in range(BLOCKS):
        meta = jnp.where(lane == 3 * BLOCKS + b, jnp.where(b < blocks_ref[0], 1, 0), meta)
    atoms_out[0, pl.ds(32, 1), :] = meta[:1].astype(jnp.float32)
    peers = 10 - jnp.where(hold, 3, jnp.where(ends, 2, 0)) - jnp.where(both(corner, pushes) | both(direct & sided_y, late), 1, 0) + jnp.where(corner & late, 3, 0)
    pl.semaphore_wait(barrier, peers)

    def answer_corner():
        for dx in across:
            signal(ready_c, dx, far_step, wrap_step)

    when(direct & late & sided_y, lambda: signal(ready_y, 0, far_step, 0))
    when(wrap[1] & sided_z, lambda: signal(ready_z, 0, 0, 1))
    when(corner & late, answer_corner)

    def slot(cx, cz, cy):
        return (cx * 3 + cz) * 3 + cy

    def piece(src, dst, target, index):
        return pltpu.make_async_remote_copy(
            src_ref=atoms_out.at[src], dst_ref=atoms_out.at[dst],
            send_sem=send_sems.at[index], recv_sem=recv_sems.at[dst],
            device_id=target, device_id_type=MESH)

    def along_y(step):
        dst = slot(0, 0, code[step])
        return [piece(0, dst, device(0, step, 0), dst)]

    def along_x(cy):
        return [piece(cy, slot(code[dx], 0, cy), device(dx, 0, 0), slot(code[dx], 0, cy)) for dx in steps]

    def fan(cy, step):
        places = [(dx, slot(code[dx] if dx else 0, code[step], cy)) for dx in across]
        return [piece(cy, dst, device(dx, 0, step), dst) for dx, dst in places]

    def corners():
        out = []
        for i, dx in enumerate(across):
            dst = slot(code[dx] if dx else 0, jnp.where(wrap[1], 1, 2), jnp.where(far[1], 1, 2))
            out.append(piece(0, dst, device(dx, far_step, wrap_step), 27 + i))
        return out

    def start(copies):
        for copy in copies:
            copy.start()

    def finish(copies):
        for copy in copies:
            copy.wait_send()

    from_far = {1: far[-1], 2: far[1]}

    def send_early(cy):
        start(along_x(cy))
        start(fan(cy, 1)[:1])
        when(jnp.logical_not(hold), lambda: start(fan(cy, -1)[:1]))
        for step in steps:
            when(jnp.logical_not(wrap[step]), lambda: start(fan(cy, step)[1:]))

    def pass_near(cy):
        along_y(1 if cy == 1 else -1)[0].wait_recv()
        send_early(cy)

    def pass_far(cy):
        along_y(1 if cy == 1 else -1)[0].wait_recv()
        start(along_x(cy))
        for step in steps:
            when(jnp.logical_not(wrap[step]), lambda: start(fan(cy, step)))

    def open_wrap():
        pl.semaphore_wait(ready_z, 1)
        start(fan(0, -1)[:1])
        for cy in (1, 2):
            when(jnp.logical_not(from_far[cy]), lambda: start(fan(cy, -1)[:1]))

    def onward(cy, step):
        src = slot(0, code[step], cy)
        return [piece(src, slot(code[dx], code[step], cy), device(dx, 0, 0), 31 + cy * 2 + i) for i, dx in enumerate(steps)]

    def pass_wrap(cy, step):
        fan(cy, step)[0].wait_recv()
        start(onward(cy, step))

    def open_corner():
        pl.semaphore_wait(ready_c, 3)
        start(corners())

    def handed():
        corner_slot = slot(0, jnp.where(wrap[1], 2, 1), jnp.where(far[1], 2, 1))
        own_slot = slot(0, 0, jnp.where(far[1], 2, 1))
        return piece(corner_slot, own_slot, device(0, 0, wrap_step), 30)

    def forward_corner():
        corner_slot = slot(0, jnp.where(wrap[1], 2, 1), jnp.where(far[1], 2, 1))
        piece(corner_slot, corner_slot, device(0, 0, wrap_step), 30).wait_recv()
        when(hands, handed().start)

    def open_far():
        pl.semaphore_wait(ready_y, 1)
        for step in steps:
            when(far[step], lambda: start(along_y(step)))

    for step in steps:
        when(jnp.logical_not(far[step] & (ends | both(sided_y, late))) | (far[step] & pushes), lambda: start(along_y(step)))
    when(corner & late, lambda: start(corners()))
    send_early(0)
    for cy in (1, 2):
        when(jnp.logical_not(from_far[cy]), lambda: pass_near(cy))
    scales = [jnp.full((1, LANES), scale_ref[a], jnp.float32) for a in range(3)]
    weigh_own(scales, atoms_out, anchor_ref, pad_x, pad_y, pad_z, wx_near, wy_near, wz_near, rights)
    store_rights = pltpu.make_async_copy(rights, right_out, load_sems.at[6])
    store_rights.start()
    spread_near(wx_near, wy_near, wz_near, near_sum)
    store_near = pltpu.make_async_copy(near_sum, near_out, load_sems.at[7])
    store_near.start()
    when(hold, open_wrap)
    when(both(corner, late), open_corner)
    when(corner, forward_corner)
    for step in steps:
        when(wrap[-step], lambda: pass_wrap(0, step))
        for cy in (1, 2):
            when(both(wrap[-step], from_far[cy]), lambda: pass_wrap(cy, step))
    when(both(direct & sided_y, late), open_far)
    for cy in (1, 2):
        when(from_far[cy], lambda: pass_far(cy))
    for cy in range(3):
        for copy in along_x(cy):
            copy.wait_recv()
        for step in steps:
            copies = fan(cy, step)
            when(jnp.logical_not(wrap[-step]), copies[0].wait_recv)
            for copy in copies[1:]:
                copy.wait_recv()
    for step in steps:
        when(jnp.logical_not(far[step] & ends) | (far[step] & pushes), lambda: finish(along_y(step)))
    for cy in range(3):
        finish(along_x(cy))
        for step in steps:
            when(jnp.logical_not(wrap[step]), lambda: finish(fan(cy, step)[1:]))
            if cy == 0:
                finish(fan(cy, step)[:1])
                when(wrap[-step], lambda: finish(onward(cy, step)))
            else:
                when(jnp.logical_not(from_far[cy] & wrap[step]), lambda: finish(fan(cy, step)[:1]))
                when(both(wrap[-step], from_far[cy]), lambda: finish(onward(cy, step)))
    when(corner, lambda: finish(corners()))
    when(hands, lambda: finish([handed()]))
    for a in range(3):
        atoms_out[SOURCES, pl.ds(a, 1), :] = jnp.full((1, LANES), scale_ref[a], jnp.float32)
    store_rights.wait()
    store_near.wait()
    rows_ref[...] = jnp.zeros_like(rows_ref)
    for n in range(SOURCES):
        rows_ref[pl.ds(n, 1), :] = atoms_out[n, pl.ds(32, 1), :]
    value = rows_ref[...].astype(jnp.int32)
    source = lax.broadcasted_iota(jnp.int32, value.shape, 0)
    place = lax.broadcasted_iota(jnp.int32, value.shape, 1)
    one = jnp.ones_like(value)
    zero = jnp.zeros_like(value)
    cx = jnp.where(source >= 9, one, zero) + jnp.where(source >= 18, one, zero)
    rest = source - 9 * cx
    cz = jnp.where(rest >= 3, one, zero) + jnp.where(rest >= 6, one, zero)
    cy = rest - 3 * cz
    is_z = (place >= 2 * BLOCKS) & (place < 3 * BLOCKS)
    is_live = place >= 3 * BLOCKS
    kind = jnp.where(place < BLOCKS, cx, jnp.where(place < 2 * BLOCKS, cy, cz))
    period = jnp.where(is_z, CZ, CX)
    low = jnp.where(is_live, 1, jnp.where(kind == 1, jnp.where(is_z, CZ - 19, 5), 0))
    high = jnp.where(jnp.logical_not(is_live) & (kind == 2), 11, 999)
    fits = jnp.where((value >= low) & (value <= high), one, zero)
    used = fits
    for group in (1, 2, 3):
        used = used * pltpu.roll(fits, LANES - group * BLOCKS, 1)
    used = pltpu.roll(used, 4 * BLOCKS, 1)
    shifted = value + jnp.where(is_live | (kind == 0), 0, jnp.where(kind == 1, -period, period))
    meta_out[...] = jnp.where(place >= 4 * BLOCKS, used, shifted)


def weigh_own(scales, atoms, anchor, pad_x, pad_y, pad_z, wx_near, wy_near, wz_near, rights):
    f32 = jnp.float32
    widths = [SPREAD * s for s in scales]
    taps = kernel_taps(scales)
    iota16 = lax.broadcasted_iota(jnp.int32, (PATCH, LANES), 0)
    iota_z = lax.broadcasted_iota(jnp.int32, (CZ, LANES), 0)
    iota8 = lax.broadcasted_iota(jnp.int32, (8, LANES), 0)
    edge_z = jnp.where(iota8 < 4, iota8 - 4, iota8 + (CZ - 4))
    for ref in (pad_x, pad_y, pad_z):
        ref[...] = jnp.zeros_like(ref)

    def weigh(b, carry):
        x = atoms[0, pl.ds(b, 1), :] * scales[0]
        y = atoms[0, pl.ds(b + BLOCKS, 1), :] * scales[1]
        z = atoms[0, pl.ds(b + 2 * BLOCKS, 1), :] * scales[2]
        q = atoms[0, pl.ds(b + 3 * BLOCKS, 1), :]
        pad_x[b, pl.ds(PAD, PATCH), :] = q * window(x, iota16, widths[0])[0]
        pad_y[b, pl.ds(PAD, PATCH), :] = window(y, iota16, widths[1])[0]
        pad_z[b, pl.ds(LENGTH, PATCH), :] = window(z, iota16, widths[2])[0]
        for a, pad, out in ((0, pad_x, wx_near), (1, pad_y, wy_near)):
            start = PAD - anchor[a, b]
            total = taps[a][0] * pad[b, pl.ds(start, SPAN), :]
            for e in range(1, RADIUS + 1):
                total = total + taps[a][e] * (pad[b, pl.ds(start - e, SPAN), :] + pad[b, pl.ds(start + e, SPAN), :])
            out[b] = total
        high, low = split(pad_z[b, pl.ds(LENGTH - 4 - anchor[2, b], LENGTH), :])
        wz_near[b, pl.ds(0, LENGTH), :] = high
        wz_near[b, pl.ds(LENGTH, LENGTH), :] = low
        wz, sz = window(z, iota_z - anchor[2, b] + RIM, widths[2])
        we, se = window(z, edge_z - anchor[2, b] + RIM, widths[2])
        main_high, main_low = split(jnp.concatenate([wz, sz], axis=1))
        rim = jnp.concatenate([we, se], axis=1)
        rim_high = rim.astype(jnp.bfloat16).astype(f32)
        rim = jnp.concatenate([rim_high, rim_high, rim - rim_high, jnp.zeros((LANES - 24, 256), f32)], axis=0)
        for i, part in enumerate((main_high, main_high, main_low, rim.astype(jnp.bfloat16))):
            rights[b, pl.ds(i * LANES, LANES), :] = part
        return carry

    lax.fori_loop(0, BLOCKS, weigh, jnp.int32(0))


def spread_near(wx_near, wy_near, wz_near, near_sum):
    def spread(quarter, carry):
        half = quarter // 2
        side = quarter % 2
        left, right = [], []
        for k in range(BLOCKS):
            wx = wx_near[k, pl.ds(pl.multiple_of(half * 16, 16), 16), :]
            wy = wy_near[k, pl.ds(pl.multiple_of(side * 16, 16), 16), :]
            right += split((wx[:, None, :] * wy[None, :, :]).reshape(256, LANES))
            left += [wz_near[k]] * 2
        patch = lax.dot_general(
            jnp.concatenate(left, axis=1), jnp.concatenate(right, axis=1),
            (((1,), (1,)), ((), ())), preferred_element_type=jnp.float32)
        near_sum[quarter] = patch[:LENGTH] + patch[LENGTH:]
        return carry

    lax.fori_loop(0, 4, spread, jnp.int32(0))


def exchange(positions, charges, block_anchor, block_atoms, brick_blocks, box_scale):
    anywhere = pl.BlockSpec(memory_space=pl.ANY)
    vmem = pl.BlockSpec(memory_space=pltpu.VMEM)
    f32, i32 = jnp.float32, jnp.int32
    return pl.pallas_call(
        exchange_kernel,
        out_shape=(pltpu.VMEM((SOURCES + 1, ROWS, LANES), f32), pltpu.VMEM((32, LANES), i32),
                   pltpu.VMEM((4, LENGTH, 256), f32),
                   pltpu.VMEM((BLOCKS, 4 * LANES, 256), jnp.bfloat16)),
        in_specs=[anywhere] * 6,
        out_specs=(vmem, vmem, anywhere, anywhere),
        scratch_shapes=[
            pltpu.VMEM((3, BLOCKS * LANES), f32),
            pltpu.VMEM((BLOCKS, LANES), f32),
            pltpu.SMEM((3, BLOCKS), i32),
            pltpu.SMEM((BLOCKS,), i32),
            pltpu.SMEM((1,), i32),
            pltpu.SMEM((3,), f32),
            pltpu.VMEM((32, LANES), f32),
            pltpu.VMEM((BLOCKS, 96, LANES), f32),
            pltpu.VMEM((BLOCKS, 96, LANES), f32),
            pltpu.VMEM((BLOCKS, 2 * LENGTH + PATCH, LANES), f32),
            pltpu.VMEM((BLOCKS, SPAN, LANES), f32),
            pltpu.VMEM((BLOCKS, SPAN, LANES), f32),
            pltpu.VMEM((BLOCKS, 2 * LENGTH, LANES), jnp.bfloat16),
            pltpu.VMEM((4, LENGTH, 256), f32),
            pltpu.VMEM((BLOCKS, 4 * LANES, 256), jnp.bfloat16),
            pltpu.SemaphoreType.DMA((8,)),
            pltpu.SemaphoreType.DMA((40,)),
            pltpu.SemaphoreType.DMA((SOURCES,)),
            pltpu.SemaphoreType.REGULAR((3,)),
        ],
        compiler_params=pltpu.CompilerParams(collective_id=0, has_side_effects=True, vmem_limit_bytes=60 * 1024 * 1024),
        name="exchange_atoms",
    )(positions, charges.reshape(BLOCKS, LANES), block_anchor, block_atoms, brick_blocks, box_scale)


def per_device(positions, charges, block_anchor, block_atoms, brick_blocks, box_scale):
    atoms, meta, near, rights = exchange(positions, charges, block_anchor, block_atoms, brick_blocks, box_scale)
    potential, forces = make_field(atoms, meta, near, rights)
    return (potential, forces)


def solution(mesh):
    split_all = ("gx", "gy", "gz")
    return jax.shard_map(
        per_device,
        mesh=mesh,
        in_specs=(P(None, split_all), P(split_all), P(None, split_all), P(split_all), P(split_all), P()),
        out_specs=(P("gx", "gy", "gz"), P(None, split_all)),
        check_vma=False,
    )
```

```python
import math
import jax, jax.numpy as jnp
from jax import lax
from jax.experimental import pallas as pl
from jax.experimental.pallas import tpu as pltpu

from jax.sharding import PartitionSpec as P

MESH = pl.DeviceIdType.MESH
CX = 24
CY = 24
CZ = 128
PATCH = 16
RIM = 4
RADIUS = 4
SPREAD = 1.0
SMOOTH = 1.5
COUPLING = 200.0
ROWS = 33
ONE_SIDED = 3
BLOCKS = 8
LANES = 128
SOURCES = 27
SLOTS = SOURCES * BLOCKS
SPAN = 32
Z_ROWS = 176
WAYS = 16
EMPTY = SLOTS + WAYS
PAD = 40
LENGTH = CZ + 2 * (RIM + RADIUS)


def norm(width):
    return 1.0 / (math.sqrt(2.0 * math.pi) * width)


def window(coord, place, width):
    offset = coord + RIM - place.astype(jnp.float32)
    inside = (place >= 0) & (place < PATCH)
    weight = jnp.exp(-offset * offset / (2.0 * width * width)) * norm(width)
    weight = jnp.where(inside, weight, 0.0)
    return weight, -offset / (width * width) * weight


def split(value):
    high = value.astype(jnp.bfloat16)
    return high, (value - high.astype(jnp.float32)).astype(jnp.bfloat16)


def kernel_taps(scales):
    taps = []
    for scale in scales:
        tau = SMOOTH * scale
        taps.append([jnp.exp(-float(e * e) / (2.0 * tau * tau)) * norm(tau) for e in range(RADIUS + 1)])
    return taps


def field_kernel(meta_in, atoms, near_in, rights, potential, forces, meta, load_sems, order, tasks, starts, pad_x, pad_y, pad_z, wx_all, wy_all, wz_all, density, field):
    f32 = jnp.float32
    load_meta = pltpu.make_async_copy(meta_in, meta, load_sems.at[0])
    load_meta.start()
    load_near = []
    for quarter in range(4):
        load_near.append(pltpu.make_async_copy(near_in.at[quarter], density.at[pl.ds(quarter * Z_ROWS + 16, LENGTH)], load_sems.at[1 + quarter]))
        load_near[-1].start()
    for quarter in range(4):
        for first in (0, 16 + LENGTH):
            density[pl.ds(quarter * Z_ROWS + first, 16), :] = jnp.zeros((16, 256), f32)
    for ref in (pad_x, pad_y, pad_z):
        ref[...] = jnp.zeros_like(ref)
    wx_all[pl.ds(EMPTY * SPAN, SPAN), :] = jnp.zeros((SPAN, LANES), f32)
    wy_all[pl.ds(EMPTY * SPAN, SPAN), :] = jnp.zeros((SPAN, LANES), f32)
    wz_all[pl.ds(EMPTY * 24, 24), :] = jnp.zeros((24, LANES), f32)
    starts[EMPTY] = 0
    load_meta.wait()

    def choose(n, count):
        for b in range(BLOCKS):
            order[count] = n * BLOCKS + b
            count = count + meta[n, 4 * BLOCKS + b]
        return count

    blocks = lax.fori_loop(1, SOURCES, choose, jnp.int32(0))
    for extra in range(WAYS - 1):
        order[blocks + extra] = 0
    scales = [atoms[SOURCES, pl.ds(a, 1), :] for a in range(3)]
    widths = [SPREAD * s for s in scales]
    taps = kernel_taps(scales)

    iota16 = lax.broadcasted_iota(jnp.int32, (PATCH, LANES), 0)

    def weigh(group, count):
        for way in range(WAYS):
            k = group * WAYS + way
            code = order[k]
            n = code // BLOCKS
            b = code % BLOCKS
            cx = n // 9
            cy = n % 3
            off_x = meta[n, b]
            off_y = meta[n, BLOCKS + b]
            off_z = meta[n, 2 * BLOCKS + b]
            x = atoms[n, pl.ds(b, 1), :] * scales[0]
            y = atoms[n, pl.ds(b + BLOCKS, 1), :] * scales[1]
            z = atoms[n, pl.ds(b + 2 * BLOCKS, 1), :] * scales[2]
            q = atoms[n, pl.ds(b + 3 * BLOCKS, 1), :]
            pad_x[way, pl.ds(PAD, PATCH), :] = q * window(x, iota16, widths[0])[0]
            pad_y[way, pl.ds(PAD, PATCH), :] = window(y, iota16, widths[1])[0]
            pad_z[way, pl.ds(8, PATCH), :] = window(z, iota16, widths[2])[0]
            for a, off, pad, out in ((0, off_x, pad_x, wx_all), (1, off_y, pad_y, wy_all)):
                start = PAD - off
                total = taps[a][0] * pad[way, pl.ds(start, SPAN), :]
                for e in range(1, RADIUS + 1):
                    total = total + taps[a][e] * (pad[way, pl.ds(start - e, SPAN), :] + pad[way, pl.ds(start + e, SPAN), :])
                out[pl.ds(pl.multiple_of(k * SPAN, SPAN), SPAN), :] = total
            first = off_z + 20
            shift = first & 7
            wz_all[pl.ds(pl.multiple_of(k * 24, 8), 24), :] = pad_z[way, pl.ds(8 - shift, 24), :]
            starts[k] = first - shift
            used = k < blocks
            for half in range(2):
                for side in range(2):
                    touches = used & ((cx == 0) | (cx == half + 1)) & ((cy == 0) | (cy == side + 1))
                    tasks[count] = k * 4 + half * 2 + side
                    count = count + touches.astype(jnp.int32)
        return count

    jobs = lax.fori_loop(0, (blocks + WAYS - 1) // WAYS, weigh, jnp.int32(0))
    for extra in range(WAYS - 1):
        tasks[jobs + extra] = EMPTY * 4

    for load in load_near:
        load.wait()

    def spread(group, carry):
        for way in range(WAYS):
            code = tasks[group * WAYS + way]
            k = code // 4
            half = code // 2 % 2
            side = code % 2
            wx = wx_all[pl.ds(pl.multiple_of(k * SPAN + half * 16, 16), 16), :]
            wy = wy_all[pl.ds(pl.multiple_of(k * SPAN + side * 16, 16), 16), :]
            product = (wx[:, None, :] * wy[None, :, :]).reshape(256, LANES)
            high, low = split(product)
            wz = wz_all[pl.ds(pl.multiple_of(k * 24, 8), 24), :]
            z_high = wz.astype(jnp.bfloat16).astype(f32)
            left = jnp.concatenate([z_high, wz - z_high], axis=0).astype(jnp.bfloat16)
            patch = lax.dot_general(
                jnp.concatenate([left, left], axis=1), jnp.concatenate([high, low], axis=1),
                (((1,), (1,)), ((), ())), preferred_element_type=f32)
            rows = pl.ds(pl.multiple_of((code % 4) * Z_ROWS + starts[k], 8), 24)
            density[rows, :] = density[rows, :] + patch[:24] + patch[24:]
        return carry

    lax.fori_loop(0, (jobs + WAYS - 1) // WAYS, spread, jnp.int32(0))

    length = LENGTH
    gap = lax.broadcasted_iota(jnp.int32, (length, length), 0) - lax.broadcasted_iota(jnp.int32, (length, length), 1)
    gap_f = gap.astype(f32)
    tau_v = jnp.broadcast_to(SMOOTH * scales[2][:, :1], (length, length))
    band = jnp.exp(-gap_f * gap_f / (2.0 * tau_v * tau_v)) * (COUPLING / (math.sqrt(2.0 * math.pi) * tau_v))
    band_high, band_low = split(jnp.where(jnp.abs(gap) <= RADIUS, band, 0.0))
    for half in range(2):
        for side in range(2):
            part = density[pl.ds((half * 2 + side) * Z_ROWS + 16, length), :]
            high, low = split(part)
            smooth = (jnp.dot(band_high, high, preferred_element_type=f32)
                      + jnp.dot(band_high, low, preferred_element_type=f32)
                      + jnp.dot(band_low, high, preferred_element_type=f32))
            turned = smooth[8:8 + CZ].T
            edge = jnp.concatenate([smooth[4:8], smooth[8 + CZ:12 + CZ]], axis=0)
            edge_high = edge.astype(jnp.bfloat16).astype(f32)
            edges = jnp.concatenate([edge_high, edge - edge_high, edge_high, jnp.zeros((LANES - 24, 256), f32)], axis=0).T
            turned_high, turned_low = split(turned)
            cube = turned.reshape(16, 16, CZ)
            low_x, low_y = (1 - half) * RIM, (1 - side) * RIM
            potential[pl.ds(half * 12, 12), pl.ds(side * 12, 12), :] = cube[low_x:low_x + 12, low_y:low_y + 12, :]
            place = (pl.ds(half * 16, 16), pl.ds(side * 16, 16))
            for i, block in enumerate((turned_high, turned_low, turned_high, edges.astype(jnp.bfloat16))):
                field[place[0], place[1], pl.ds(i * LANES, LANES)] = block.reshape(16, 16, LANES)

    iota32 = lax.broadcasted_iota(jnp.int32, (SPAN, LANES), 0)
    def force(b):
        x = atoms[0, pl.ds(b, 1), :] * scales[0]
        y = atoms[0, pl.ds(b + BLOCKS, 1), :] * scales[1]
        q = atoms[0, pl.ds(b + 3 * BLOCKS, 1), :]
        at_x = meta[0, b]
        at_y = meta[0, BLOCKS + b]
        wx, sx = window(x, iota16, widths[0])
        wy, sy = window(y, iota32 - at_y, widths[1])
        left = field[pl.ds(at_x, PATCH)].reshape(PATCH * SPAN, 4 * LANES)
        values = jnp.dot(left, rights[b], preferred_element_type=f32).reshape(PATCH, SPAN, 256)
        by_sx = jnp.zeros((SPAN, LANES), f32)
        by_wx = jnp.zeros((SPAN, LANES), f32)
        by_wz = jnp.zeros((SPAN, LANES), f32)
        for i in range(PATCH):
            level = values[i, :, :LANES]
            by_sx = by_sx + level * sx[i:i + 1]
            by_wx = by_wx + level * wx[i:i + 1]
            by_wz = by_wz + values[i, :, LANES:] * wx[i:i + 1]
        for a, total in enumerate((by_sx * wy, by_wx * sy, by_wz * wy)):
            forces[a:a + 1, b * LANES:(b + 1) * LANES] = -q * scales[a] * jnp.sum(total, axis=0, keepdims=True)

    for b in range(BLOCKS):
        force(b)


def make_field(atoms, meta, near, rights):
    anywhere = pl.BlockSpec(memory_space=pl.ANY)
    vmem = pl.BlockSpec(memory_space=pltpu.VMEM)
    f32, i32 = jnp.float32, jnp.int32
    return pl.pallas_call(
        field_kernel,
        out_shape=(jax.ShapeDtypeStruct((CX, CY, CZ), f32), jax.ShapeDtypeStruct((3, BLOCKS * LANES), f32)),
        in_specs=[anywhere, vmem, anywhere, vmem],
        out_specs=(vmem, vmem),
        scratch_shapes=[
            pltpu.SMEM((32, LANES), i32),
            pltpu.SemaphoreType.DMA((5,)),
            pltpu.SMEM((EMPTY + 1,), i32),
            pltpu.SMEM((SLOTS * 4 + WAYS,), i32),
            pltpu.SMEM((EMPTY + 1,), i32),
            pltpu.VMEM((WAYS, 96, LANES), f32),
            pltpu.VMEM((WAYS, 96, LANES), f32),
            pltpu.VMEM((WAYS, 32, LANES), f32),
            pltpu.VMEM(((EMPTY + 1) * SPAN, LANES), f32),
            pltpu.VMEM(((EMPTY + 1) * SPAN, LANES), f32),
            pltpu.VMEM(((EMPTY + 1) * 24, LANES), f32),
            pltpu.VMEM((4 * Z_ROWS, 256), f32),
            pltpu.VMEM((SPAN, SPAN, 4 * LANES), jnp.bfloat16),
        ],
        compiler_params=pltpu.CompilerParams(vmem_limit_bytes=24 * 1024 * 1024),
        name="field_and_forces",
    )(meta, atoms, near, rights)


def exchange_kernel(pos_in, q_in, anchor_in, atoms_in, blocks_in, scale_in, atoms_out, meta_out, near_out, right_out, pos_ref, q_ref, anchor_ref, atoms_ref, blocks_ref, scale_ref, rows_ref, pad_x, pad_y, pad_z, cell_x, cell_y, wx_near, wy_near, wz_near, near_sum, rights, load_sems, send_sems, recv_sems, ready_sems):
    gx, gy, gz = (lax.axis_index(a) for a in ("gx", "gy", "gz"))
    nx, ny, nz = (lax.axis_size(a) for a in ("gx", "gy", "gz"))
    half = ny // 2

    def device(dx, dy, dz):
        return (lax.rem(gx + dx + nx, nx), lax.rem(gy + dy + ny, ny), lax.rem(gz + dz + nz, nz))

    def both(condition, other):
        return condition & jnp.logical_not(other)

    late = gy >= half
    far = {1: lax.rem(gy, half) == half - 1, -1: lax.rem(gy, half) == 0}
    wrap = {1: gz == nz - 1, -1: gz == 0}
    far_any = far[1] | far[-1]
    sided_y = gz < ONE_SIDED
    sided_z = jnp.logical_not(late & jnp.logical_not(far_any))
    hold = wrap[-1] & sided_z
    ends = wrap[1] | wrap[-1]
    direct = both(far_any, ends)
    corner = far_any & (wrap[1] | wrap[-1])
    pushes = corner & late & wrap[-1]
    pushed = both(corner & wrap[-1], late)
    hands = both(corner, wrap[1] & jnp.logical_not(late))
    far_step = jnp.where(far[1], 1, -1)
    wrap_step = jnp.where(wrap[1], 1, -1)
    steps = (1, -1)
    code = {1: 1, -1: 2}
    across = (0, 1, -1)
    ready_z, ready_y, ready_c = (ready_sems.at[i] for i in range(3))

    def when(condition, action):
        pl.when(condition)(action)

    def signal(semaphore, *offsets):
        pl.semaphore_signal(semaphore, inc=1, device_id=device(*offsets), device_id_type=MESH)

    barrier = pltpu.get_barrier_semaphore()

    def greet_far():
        signal(barrier, 0, far_step, 0)

    def greet_corner():
        for dx in across:
            signal(barrier, dx, far_step, wrap_step)

    def greet_z(step):
        signal(barrier, 0, 0, step)
        for dx in steps:
            when(jnp.logical_not(wrap[step]), lambda: signal(barrier, dx, 0, step))

    when(both(direct, late & sided_y) | pushed, greet_far)
    when(both(corner, late), greet_corner)
    for step in steps:
        signal(barrier, step, 0, 0)
        when(jnp.logical_not(far[step]), lambda: signal(barrier, 0, step, 0))
    greet_z(-1)
    when(jnp.logical_not(wrap[1] & sided_z), lambda: greet_z(1))
    loads = []
    for i, (src, dst) in enumerate(((pos_in, pos_ref), (q_in, q_ref), (anchor_in, anchor_ref), (atoms_in, atoms_ref), (blocks_in, blocks_ref), (scale_in, scale_ref))):
        loads.append(pltpu.make_async_copy(src, dst, load_sems.at[i]))
        loads[-1].start()
    for load in loads:
        load.wait()
    for a in range(3):
        for b in range(BLOCKS):
            atoms_out[0, pl.ds(a * BLOCKS + b, 1), :] = pos_ref[pl.ds(a, 1), pl.ds(b * LANES, LANES)]
    row = lax.broadcasted_iota(jnp.int32, (BLOCKS, LANES), 0)
    lane = lax.broadcasted_iota(jnp.int32, (BLOCKS, LANES), 1)
    filled = jnp.zeros((BLOCKS, LANES), jnp.int32)
    for b in range(BLOCKS):
        filled = jnp.where(row == b, jnp.where(b < blocks_ref[0], atoms_ref[b], 0), filled)
    atoms_out[0, pl.ds(3 * BLOCKS, BLOCKS), :] = jnp.where(lane < filled, q_ref[...], 0.0)
    meta = jnp.zeros((BLOCKS, LANES), jnp.int32)
    for a in range(3):
        for b in range(BLOCKS):
            meta = jnp.where(lane == a * BLOCKS + b, anchor_ref[a, b], meta)
    for b in range(BLOCKS):
        meta = jnp.where(lane == 3 * BLOCKS + b, jnp.where(b < blocks_ref[0], 1, 0), meta)
    atoms_out[0, pl.ds(32, 1), :] = meta[:1].astype(jnp.float32)
    peers = 10 - jnp.where(hold, 3, jnp.where(ends, 2, 0)) - jnp.where(both(corner, pushes) | both(direct & sided_y, late), 1, 0) + jnp.where(corner & late, 3, 0)
    pl.semaphore_wait(barrier, peers)

    def answer_corner():
        for dx in across:
            signal(ready_c, dx, far_step, wrap_step)

    when(direct & late & sided_y, lambda: signal(ready_y, 0, far_step, 0))
    when(wrap[1] & sided_z, lambda: signal(ready_z, 0, 0, 1))
    when(corner & late, answer_corner)

    def slot(cx, cz, cy):
        return (cx * 3 + cz) * 3 + cy

    def piece(src, dst, target, index):
        return pltpu.make_async_remote_copy(
            src_ref=atoms_out.at[src], dst_ref=atoms_out.at[dst],
            send_sem=send_sems.at[index], recv_sem=recv_sems.at[dst],
            device_id=target, device_id_type=MESH)

    def along_y(step):
        dst = slot(0, 0, code[step])
        return [piece(0, dst, device(0, step, 0), dst)]

    def along_x(cy):
        return [piece(cy, slot(code[dx], 0, cy), device(dx, 0, 0), slot(code[dx], 0, cy)) for dx in steps]

    def fan(cy, step):
        places = [(dx, slot(code[dx] if dx else 0, code[step], cy)) for dx in across]
        return [piece(cy, dst, device(dx, 0, step), dst) for dx, dst in places]

    def corners():
        out = []
        for i, dx in enumerate(across):
            dst = slot(code[dx] if dx else 0, jnp.where(wrap[1], 1, 2), jnp.where(far[1], 1, 2))
            out.append(piece(0, dst, device(dx, far_step, wrap_step), 27 + i))
        return out

    def start(copies):
        for copy in copies:
            copy.start()

    def finish(copies):
        for copy in copies:
            copy.wait_send()

    from_far = {1: far[-1], 2: far[1]}

    def send_early(cy):
        start(along_x(cy))
        start(fan(cy, 1)[:1])
        when(jnp.logical_not(hold), lambda: start(fan(cy, -1)[:1]))
        for step in steps:
            when(jnp.logical_not(wrap[step]), lambda: start(fan(cy, step)[1:]))

    def pass_near(cy):
        along_y(1 if cy == 1 else -1)[0].wait_recv()
        send_early(cy)

    def pass_far(cy):
        along_y(1 if cy == 1 else -1)[0].wait_recv()
        start(along_x(cy))
        for step in steps:
            when(jnp.logical_not(wrap[step]), lambda: start(fan(cy, step)))

    def open_wrap():
        pl.semaphore_wait(ready_z, 1)
        start(fan(0, -1)[:1])
        for cy in (1, 2):
            when(jnp.logical_not(from_far[cy]), lambda: start(fan(cy, -1)[:1]))

    def onward(cy, step):
        src = slot(0, code[step], cy)
        return [piece(src, slot(code[dx], code[step], cy), device(dx, 0, 0), 31 + cy * 2 + i) for i, dx in enumerate(steps)]

    def pass_wrap(cy, step):
        fan(cy, step)[0].wait_recv()
        start(onward(cy, step))

    def open_corner():
        pl.semaphore_wait(ready_c, 3)
        start(corners())

    def handed():
        corner_slot = slot(0, jnp.where(wrap[1], 2, 1), jnp.where(far[1], 2, 1))
        own_slot = slot(0, 0, jnp.where(far[1], 2, 1))
        return piece(corner_slot, own_slot, device(0, 0, wrap_step), 30)

    def forward_corner():
        corner_slot = slot(0, jnp.where(wrap[1], 2, 1), jnp.where(far[1], 2, 1))
        piece(corner_slot, corner_slot, device(0, 0, wrap_step), 30).wait_recv()
        when(hands, handed().start)

    def open_far():
        pl.semaphore_wait(ready_y, 1)
        for step in steps:
            when(far[step], lambda: start(along_y(step)))

    for step in steps:
        when(jnp.logical_not(far[step] & (ends | both(sided_y, late))) | (far[step] & pushes), lambda: start(along_y(step)))
    when(corner & late, lambda: start(corners()))
    send_early(0)
    for cy in (1, 2):
        when(jnp.logical_not(from_far[cy]), lambda: pass_near(cy))
    scales = [jnp.full((1, LANES), scale_ref[a], jnp.float32) for a in range(3)]
    weigh_own(scales, atoms_out, anchor_ref, pad_x, pad_y, pad_z, wx_near, wy_near, wz_near, rights)
    store_rights = pltpu.make_async_copy(rights, right_out, load_sems.at[6])
    store_rights.start()
    beside = both(far_any & sided_y, late)

    def spread_beside():
        for copy in along_x(0):
            copy.wait_recv()
        weigh_beside(scales, atoms_out, cell_x, cell_y, wx_near, wy_near, wz_near)
        spread_near(2 * BLOCKS, wx_near, wy_near, wz_near, near_sum)

    when(beside, spread_beside)
    when(jnp.logical_not(beside), lambda: spread_near(BLOCKS, wx_near, wy_near, wz_near, near_sum))
    store_near = pltpu.make_async_copy(near_sum, near_out, load_sems.at[7])
    store_near.start()
    when(hold, open_wrap)
    when(both(corner, late), open_corner)
    when(corner, forward_corner)
    for step in steps:
        when(wrap[-step], lambda: pass_wrap(0, step))
        for cy in (1, 2):
            when(both(wrap[-step], from_far[cy]), lambda: pass_wrap(cy, step))
    when(both(direct & sided_y, late), open_far)
    for cy in (1, 2):
        when(from_far[cy], lambda: pass_far(cy))
    for cy in range(3):
        for copy in along_x(cy):
            if cy:
                copy.wait_recv()
            else:
                when(jnp.logical_not(beside), copy.wait_recv)
        for step in steps:
            copies = fan(cy, step)
            when(jnp.logical_not(wrap[-step]), copies[0].wait_recv)
            for copy in copies[1:]:
                copy.wait_recv()
    for step in steps:
        when(jnp.logical_not(far[step] & ends) | (far[step] & pushes), lambda: finish(along_y(step)))
    for cy in range(3):
        finish(along_x(cy))
        for step in steps:
            when(jnp.logical_not(wrap[step]), lambda: finish(fan(cy, step)[1:]))
            if cy == 0:
                finish(fan(cy, step)[:1])
                when(wrap[-step], lambda: finish(onward(cy, step)))
            else:
                when(jnp.logical_not(from_far[cy] & wrap[step]), lambda: finish(fan(cy, step)[:1]))
                when(both(wrap[-step], from_far[cy]), lambda: finish(onward(cy, step)))
    when(corner, lambda: finish(corners()))
    when(hands, lambda: finish([handed()]))
    for a in range(3):
        atoms_out[SOURCES, pl.ds(a, 1), :] = jnp.full((1, LANES), scale_ref[a], jnp.float32)
    store_rights.wait()
    store_near.wait()
    rows_ref[...] = jnp.zeros_like(rows_ref)
    for n in range(SOURCES):
        rows_ref[pl.ds(n, 1), :] = atoms_out[n, pl.ds(32, 1), :]
    value = rows_ref[...].astype(jnp.int32)
    source = lax.broadcasted_iota(jnp.int32, value.shape, 0)
    place = lax.broadcasted_iota(jnp.int32, value.shape, 1)
    one = jnp.ones_like(value)
    zero = jnp.zeros_like(value)
    cx = jnp.where(source >= 9, one, zero) + jnp.where(source >= 18, one, zero)
    rest = source - 9 * cx
    cz = jnp.where(rest >= 3, one, zero) + jnp.where(rest >= 6, one, zero)
    cy = rest - 3 * cz
    is_z = (place >= 2 * BLOCKS) & (place < 3 * BLOCKS)
    is_live = place >= 3 * BLOCKS
    kind = jnp.where(place < BLOCKS, cx, jnp.where(place < 2 * BLOCKS, cy, cz))
    period = jnp.where(is_z, CZ, CX)
    low = jnp.where(is_live, 1, jnp.where(kind == 1, jnp.where(is_z, CZ - 19, 5), 0))
    high = jnp.where(jnp.logical_not(is_live) & (kind == 2), 11, 999)
    fits = jnp.where((value >= low) & (value <= high), one, zero)
    used = fits
    for group in (1, 2, 3):
        used = used * pltpu.roll(fits, LANES - group * BLOCKS, 1)
    used = pltpu.roll(used, 4 * BLOCKS, 1) * jnp.where(rest == 0, 1 - beside.astype(jnp.int32), one)
    shifted = value + jnp.where(is_live | (kind == 0), 0, jnp.where(kind == 1, -period, period))
    meta_out[...] = jnp.where(place >= 4 * BLOCKS, used, shifted)


def weigh_own(scales, atoms, anchor, pad_x, pad_y, pad_z, wx_near, wy_near, wz_near, rights):
    f32 = jnp.float32
    widths = [SPREAD * s for s in scales]
    taps = kernel_taps(scales)
    iota16 = lax.broadcasted_iota(jnp.int32, (PATCH, LANES), 0)
    iota_z = lax.broadcasted_iota(jnp.int32, (CZ, LANES), 0)
    iota8 = lax.broadcasted_iota(jnp.int32, (8, LANES), 0)
    edge_z = jnp.where(iota8 < 4, iota8 - 4, iota8 + (CZ - 4))
    for ref in (pad_x, pad_y, pad_z):
        ref[...] = jnp.zeros_like(ref)

    def weigh(b, carry):
        x = atoms[0, pl.ds(b, 1), :] * scales[0]
        y = atoms[0, pl.ds(b + BLOCKS, 1), :] * scales[1]
        z = atoms[0, pl.ds(b + 2 * BLOCKS, 1), :] * scales[2]
        q = atoms[0, pl.ds(b + 3 * BLOCKS, 1), :]
        pad_x[b, pl.ds(PAD, PATCH), :] = q * window(x, iota16, widths[0])[0]
        pad_y[b, pl.ds(PAD, PATCH), :] = window(y, iota16, widths[1])[0]
        pad_z[b, pl.ds(LENGTH, PATCH), :] = window(z, iota16, widths[2])[0]
        for a, pad, out in ((0, pad_x, wx_near), (1, pad_y, wy_near)):
            start = PAD - anchor[a, b]
            total = taps[a][0] * pad[b, pl.ds(start, SPAN), :]
            for e in range(1, RADIUS + 1):
                total = total + taps[a][e] * (pad[b, pl.ds(start - e, SPAN), :] + pad[b, pl.ds(start + e, SPAN), :])
            out[b] = total
        high, low = split(pad_z[b, pl.ds(LENGTH - 4 - anchor[2, b], LENGTH), :])
        wz_near[b, pl.ds(0, LENGTH), :] = high
        wz_near[b, pl.ds(LENGTH, LENGTH), :] = low
        wz, sz = window(z, iota_z - anchor[2, b] + RIM, widths[2])
        we, se = window(z, edge_z - anchor[2, b] + RIM, widths[2])
        main_high, main_low = split(jnp.concatenate([wz, sz], axis=1))
        rim = jnp.concatenate([we, se], axis=1)
        rim_high = rim.astype(jnp.bfloat16).astype(f32)
        rim = jnp.concatenate([rim_high, rim_high, rim - rim_high, jnp.zeros((LANES - 24, 256), f32)], axis=0)
        for i, part in enumerate((main_high, main_high, main_low, rim.astype(jnp.bfloat16))):
            rights[b, pl.ds(i * LANES, LANES), :] = part
        return carry

    lax.fori_loop(0, BLOCKS, weigh, jnp.int32(0))


def weigh_beside(scales, atoms, cell_x, cell_y, wx_near, wy_near, wz_near):
    i32 = jnp.int32
    widths = [SPREAD * s for s in scales]
    taps = kernel_taps(scales)
    iota_x = lax.broadcasted_iota(i32, (24, LANES), 0)
    iota_y = lax.broadcasted_iota(i32, (40, LANES), 0)
    iota_z = lax.broadcasted_iota(i32, (LENGTH, LANES), 0)
    lane = lax.broadcasted_iota(i32, (1, LANES), 1)

    def weigh(b, carry):
        for half in range(2):
            n = 9 * (1 + half)
            k = BLOCKS * (1 + half) + b
            x = atoms[n, pl.ds(b, 1), :] * scales[0]
            y = atoms[n, pl.ds(b + BLOCKS, 1), :] * scales[1]
            z = atoms[n, pl.ds(b + 2 * BLOCKS, 1), :] * scales[2]
            q = atoms[n, pl.ds(b + 3 * BLOCKS, 1), :]
            row = atoms[n, pl.ds(32, 1), :]
            at = [jnp.sum(jnp.where(lane == a * BLOCKS + b, row, 0.0), axis=1, keepdims=True) for a in range(3)]
            at_x, at_y, at_z = [jnp.broadcast_to(v, (1, LANES)).astype(i32) for v in at]
            at_x = at_x + (CX if half else -CX)
            cell_x[half] = q * window(x, iota_x + (half * 16 - 4) - at_x, widths[0])[0]
            cell_y[half] = window(y, iota_y - 4 - at_y, widths[1])[0]
            for a, cell, out, count, first in ((0, cell_x, wx_near, 16, half * 16), (1, cell_y, wy_near, SPAN, 0)):
                total = taps[a][0] * cell[half, pl.ds(4, count), :]
                for e in range(1, RADIUS + 1):
                    total = total + taps[a][e] * (cell[half, pl.ds(4 - e, count), :] + cell[half, pl.ds(4 + e, count), :])
                out[k, pl.ds(first, count), :] = total
            high, low = split(window(z, iota_z - 4 - at_z, widths[2])[0])
            wz_near[k, pl.ds(0, LENGTH), :] = high
            wz_near[k, pl.ds(LENGTH, LENGTH), :] = low
        return carry

    lax.fori_loop(0, BLOCKS, weigh, jnp.int32(0))


def spread_near(count, wx_near, wy_near, wz_near, near_sum):
    def spread(quarter, carry):
        half = quarter // 2
        side = quarter % 2
        left, right = [], []
        for b in range(count):
            k = b if b < BLOCKS else b + BLOCKS * half
            wx = wx_near[k, pl.ds(pl.multiple_of(half * 16, 16), 16), :]
            wy = wy_near[k, pl.ds(pl.multiple_of(side * 16, 16), 16), :]
            right += split((wx[:, None, :] * wy[None, :, :]).reshape(256, LANES))
            left += [wz_near[k]] * 2
        patch = lax.dot_general(
            jnp.concatenate(left, axis=1), jnp.concatenate(right, axis=1),
            (((1,), (1,)), ((), ())), preferred_element_type=jnp.float32)
        near_sum[quarter] = patch[:LENGTH] + patch[LENGTH:]
        return carry

    lax.fori_loop(0, 4, spread, jnp.int32(0))


def exchange(positions, charges, block_anchor, block_atoms, brick_blocks, box_scale):
    anywhere = pl.BlockSpec(memory_space=pl.ANY)
    vmem = pl.BlockSpec(memory_space=pltpu.VMEM)
    f32, i32 = jnp.float32, jnp.int32
    return pl.pallas_call(
        exchange_kernel,
        out_shape=(pltpu.VMEM((SOURCES + 1, ROWS, LANES), f32), pltpu.VMEM((32, LANES), i32),
                   pltpu.VMEM((4, LENGTH, 256), f32),
                   pltpu.VMEM((BLOCKS, 4 * LANES, 256), jnp.bfloat16)),
        in_specs=[anywhere] * 6,
        out_specs=(vmem, vmem, anywhere, anywhere),
        scratch_shapes=[
            pltpu.VMEM((3, BLOCKS * LANES), f32),
            pltpu.VMEM((BLOCKS, LANES), f32),
            pltpu.SMEM((3, BLOCKS), i32),
            pltpu.SMEM((BLOCKS,), i32),
            pltpu.SMEM((1,), i32),
            pltpu.SMEM((3,), f32),
            pltpu.VMEM((32, LANES), f32),
            pltpu.VMEM((BLOCKS, 96, LANES), f32),
            pltpu.VMEM((BLOCKS, 96, LANES), f32),
            pltpu.VMEM((BLOCKS, 2 * LENGTH + PATCH, LANES), f32),
            pltpu.VMEM((2, 24, LANES), f32),
            pltpu.VMEM((2, 40, LANES), f32),
            pltpu.VMEM((3 * BLOCKS, SPAN, LANES), f32),
            pltpu.VMEM((3 * BLOCKS, SPAN, LANES), f32),
            pltpu.VMEM((3 * BLOCKS, 2 * LENGTH, LANES), jnp.bfloat16),
            pltpu.VMEM((4, LENGTH, 256), f32),
            pltpu.VMEM((BLOCKS, 4 * LANES, 256), jnp.bfloat16),
            pltpu.SemaphoreType.DMA((8,)),
            pltpu.SemaphoreType.DMA((40,)),
            pltpu.SemaphoreType.DMA((SOURCES,)),
            pltpu.SemaphoreType.REGULAR((3,)),
        ],
        compiler_params=pltpu.CompilerParams(collective_id=0, has_side_effects=True, vmem_limit_bytes=60 * 1024 * 1024),
        name="exchange_atoms",
    )(positions, charges.reshape(BLOCKS, LANES), block_anchor, block_atoms, brick_blocks, box_scale)


def per_device(positions, charges, block_anchor, block_atoms, brick_blocks, box_scale):
    atoms, meta, near, rights = exchange(positions, charges, block_anchor, block_atoms, brick_blocks, box_scale)
    potential, forces = make_field(atoms, meta, near, rights)
    return (potential, forces)


def solution(mesh):
    split_all = ("gx", "gy", "gz")
    return jax.shard_map(
        per_device,
        mesh=mesh,
        in_specs=(P(None, split_all), P(split_all), P(None, split_all), P(split_all), P(split_all), P()),
        out_specs=(P("gx", "gy", "gz"), P(None, split_all)),
        check_vma=False,
    )
```

```python
import math
import jax, jax.numpy as jnp
from jax import lax
from jax.experimental import pallas as pl
from jax.experimental.pallas import tpu as pltpu

from jax.sharding import PartitionSpec as P

MESH = pl.DeviceIdType.MESH
CX = 24
CY = 24
CZ = 128
PATCH = 16
RIM = 4
RADIUS = 4
SPREAD = 1.0
SMOOTH = 1.5
COUPLING = 200.0
ROWS = 33
ONE_SIDED = 3
BLOCKS = 8
LANES = 128
SOURCES = 27
SLOTS = SOURCES * BLOCKS
SPAN = 32
Z_ROWS = 176
WAYS = 16
EMPTY = SLOTS + WAYS
PAD = 40
LENGTH = CZ + 2 * (RIM + RADIUS)


def norm(width):
    return 1.0 / (math.sqrt(2.0 * math.pi) * width)


def window(coord, place, width):
    offset = coord + RIM - place.astype(jnp.float32)
    inside = (place >= 0) & (place < PATCH)
    weight = jnp.exp(-offset * offset / (2.0 * width * width)) * norm(width)
    weight = jnp.where(inside, weight, 0.0)
    return weight, -offset / (width * width) * weight


def split(value):
    high = value.astype(jnp.bfloat16)
    return high, (value - high.astype(jnp.float32)).astype(jnp.bfloat16)


def kernel_taps(scales):
    taps = []
    for scale in scales:
        tau = SMOOTH * scale
        taps.append([jnp.exp(-float(e * e) / (2.0 * tau * tau)) * norm(tau) for e in range(RADIUS + 1)])
    return taps


def field_kernel(meta_in, atoms, near_in, rights, potential, forces, meta, load_sems, order, tasks, starts, pad_x, pad_y, pad_z, wx_all, wy_all, wz_all, density, field):
    f32 = jnp.float32
    load_meta = pltpu.make_async_copy(meta_in, meta, load_sems.at[0])
    load_meta.start()
    load_near = []
    for quarter in range(4):
        load_near.append(pltpu.make_async_copy(near_in.at[quarter], density.at[pl.ds(quarter * Z_ROWS + 16, LENGTH)], load_sems.at[1 + quarter]))
        load_near[-1].start()
    for quarter in range(4):
        for first in (0, 16 + LENGTH):
            density[pl.ds(quarter * Z_ROWS + first, 16), :] = jnp.zeros((16, 256), f32)
    for ref in (pad_x, pad_y, pad_z):
        ref[...] = jnp.zeros_like(ref)
    wx_all[pl.ds(EMPTY * SPAN, SPAN), :] = jnp.zeros((SPAN, LANES), f32)
    wy_all[pl.ds(EMPTY * SPAN, SPAN), :] = jnp.zeros((SPAN, LANES), f32)
    wz_all[pl.ds(EMPTY * 24, 24), :] = jnp.zeros((24, LANES), f32)
    starts[EMPTY] = 0
    load_meta.wait()

    def choose(n, count):
        for b in range(BLOCKS):
            order[count] = n * BLOCKS + b
            count = count + meta[n, 4 * BLOCKS + b]
        return count

    blocks = lax.fori_loop(1, SOURCES, choose, jnp.int32(0))
    for extra in range(WAYS - 1):
        order[blocks + extra] = 0
    scales = [atoms[SOURCES, pl.ds(a, 1), :] for a in range(3)]
    widths = [SPREAD * s for s in scales]
    taps = kernel_taps(scales)

    iota16 = lax.broadcasted_iota(jnp.int32, (PATCH, LANES), 0)

    def weigh(group, count):
        for way in range(WAYS):
            k = group * WAYS + way
            code = order[k]
            n = code // BLOCKS
            b = code % BLOCKS
            cx = n // 9
            cy = n % 3
            off_x = meta[n, b]
            off_y = meta[n, BLOCKS + b]
            off_z = meta[n, 2 * BLOCKS + b]
            x = atoms[n, pl.ds(b, 1), :] * scales[0]
            y = atoms[n, pl.ds(b + BLOCKS, 1), :] * scales[1]
            z = atoms[n, pl.ds(b + 2 * BLOCKS, 1), :] * scales[2]
            q = atoms[n, pl.ds(b + 3 * BLOCKS, 1), :]
            pad_x[way, pl.ds(PAD, PATCH), :] = q * window(x, iota16, widths[0])[0]
            pad_y[way, pl.ds(PAD, PATCH), :] = window(y, iota16, widths[1])[0]
            pad_z[way, pl.ds(8, PATCH), :] = window(z, iota16, widths[2])[0]
            for a, off, pad, out in ((0, off_x, pad_x, wx_all), (1, off_y, pad_y, wy_all)):
                start = PAD - off
                total = taps[a][0] * pad[way, pl.ds(start, SPAN), :]
                for e in range(1, RADIUS + 1):
                    total = total + taps[a][e] * (pad[way, pl.ds(start - e, SPAN), :] + pad[way, pl.ds(start + e, SPAN), :])
                out[pl.ds(pl.multiple_of(k * SPAN, SPAN), SPAN), :] = total
            first = off_z + 20
            shift = first & 7
            wz_all[pl.ds(pl.multiple_of(k * 24, 8), 24), :] = pad_z[way, pl.ds(8 - shift, 24), :]
            starts[k] = first - shift
            used = k < blocks
            for half in range(2):
                for side in range(2):
                    touches = used & ((cx == 0) | (cx == half + 1)) & ((cy == 0) | (cy == side + 1))
                    tasks[count] = k * 4 + half * 2 + side
                    count = count + touches.astype(jnp.int32)
        return count

    jobs = lax.fori_loop(0, (blocks + WAYS - 1) // WAYS, weigh, jnp.int32(0))
    for extra in range(WAYS - 1):
        tasks[jobs + extra] = EMPTY * 4

    for load in load_near:
        load.wait()

    def spread(group, carry):
        for way in range(WAYS):
            code = tasks[group * WAYS + way]
            k = code // 4
            half = code // 2 % 2
            side = code % 2
            wx = wx_all[pl.ds(pl.multiple_of(k * SPAN + half * 16, 16), 16), :]
            wy = wy_all[pl.ds(pl.multiple_of(k * SPAN + side * 16, 16), 16), :]
            product = (wx[:, None, :] * wy[None, :, :]).reshape(256, LANES)
            high, low = split(product)
            wz = wz_all[pl.ds(pl.multiple_of(k * 24, 8), 24), :]
            z_high = wz.astype(jnp.bfloat16).astype(f32)
            left = jnp.concatenate([z_high, wz - z_high], axis=0).astype(jnp.bfloat16)
            patch = lax.dot_general(
                jnp.concatenate([left, left], axis=1), jnp.concatenate([high, low], axis=1),
                (((1,), (1,)), ((), ())), preferred_element_type=f32)
            rows = pl.ds(pl.multiple_of((code % 4) * Z_ROWS + starts[k], 8), 24)
            density[rows, :] = density[rows, :] + patch[:24] + patch[24:]
        return carry

    lax.fori_loop(0, (jobs + WAYS - 1) // WAYS, spread, jnp.int32(0))

    length = LENGTH
    gap = lax.broadcasted_iota(jnp.int32, (length, length), 0) - lax.broadcasted_iota(jnp.int32, (length, length), 1)
    gap_f = gap.astype(f32)
    tau_v = jnp.broadcast_to(SMOOTH * scales[2][:, :1], (length, length))
    band = jnp.exp(-gap_f * gap_f / (2.0 * tau_v * tau_v)) * (COUPLING / (math.sqrt(2.0 * math.pi) * tau_v))
    band_high, band_low = split(jnp.where(jnp.abs(gap) <= RADIUS, band, 0.0))
    for half in range(2):
        for side in range(2):
            part = density[pl.ds((half * 2 + side) * Z_ROWS + 16, length), :]
            high, low = split(part)
            smooth = (jnp.dot(band_high, high, preferred_element_type=f32)
                      + jnp.dot(band_high, low, preferred_element_type=f32)
                      + jnp.dot(band_low, high, preferred_element_type=f32))
            turned = smooth[8:8 + CZ].T
            edge = jnp.concatenate([smooth[4:8], smooth[8 + CZ:12 + CZ]], axis=0)
            edge_high = edge.astype(jnp.bfloat16).astype(f32)
            edges = jnp.concatenate([edge_high, edge - edge_high, edge_high, jnp.zeros((LANES - 24, 256), f32)], axis=0).T
            turned_high, turned_low = split(turned)
            cube = turned.reshape(16, 16, CZ)
            low_x, low_y = (1 - half) * RIM, (1 - side) * RIM
            potential[pl.ds(half * 12, 12), pl.ds(side * 12, 12), :] = cube[low_x:low_x + 12, low_y:low_y + 12, :]
            place = (pl.ds(half * 16, 16), pl.ds(side * 16, 16))
            for i, block in enumerate((turned_high, turned_low, turned_high, edges.astype(jnp.bfloat16))):
                field[place[0], place[1], pl.ds(i * LANES, LANES)] = block.reshape(16, 16, LANES)

    iota32 = lax.broadcasted_iota(jnp.int32, (SPAN, LANES), 0)
    def force(b):
        x = atoms[0, pl.ds(b, 1), :] * scales[0]
        y = atoms[0, pl.ds(b + BLOCKS, 1), :] * scales[1]
        q = atoms[0, pl.ds(b + 3 * BLOCKS, 1), :]
        at_x = meta[0, b]
        at_y = meta[0, BLOCKS + b]
        wx, sx = window(x, iota16, widths[0])
        wy, sy = window(y, iota32 - at_y, widths[1])
        left = field[pl.ds(at_x, PATCH)].reshape(PATCH * SPAN, 4 * LANES)
        values = jnp.dot(left, rights[b], preferred_element_type=f32).reshape(PATCH, SPAN, 256)
        by_sx = jnp.zeros((SPAN, LANES), f32)
        by_wx = jnp.zeros((SPAN, LANES), f32)
        by_wz = jnp.zeros((SPAN, LANES), f32)
        for i in range(PATCH):
            level = values[i, :, :LANES]
            by_sx = by_sx + level * sx[i:i + 1]
            by_wx = by_wx + level * wx[i:i + 1]
            by_wz = by_wz + values[i, :, LANES:] * wx[i:i + 1]
        for a, total in enumerate((by_sx * wy, by_wx * sy, by_wz * wy)):
            forces[a:a + 1, b * LANES:(b + 1) * LANES] = -q * scales[a] * jnp.sum(total, axis=0, keepdims=True)

    for b in range(BLOCKS):
        force(b)


def make_field(atoms, meta, near, rights):
    anywhere = pl.BlockSpec(memory_space=pl.ANY)
    vmem = pl.BlockSpec(memory_space=pltpu.VMEM)
    f32, i32 = jnp.float32, jnp.int32
    return pl.pallas_call(
        field_kernel,
        out_shape=(jax.ShapeDtypeStruct((CX, CY, CZ), f32), jax.ShapeDtypeStruct((3, BLOCKS * LANES), f32)),
        in_specs=[anywhere, vmem, anywhere, vmem],
        out_specs=(vmem, vmem),
        scratch_shapes=[
            pltpu.SMEM((32, LANES), i32),
            pltpu.SemaphoreType.DMA((5,)),
            pltpu.SMEM((EMPTY + 1,), i32),
            pltpu.SMEM((SLOTS * 4 + WAYS,), i32),
            pltpu.SMEM((EMPTY + 1,), i32),
            pltpu.VMEM((WAYS, 96, LANES), f32),
            pltpu.VMEM((WAYS, 96, LANES), f32),
            pltpu.VMEM((WAYS, 32, LANES), f32),
            pltpu.VMEM(((EMPTY + 1) * SPAN, LANES), f32),
            pltpu.VMEM(((EMPTY + 1) * SPAN, LANES), f32),
            pltpu.VMEM(((EMPTY + 1) * 24, LANES), f32),
            pltpu.VMEM((4 * Z_ROWS, 256), f32),
            pltpu.VMEM((SPAN, SPAN, 4 * LANES), jnp.bfloat16),
        ],
        compiler_params=pltpu.CompilerParams(vmem_limit_bytes=24 * 1024 * 1024),
        name="field_and_forces",
    )(meta, atoms, near, rights)


def exchange_kernel(pos_in, q_in, anchor_in, atoms_in, blocks_in, scale_in, atoms_out, meta_out, near_out, right_out, pos_ref, q_ref, anchor_ref, atoms_ref, blocks_ref, scale_ref, rows_ref, pad_x, pad_y, pad_z, cell_x, cell_y, wx_near, wy_near, wz_near, near_sum, rights, load_sems, send_sems, recv_sems, ready_sems):
    gx, gy, gz = (lax.axis_index(a) for a in ("gx", "gy", "gz"))
    nx, ny, nz = (lax.axis_size(a) for a in ("gx", "gy", "gz"))
    half = ny // 2

    def device(dx, dy, dz):
        return (lax.rem(gx + dx + nx, nx), lax.rem(gy + dy + ny, ny), lax.rem(gz + dz + nz, nz))

    def both(condition, other):
        return condition & jnp.logical_not(other)

    late = gy >= half
    far = {1: lax.rem(gy, half) == half - 1, -1: lax.rem(gy, half) == 0}
    wrap = {1: gz == nz - 1, -1: gz == 0}
    far_any = far[1] | far[-1]
    sided_y = gz < ONE_SIDED
    sided_z = jnp.logical_not(late & jnp.logical_not(far_any))
    hold = wrap[-1] & sided_z
    ends = wrap[1] | wrap[-1]
    direct = both(far_any, ends)
    corner = far_any & (wrap[1] | wrap[-1])
    pushes = corner & late & wrap[-1]
    pushed = both(corner & wrap[-1], late)
    hands = both(corner, wrap[1] & jnp.logical_not(late))
    far_step = jnp.where(far[1], 1, -1)
    wrap_step = jnp.where(wrap[1], 1, -1)
    steps = (1, -1)
    code = {1: 1, -1: 2}
    across = (0, 1, -1)
    ready_z, ready_y, ready_c = (ready_sems.at[i] for i in range(3))

    def when(condition, action):
        pl.when(condition)(action)

    def signal(semaphore, *offsets):
        pl.semaphore_signal(semaphore, inc=1, device_id=device(*offsets), device_id_type=MESH)

    barrier = pltpu.get_barrier_semaphore()

    def greet_far():
        signal(barrier, 0, far_step, 0)

    def greet_corner():
        for dx in across:
            signal(barrier, dx, far_step, wrap_step)

    def greet_z(step):
        signal(barrier, 0, 0, step)
        for dx in steps:
            when(jnp.logical_not(wrap[step]), lambda: signal(barrier, dx, 0, step))

    when(both(direct, late & sided_y) | pushed, greet_far)
    when(both(corner, late), greet_corner)
    for step in steps:
        signal(barrier, step, 0, 0)
        when(jnp.logical_not(far[step]), lambda: signal(barrier, 0, step, 0))
    greet_z(-1)
    when(jnp.logical_not(wrap[1] & sided_z), lambda: greet_z(1))
    loads = []
    for i, (src, dst) in enumerate(((pos_in, pos_ref), (q_in, q_ref), (anchor_in, anchor_ref), (atoms_in, atoms_ref), (blocks_in, blocks_ref), (scale_in, scale_ref))):
        loads.append(pltpu.make_async_copy(src, dst, load_sems.at[i]))
        loads[-1].start()
    for load in loads:
        load.wait()
    for a in range(3):
        for b in range(BLOCKS):
            atoms_out[0, pl.ds(a * BLOCKS + b, 1), :] = pos_ref[pl.ds(a, 1), pl.ds(b * LANES, LANES)]
    row = lax.broadcasted_iota(jnp.int32, (BLOCKS, LANES), 0)
    lane = lax.broadcasted_iota(jnp.int32, (BLOCKS, LANES), 1)
    filled = jnp.zeros((BLOCKS, LANES), jnp.int32)
    for b in range(BLOCKS):
        filled = jnp.where(row == b, jnp.where(b < blocks_ref[0], atoms_ref[b], 0), filled)
    atoms_out[0, pl.ds(3 * BLOCKS, BLOCKS), :] = jnp.where(lane < filled, q_ref[...], 0.0)
    meta = jnp.zeros((BLOCKS, LANES), jnp.int32)
    for a in range(3):
        for b in range(BLOCKS):
            meta = jnp.where(lane == a * BLOCKS + b, anchor_ref[a, b], meta)
    for b in range(BLOCKS):
        meta = jnp.where(lane == 3 * BLOCKS + b, jnp.where(b < blocks_ref[0], 1, 0), meta)
    atoms_out[0, pl.ds(32, 1), :] = meta[:1].astype(jnp.float32)
    peers = 10 - jnp.where(hold, 3, jnp.where(ends, 2, 0)) - jnp.where(both(corner, pushes) | both(direct & sided_y, late), 1, 0) + jnp.where(corner & late, 3, 0)
    pl.semaphore_wait(barrier, peers)

    def answer_corner():
        for dx in across:
            signal(ready_c, dx, far_step, wrap_step)

    when(direct & late & sided_y, lambda: signal(ready_y, 0, far_step, 0))
    when(wrap[1] & sided_z, lambda: signal(ready_z, 0, 0, 1))
    when(corner & late, answer_corner)

    def slot(cx, cz, cy):
        return (cx * 3 + cz) * 3 + cy

    def piece(src, dst, target, index):
        return pltpu.make_async_remote_copy(
            src_ref=atoms_out.at[src], dst_ref=atoms_out.at[dst],
            send_sem=send_sems.at[index], recv_sem=recv_sems.at[dst],
            device_id=target, device_id_type=MESH)

    def along_y(step):
        dst = slot(0, 0, code[step])
        return [piece(0, dst, device(0, step, 0), dst)]

    def along_x(cy):
        return [piece(cy, slot(code[dx], 0, cy), device(dx, 0, 0), slot(code[dx], 0, cy)) for dx in steps]

    def fan(cy, step):
        places = [(dx, slot(code[dx] if dx else 0, code[step], cy)) for dx in across]
        return [piece(cy, dst, device(dx, 0, step), dst) for dx, dst in places]

    def corners():
        out = []
        for i, dx in enumerate(across):
            dst = slot(code[dx] if dx else 0, jnp.where(wrap[1], 1, 2), jnp.where(far[1], 1, 2))
            out.append(piece(0, dst, device(dx, far_step, wrap_step), 27 + i))
        return out

    def start(copies):
        for copy in copies:
            copy.start()

    def finish(copies):
        for copy in copies:
            copy.wait_send()

    from_far = {1: far[-1], 2: far[1]}

    def send_early(cy):
        start(along_x(cy))
        start(fan(cy, 1)[:1])
        when(jnp.logical_not(hold), lambda: start(fan(cy, -1)[:1]))
        for step in steps:
            when(jnp.logical_not(wrap[step]), lambda: start(fan(cy, step)[1:]))

    def pass_near(cy):
        along_y(1 if cy == 1 else -1)[0].wait_recv()
        send_early(cy)

    def pass_far(cy):
        along_y(1 if cy == 1 else -1)[0].wait_recv()
        start(along_x(cy))
        for step in steps:
            when(jnp.logical_not(wrap[step]), lambda: start(fan(cy, step)))

    def open_wrap():
        pl.semaphore_wait(ready_z, 1)
        start(fan(0, -1)[:1])
        for cy in (1, 2):
            when(jnp.logical_not(from_far[cy]), lambda: start(fan(cy, -1)[:1]))

    def onward(cy, step):
        src = slot(0, code[step], cy)
        return [piece(src, slot(code[dx], code[step], cy), device(dx, 0, 0), 31 + cy * 2 + i) for i, dx in enumerate(steps)]

    def pass_wrap(cy, step):
        fan(cy, step)[0].wait_recv()
        start(onward(cy, step))

    def open_corner():
        pl.semaphore_wait(ready_c, 3)
        start(corners())

    def handed():
        corner_slot = slot(0, jnp.where(wrap[1], 2, 1), jnp.where(far[1], 2, 1))
        own_slot = slot(0, 0, jnp.where(far[1], 2, 1))
        return piece(corner_slot, own_slot, device(0, 0, wrap_step), 30)

    def forward_corner():
        corner_slot = slot(0, jnp.where(wrap[1], 2, 1), jnp.where(far[1], 2, 1))
        piece(corner_slot, corner_slot, device(0, 0, wrap_step), 30).wait_recv()
        when(hands, handed().start)

    def open_far():
        pl.semaphore_wait(ready_y, 1)
        for step in steps:
            when(far[step], lambda: start(along_y(step)))

    for step in steps:
        when(jnp.logical_not(far[step] & (ends | both(sided_y, late))) | (far[step] & pushes), lambda: start(along_y(step)))
    when(corner & late, lambda: start(corners()))
    send_early(0)
    for cy in (1, 2):
        when(jnp.logical_not(from_far[cy]), lambda: pass_near(cy))
    scales = [jnp.full((1, LANES), scale_ref[a], jnp.float32) for a in range(3)]
    weigh_own(scales, atoms_out, anchor_ref, pad_x, pad_y, pad_z, wx_near, wy_near, wz_near, rights)
    store_rights = pltpu.make_async_copy(rights, right_out, load_sems.at[6])
    store_rights.start()
    beside = both(far_any & sided_y, late) | (far_any & late & (gz > 0) & (gz < nz - 2))

    def spread_beside():
        for copy in along_x(0):
            copy.wait_recv()
        weigh_beside(scales, atoms_out, cell_x, cell_y, wx_near, wy_near, wz_near)
        spread_near(2 * BLOCKS, wx_near, wy_near, wz_near, near_sum)

    when(beside, spread_beside)
    when(jnp.logical_not(beside), lambda: spread_near(BLOCKS, wx_near, wy_near, wz_near, near_sum))
    store_near = pltpu.make_async_copy(near_sum, near_out, load_sems.at[7])
    store_near.start()
    when(hold, open_wrap)
    when(both(corner, late), open_corner)
    when(corner, forward_corner)
    for step in steps:
        when(wrap[-step], lambda: pass_wrap(0, step))
        for cy in (1, 2):
            when(both(wrap[-step], from_far[cy]), lambda: pass_wrap(cy, step))
    when(both(direct & sided_y, late), open_far)
    for cy in (1, 2):
        when(from_far[cy], lambda: pass_far(cy))
    for cy in range(3):
        for copy in along_x(cy):
            if cy:
                copy.wait_recv()
            else:
                when(jnp.logical_not(beside), copy.wait_recv)
        for step in steps:
            copies = fan(cy, step)
            when(jnp.logical_not(wrap[-step]), copies[0].wait_recv)
            for copy in copies[1:]:
                copy.wait_recv()
    for step in steps:
        when(jnp.logical_not(far[step] & ends) | (far[step] & pushes), lambda: finish(along_y(step)))
    for cy in range(3):
        finish(along_x(cy))
        for step in steps:
            when(jnp.logical_not(wrap[step]), lambda: finish(fan(cy, step)[1:]))
            if cy == 0:
                finish(fan(cy, step)[:1])
                when(wrap[-step], lambda: finish(onward(cy, step)))
            else:
                when(jnp.logical_not(from_far[cy] & wrap[step]), lambda: finish(fan(cy, step)[:1]))
                when(both(wrap[-step], from_far[cy]), lambda: finish(onward(cy, step)))
    when(corner, lambda: finish(corners()))
    when(hands, lambda: finish([handed()]))
    for a in range(3):
        atoms_out[SOURCES, pl.ds(a, 1), :] = jnp.full((1, LANES), scale_ref[a], jnp.float32)
    store_rights.wait()
    store_near.wait()
    rows_ref[...] = jnp.zeros_like(rows_ref)
    for n in range(SOURCES):
        rows_ref[pl.ds(n, 1), :] = atoms_out[n, pl.ds(32, 1), :]
    value = rows_ref[...].astype(jnp.int32)
    source = lax.broadcasted_iota(jnp.int32, value.shape, 0)
    place = lax.broadcasted_iota(jnp.int32, value.shape, 1)
    one = jnp.ones_like(value)
    zero = jnp.zeros_like(value)
    cx = jnp.where(source >= 9, one, zero) + jnp.where(source >= 18, one, zero)
    rest = source - 9 * cx
    cz = jnp.where(rest >= 3, one, zero) + jnp.where(rest >= 6, one, zero)
    cy = rest - 3 * cz
    is_z = (place >= 2 * BLOCKS) & (place < 3 * BLOCKS)
    is_live = place >= 3 * BLOCKS
    kind = jnp.where(place < BLOCKS, cx, jnp.where(place < 2 * BLOCKS, cy, cz))
    period = jnp.where(is_z, CZ, CX)
    low = jnp.where(is_live, 1, jnp.where(kind == 1, jnp.where(is_z, CZ - 19, 5), 0))
    high = jnp.where(jnp.logical_not(is_live) & (kind == 2), 11, 999)
    fits = jnp.where((value >= low) & (value <= high), one, zero)
    used = fits
    for group in (1, 2, 3):
        used = used * pltpu.roll(fits, LANES - group * BLOCKS, 1)
    used = pltpu.roll(used, 4 * BLOCKS, 1) * jnp.where(rest == 0, 1 - beside.astype(jnp.int32), one)
    shifted = value + jnp.where(is_live | (kind == 0), 0, jnp.where(kind == 1, -period, period))
    meta_out[...] = jnp.where(place >= 4 * BLOCKS, used, shifted)


def weigh_own(scales, atoms, anchor, pad_x, pad_y, pad_z, wx_near, wy_near, wz_near, rights):
    f32 = jnp.float32
    widths = [SPREAD * s for s in scales]
    taps = kernel_taps(scales)
    iota16 = lax.broadcasted_iota(jnp.int32, (PATCH, LANES), 0)
    iota_z = lax.broadcasted_iota(jnp.int32, (CZ, LANES), 0)
    iota8 = lax.broadcasted_iota(jnp.int32, (8, LANES), 0)
    edge_z = jnp.where(iota8 < 4, iota8 - 4, iota8 + (CZ - 4))
    for ref in (pad_x, pad_y, pad_z):
        ref[...] = jnp.zeros_like(ref)

    def weigh(b, carry):
        x = atoms[0, pl.ds(b, 1), :] * scales[0]
        y = atoms[0, pl.ds(b + BLOCKS, 1), :] * scales[1]
        z = atoms[0, pl.ds(b + 2 * BLOCKS, 1), :] * scales[2]
        q = atoms[0, pl.ds(b + 3 * BLOCKS, 1), :]
        pad_x[b, pl.ds(PAD, PATCH), :] = q * window(x, iota16, widths[0])[0]
        pad_y[b, pl.ds(PAD, PATCH), :] = window(y, iota16, widths[1])[0]
        pad_z[b, pl.ds(LENGTH, PATCH), :] = window(z, iota16, widths[2])[0]
        for a, pad, out in ((0, pad_x, wx_near), (1, pad_y, wy_near)):
            start = PAD - anchor[a, b]
            total = taps[a][0] * pad[b, pl.ds(start, SPAN), :]
            for e in range(1, RADIUS + 1):
                total = total + taps[a][e] * (pad[b, pl.ds(start - e, SPAN), :] + pad[b, pl.ds(start + e, SPAN), :])
            out[b] = total
        high, low = split(pad_z[b, pl.ds(LENGTH - 4 - anchor[2, b], LENGTH), :])
        wz_near[b, pl.ds(0, LENGTH), :] = high
        wz_near[b, pl.ds(LENGTH, LENGTH), :] = low
        wz, sz = window(z, iota_z - anchor[2, b] + RIM, widths[2])
        we, se = window(z, edge_z - anchor[2, b] + RIM, widths[2])
        main_high, main_low = split(jnp.concatenate([wz, sz], axis=1))
        rim = jnp.concatenate([we, se], axis=1)
        rim_high = rim.astype(jnp.bfloat16).astype(f32)
        rim = jnp.concatenate([rim_high, rim_high, rim - rim_high, jnp.zeros((LANES - 24, 256), f32)], axis=0)
        for i, part in enumerate((main_high, main_high, main_low, rim.astype(jnp.bfloat16))):
            rights[b, pl.ds(i * LANES, LANES), :] = part
        return carry

    lax.fori_loop(0, BLOCKS, weigh, jnp.int32(0))


def weigh_beside(scales, atoms, cell_x, cell_y, wx_near, wy_near, wz_near):
    i32 = jnp.int32
    widths = [SPREAD * s for s in scales]
    taps = kernel_taps(scales)
    iota_x = lax.broadcasted_iota(i32, (24, LANES), 0)
    iota_y = lax.broadcasted_iota(i32, (40, LANES), 0)
    iota_z = lax.broadcasted_iota(i32, (LENGTH, LANES), 0)
    lane = lax.broadcasted_iota(i32, (1, LANES), 1)

    def weigh(b, carry):
        for half in range(2):
            n = 9 * (1 + half)
            k = BLOCKS * (1 + half) + b
            x = atoms[n, pl.ds(b, 1), :] * scales[0]
            y = atoms[n, pl.ds(b + BLOCKS, 1), :] * scales[1]
            z = atoms[n, pl.ds(b + 2 * BLOCKS, 1), :] * scales[2]
            q = atoms[n, pl.ds(b + 3 * BLOCKS, 1), :]
            row = atoms[n, pl.ds(32, 1), :]
            at = [jnp.sum(jnp.where(lane == a * BLOCKS + b, row, 0.0), axis=1, keepdims=True) for a in range(3)]
            at_x, at_y, at_z = [jnp.broadcast_to(v, (1, LANES)).astype(i32) for v in at]
            at_x = at_x + (CX if half else -CX)
            cell_x[half] = q * window(x, iota_x + (half * 16 - 4) - at_x, widths[0])[0]
            cell_y[half] = window(y, iota_y - 4 - at_y, widths[1])[0]
            for a, cell, out, count, first in ((0, cell_x, wx_near, 16, half * 16), (1, cell_y, wy_near, SPAN, 0)):
                total = taps[a][0] * cell[half, pl.ds(4, count), :]
                for e in range(1, RADIUS + 1):
                    total = total + taps[a][e] * (cell[half, pl.ds(4 - e, count), :] + cell[half, pl.ds(4 + e, count), :])
                out[k, pl.ds(first, count), :] = total
            high, low = split(window(z, iota_z - 4 - at_z, widths[2])[0])
            wz_near[k, pl.ds(0, LENGTH), :] = high
            wz_near[k, pl.ds(LENGTH, LENGTH), :] = low
        return carry

    lax.fori_loop(0, BLOCKS, weigh, jnp.int32(0))


def spread_near(count, wx_near, wy_near, wz_near, near_sum):
    def spread(quarter, carry):
        half = quarter // 2
        side = quarter % 2
        left, right = [], []
        for b in range(count):
            k = b if b < BLOCKS else b + BLOCKS * half
            wx = wx_near[k, pl.ds(pl.multiple_of(half * 16, 16), 16), :]
            wy = wy_near[k, pl.ds(pl.multiple_of(side * 16, 16), 16), :]
            right += split((wx[:, None, :] * wy[None, :, :]).reshape(256, LANES))
            left += [wz_near[k]] * 2
        patch = lax.dot_general(
            jnp.concatenate(left, axis=1), jnp.concatenate(right, axis=1),
            (((1,), (1,)), ((), ())), preferred_element_type=jnp.float32)
        near_sum[quarter] = patch[:LENGTH] + patch[LENGTH:]
        return carry

    lax.fori_loop(0, 4, spread, jnp.int32(0))


def exchange(positions, charges, block_anchor, block_atoms, brick_blocks, box_scale):
    anywhere = pl.BlockSpec(memory_space=pl.ANY)
    vmem = pl.BlockSpec(memory_space=pltpu.VMEM)
    f32, i32 = jnp.float32, jnp.int32
    return pl.pallas_call(
        exchange_kernel,
        out_shape=(pltpu.VMEM((SOURCES + 1, ROWS, LANES), f32), pltpu.VMEM((32, LANES), i32),
                   pltpu.VMEM((4, LENGTH, 256), f32),
                   pltpu.VMEM((BLOCKS, 4 * LANES, 256), jnp.bfloat16)),
        in_specs=[anywhere] * 6,
        out_specs=(vmem, vmem, anywhere, anywhere),
        scratch_shapes=[
            pltpu.VMEM((3, BLOCKS * LANES), f32),
            pltpu.VMEM((BLOCKS, LANES), f32),
            pltpu.SMEM((3, BLOCKS), i32),
            pltpu.SMEM((BLOCKS,), i32),
            pltpu.SMEM((1,), i32),
            pltpu.SMEM((3,), f32),
            pltpu.VMEM((32, LANES), f32),
            pltpu.VMEM((BLOCKS, 96, LANES), f32),
            pltpu.VMEM((BLOCKS, 96, LANES), f32),
            pltpu.VMEM((BLOCKS, 2 * LENGTH + PATCH, LANES), f32),
            pltpu.VMEM((2, 24, LANES), f32),
            pltpu.VMEM((2, 40, LANES), f32),
            pltpu.VMEM((3 * BLOCKS, SPAN, LANES), f32),
            pltpu.VMEM((3 * BLOCKS, SPAN, LANES), f32),
            pltpu.VMEM((3 * BLOCKS, 2 * LENGTH, LANES), jnp.bfloat16),
            pltpu.VMEM((4, LENGTH, 256), f32),
            pltpu.VMEM((BLOCKS, 4 * LANES, 256), jnp.bfloat16),
            pltpu.SemaphoreType.DMA((8,)),
            pltpu.SemaphoreType.DMA((40,)),
            pltpu.SemaphoreType.DMA((SOURCES,)),
            pltpu.SemaphoreType.REGULAR((3,)),
        ],
        compiler_params=pltpu.CompilerParams(collective_id=0, has_side_effects=True, vmem_limit_bytes=60 * 1024 * 1024),
        name="exchange_atoms",
    )(positions, charges.reshape(BLOCKS, LANES), block_anchor, block_atoms, brick_blocks, box_scale)


def per_device(positions, charges, block_anchor, block_atoms, brick_blocks, box_scale):
    atoms, meta, near, rights = exchange(positions, charges, block_anchor, block_atoms, brick_blocks, box_scale)
    potential, forces = make_field(atoms, meta, near, rights)
    return (potential, forces)


def solution(mesh):
    split_all = ("gx", "gy", "gz")
    return jax.shard_map(
        per_device,
        mesh=mesh,
        in_specs=(P(None, split_all), P(split_all), P(None, split_all), P(split_all), P(split_all), P()),
        out_specs=(P("gx", "gy", "gz"), P(None, split_all)),
        check_vma=False,
    )
```
